512 devices in a mesh: gx: 8 (over x, core), gy: 8 (over z), gz: 8 (over y).
Axes of the slice: x: 4, y: 8, z: 8, core: 2. Of those that a mesh axis runs over, the one named last changes fastest.
Arguments:
- fine_coef: bfloat16 [4096, 512], P(('gx', 'gy', 'gz')), may hold values from -6 to 6
- mid_leaf: bfloat16 [512, 512], P(('gx', 'gy', 'gz')), may hold values from -6 to 6
- mid_child: int32 [512, 8], P(('gx', 'gy', 'gz')), may hold values from 0 to 7, as said below
- mid_parent: int32 [512], P(('gx', 'gy', 'gz')), may hold values from 0 to 511, each once
- mid_refined: int32 [512], P(('gx', 'gy', 'gz')), may hold values 0 or 1
- fine_nbr: int32 [4096, 27], P(('gx', 'gy', 'gz')), may hold values from -1 to 4095, as said below
- mid_nbr: int32 [512, 27], P(('gx', 'gy', 'gz')), may hold values from -1 to 511, as said below
- coarse_nbr: int32 [64, 27], replicated, may hold values from -1 to 63, as said below
- op_factor: float32 [3, 32, 3, 8, 8], replicated, may hold values from -1 to 1
- term_weight: float32 [32], replicated, may hold values from 0.05 to 1
Outputs:
- fine_out: float32 [4096, 512], P(('gx', 'gy', 'gz'))
- mid_out: float32 [512, 512], P(('gx', 'gy', 'gz'))
The draws below stay inside these ranges and needn't reach their ends.
Inputs may be any that keep to these rules, and one draw needn't show every extreme that they name: `fine_nbr`: column d names the fine box adjacent across displacement (d // 9 - 1, d // 3 % 3 - 1, d % 3 - 1), or -1. Column 13 is the row's own box. Box g lies on device g // 8; the named box's device differs from the row's device along each of gx, gy, gz by 0 or by that component of the displacement. `mid_nbr`: column d names the middle box adjacent across displacement (d // 9 - 1, d // 3 % 3 - 1, d % 3 - 1), or -1. Column 13 is the row's own box. Box g lies on device g; the named box's device differs from the row's device along each of gx, gy, gz by 0 or by that component of the displacement. `coarse_nbr`: column d names the coarse box adjacent across displacement (d // 9 - 1, d // 3 % 3 - 1, d % 3 - 1), or -1. Column 13 is the row's own box. `mid_child`: the 1 row of one device together name each of its 8 local fine slots exactly once. `mid_parent`: each value appears once.
All inputs are finite; a program needn't handle non-finite values. No bound on the sum of `mid_refined` on one device may be relied on, other than what follows from the above.
Results may differ from the reference program's by a relative error of at most 0.006.
Values may be sent and summed in bfloat16 or wider, within the bound.
No kernel may reach another device: no remote copies, remote signals or barrier semaphores. Data moves between devices by JAX's collectives and lax.ppermute only.
A program may use at most 64 MiB of HBM per device.

```python
import math
import jax
import jax.numpy as jnp
import numpy as np
from jax import lax

K = 8
TERMS = 32
MB_DEV = 1
FINE = 4096
MID = 512
COARSE = 64
N_GX = 8
N_GY = 8
N_GZ = 8
DEVICES = 512


def near_boxes(key, per_device):
    box_total = per_device * DEVICES
    box_index = jnp.arange(box_total, dtype=jnp.int32)
    device = box_index // per_device
    coord_x = device // (N_GY * N_GZ)
    coord_y = device // N_GZ % N_GY
    coord_z = device % N_GZ
    column = jnp.arange(27, dtype=jnp.int32)
    step_x = column // 9 - 1
    step_y = column // 3 % 3 - 1
    step_z = column % 3 - 1
    key_hop, key_slot, key_gone = jax.random.split(key, 3)
    hop_bits = jax.random.randint(key_hop, (box_total, 3, 27), 0, 2, dtype=jnp.int32)
    near_x = coord_x[:, None] + step_x[None, :] * hop_bits[:, 0]
    near_y = coord_y[:, None] + step_y[None, :] * hop_bits[:, 1]
    near_z = coord_z[:, None] + step_z[None, :] * hop_bits[:, 2]
    inside = (near_x >= 0) & (near_x < N_GX) & (near_y >= 0) & (near_y < N_GY) & (near_z >= 0) & (near_z < N_GZ)
    slot_pick = jax.random.randint(key_slot, (box_total, 27), 0, per_device, dtype=jnp.int32)
    gone_mask = jax.random.randint(key_gone, (box_total, 27), 0, 5, dtype=jnp.int32) == 0
    named_box = ((near_x * N_GY + near_y) * N_GZ + near_z) * per_device + slot_pick
    result = jnp.where(inside & jnp.logical_not(gone_mask), named_box, -1)
    result = jnp.where(column[None, :] == 13, box_index[:, None], result)
    return result.astype(jnp.int32)


def draw_fine_nbr(key, part):
    return near_boxes(jax.random.fold_in(key, 11), 8 * MB_DEV)


def draw_mid_nbr(key, part):
    return near_boxes(jax.random.fold_in(key, 12), MB_DEV)


def draw_coarse_nbr(key, part):
    key_pick, key_gone = jax.random.split(jax.random.fold_in(key, 13), 2)
    column = jnp.arange(27, dtype=jnp.int32)
    box_index = jnp.arange(COARSE, dtype=jnp.int32)
    picked = jax.random.randint(key_pick, (COARSE, 27), 0, COARSE, dtype=jnp.int32)
    gone_mask = jax.random.randint(key_gone, (COARSE, 27), 0, 5, dtype=jnp.int32) == 0
    result = jnp.where(gone_mask, -1, picked)
    result = jnp.where(column[None, :] == 13, box_index[:, None], result)
    return result.astype(jnp.int32)


def shuffle_slots(single_key):
    return jax.random.permutation(single_key, 8 * MB_DEV)


def draw_mid_child(key, part):
    all_keys = jax.random.split(jax.random.fold_in(key, 14), DEVICES)
    orders = jax.vmap(shuffle_slots)(all_keys)
    return orders.reshape(MID, 8).astype(jnp.int32)


def place_ends(entries, key, low, top_value):
    index_at = [jax.random.randint(jax.random.fold_in(key, axis), (), 0, length) for axis, length in enumerate(entries.shape)]
    longest = entries.shape.index(max(entries.shape))
    next_to = index_at[:longest] + [(index_at[longest] + 1) % entries.shape[longest]] + index_at[longest + 1:]
    return entries.at[tuple(index_at)].set(low).at[tuple(next_to)].set(top_value)


def steps_of(rng, extent, shards, low, high):
    def one(axis_at, shards_of):
        draws = jax.random.uniform(jax.random.fold_in(jax.random.fold_in(rng, 6), axis_at), (shards_of,), jnp.float32, low / len(shards), high / len(shards))
        return jnp.repeat(jnp.exp(draws), extent[axis_at] // shards_of).reshape((-1,) + (1,) * (len(extent) - axis_at - 1))

    level = one(*shards[0])
    for cut in shards[1:]:
        level = level * one(*cut)
    return level


def normal_values(key, shape, scale, reach, cuts=(), held_as=jnp.bfloat16):
    array = jax.random.normal(key, shape, jnp.float32) * scale
    if len(cuts) > 0:
        array = steps_of(key, shape, cuts, -0.22, 0.18) * array
    return jnp.clip(array, min=-reach, max=reach).astype(held_as)


def setup_inputs(seed: int = 0) -> dict:
    keys = jax.random.split(jax.random.key(seed), 11)
    fine_coef = normal_values(keys[0], (FINE, K ** 3), 1.0, 6.0, ((0, 512),))
    mid_leaf = normal_values(keys[1], (MID, K ** 3), 1.0, 6.0, ((0, 512),))
    mid_child = draw_mid_child(jax.random.fold_in(keys[10], 71), 0)
    mid_parent = jax.random.permutation(keys[3], MID).astype(jnp.int32)
    mid_refined = place_ends((jax.random.randint(keys[4], (MID,), 0, 3) < 2).astype(jnp.int32), jax.random.fold_in(keys[4], 1), 0, 1)
    fine_nbr = draw_fine_nbr(jax.random.fold_in(keys[10], 71), 0)
    mid_nbr = draw_mid_nbr(jax.random.fold_in(keys[10], 71), 0)
    coarse_nbr = draw_coarse_nbr(jax.random.fold_in(keys[10], 71), 0)
    op_factor = normal_values(keys[8], (3, TERMS, 3, K, K), 0.16, 1.0, (), jnp.float32)
    term_weight = jnp.clip(jnp.exp(jax.random.uniform(keys[9], (TERMS,), jnp.float32, math.log(0.05), math.log(1.0))), 0.05, 1.0)
    return dict(fine_coef=fine_coef, mid_leaf=mid_leaf, mid_child=mid_child, mid_parent=mid_parent, mid_refined=mid_refined, fine_nbr=fine_nbr, mid_nbr=mid_nbr, coarse_nbr=coarse_nbr, op_factor=op_factor, term_weight=term_weight)


exact_mode = lax.Precision.HIGHEST

def poly_multiply(left, right):
    result = [0.0] * (len(left) + len(right) - 1)
    for first, left_coef in enumerate(left):
        for second, right_coef in enumerate(right):
            result[first + second] += left_coef * right_coef
    return result

def poly_compose(coeffs, factor, offset):
    result = [0.0]
    power_term = [1.0]
    for coef in coeffs:
        padded = result + [0.0] * (len(power_term) - len(result))
        result = [padded[place] + coef * power_term[place] for place in range(len(power_term))]
        power_term = poly_multiply(power_term, [offset, factor])
    return result

def legendre_table(basis_order):
    polys = [[1.0], [0.0, 1.0]]
    for degree in range(1, basis_order):
        upper = [0.0] + [(2 * degree + 1) * coef for coef in polys[degree]]
        lower = [degree * coef for coef in polys[degree - 1]] + [0.0] * (len(upper) - len(polys[degree - 1]))
        polys.append([(upper[place] - lower[place]) / (degree + 1) for place in range(len(upper))])
    return [[math.sqrt(2 * degree + 1) * coef for coef in poly_compose(polys[degree], 2.0, -1.0)] for degree in range(basis_order)]

def two_scale(basis_order):
    shifted = legendre_table(basis_order)
    filters = np.zeros((2, basis_order, basis_order))
    for which_half in range(2):
        for row_at in range(basis_order):
            halved = poly_compose(shifted[row_at], 0.5, 0.5 * which_half)
            for col_at in range(basis_order):
                product = poly_multiply(halved, shifted[col_at])
                total = sum((coef / (place + 1) for place, coef in enumerate(product)))
                filters[which_half, row_at, col_at] = total / math.sqrt(2.0)
    return jnp.asarray(filters, jnp.float32)

def compress(children, filters):
    box_count = children.shape[0]
    basis_order = filters.shape[1]
    cube_form = children.reshape(box_count, 2, 2, 2, basis_order, basis_order, basis_order)
    section_one = jnp.einsum('bijlxyz,ipx->bjlpyz', cube_form, filters, precision=exact_mode)
    section_two = jnp.einsum('bjlpyz,jqy->blpqz', section_one, filters, precision=exact_mode)
    section_three = jnp.einsum('blpqz,lrz->bpqr', section_two, filters, precision=exact_mode)
    return section_three.reshape(box_count, basis_order ** 3)

def prolong(parents, filters):
    box_count = parents.shape[0]
    basis_order = filters.shape[1]
    cube_form = parents.reshape(box_count, basis_order, basis_order, basis_order)
    section_one = jnp.einsum('bpqr,ipx->bixqr', cube_form, filters, precision=exact_mode)
    section_two = jnp.einsum('bixqr,jqy->bijxyr', section_one, filters, precision=exact_mode)
    section_three = jnp.einsum('bijxyr,lrz->bijlxyz', section_two, filters, precision=exact_mode)
    return section_three.reshape(box_count, 8, basis_order ** 3)

def level_tables(factors, weights):
    basis_order = factors.shape[-1]
    term_count = factors.shape[0]
    across = jnp.transpose(factors, (1, 0, 3, 2))
    blocks = weights[None, None, :, None, None, None, None] * across[:, None, :, :, None, :, None] * across[None, :, :, None, :, None, :]
    blocks = blocks.reshape(3, 3, term_count * basis_order * basis_order, basis_order * basis_order)
    return (factors.astype(jnp.bfloat16), blocks.astype(jnp.bfloat16))

def apply_boxes(sources, factor_bf, blocks):
    box_count = sources.shape[0]
    basis_order = factor_bf.shape[-1]
    plane_size = basis_order * basis_order
    cube_form = sources.reshape(box_count, 3, 3, 3, basis_order, plane_size)
    running = jnp.zeros((box_count * basis_order, plane_size), jnp.float32)
    for along_y in range(3):
        for along_z in range(3):
            picked = cube_form[:, :, along_y, along_z]
            mixed_terms = jnp.einsum('mdax,bdxq->bamq', factor_bf.astype(jnp.float32), picked.astype(jnp.float32), precision=exact_mode).astype(jnp.bfloat16)
            flat_terms = mixed_terms.reshape(box_count * basis_order, -1)
            running = running + jnp.dot(flat_terms.astype(jnp.float32), blocks[along_y, along_z].astype(jnp.float32), precision=exact_mode)
    return running.reshape(box_count, basis_order ** 3)

def apply_level(source_table, near_ids, factors, weights):
    factor_bf, blocks = level_tables(factors, weights)
    total_rows = near_ids.shape[0]
    block_rows = math.gcd(total_rows, 128)
    grouped = near_ids.reshape(total_rows // block_rows, block_rows, 27)

    def one_block(some_rows):
        sources = source_table[jnp.maximum(some_rows, 0)] * (some_rows >= 0)[:, :, None].astype(source_table.dtype)
        return apply_boxes(sources, factor_bf, blocks)
    return lax.map(one_block, grouped).reshape(total_rows, -1)

def reference(fine_coef, mid_leaf, mid_child, mid_parent, mid_refined, fine_nbr, mid_nbr, coarse_nbr, op_factor, term_weight):
    filters = two_scale(K)
    slots_dev = 8 * MB_DEV
    mid_count = mid_child.shape[0]
    volume = fine_coef.shape[1]
    owner_dev = jnp.arange(mid_count, dtype=jnp.int32) // MB_DEV
    child_rows = (owner_dev[:, None] * slots_dev + mid_child).astype(jnp.int32)
    flat_rows = child_rows.reshape(-1)
    refined = mid_refined.astype(jnp.float32)
    live_mask = jnp.zeros((FINE,), jnp.float32).at[flat_rows].set(jnp.repeat(refined, 8))
    children = fine_coef[child_rows].astype(jnp.float32)
    compressed = compress(children, filters)
    mid_source = jnp.where(mid_refined[:, None] > 0, compressed, mid_leaf.astype(jnp.float32)).astype(jnp.bfloat16)
    mid_float = mid_source.astype(jnp.float32)
    spread = prolong(mid_float, filters)
    fine_from = jnp.zeros((FINE, volume), jnp.float32).at[flat_rows].set(spread.reshape(-1, volume))
    fine_detail = (live_mask[:, None] * (fine_coef.astype(jnp.float32) - fine_from)).astype(jnp.bfloat16)
    parent = (mid_parent // 8).astype(jnp.int32)
    octant = mid_parent % 8
    octant_hot = (octant[:, None] == jnp.arange(8, dtype=jnp.int32)[None, :]).astype(jnp.float32)
    placed = octant_hot[:, :, None] * mid_float[:, None, :]
    coarse_source = jnp.zeros((COARSE, volume), jnp.float32).at[parent].add(compress(placed, filters))
    parent_source = coarse_source[parent]
    from_coarse = lax.optimization_barrier(jnp.sum(octant_hot[:, :, None] * prolong(parent_source, filters), axis=1))
    mid_detail = (mid_float - from_coarse).astype(jnp.bfloat16)
    coarse_table = coarse_source.astype(jnp.bfloat16)
    coarse_output = apply_level(coarse_table, coarse_nbr, op_factor[2], term_weight)
    parent_out = coarse_output[parent]
    mid_out = apply_level(mid_detail, mid_nbr, op_factor[1], term_weight) + lax.optimization_barrier(jnp.sum(octant_hot[:, :, None] * prolong(parent_out, filters), axis=1))
    fine_back = jnp.zeros((FINE, volume), jnp.float32).at[flat_rows].set(prolong(mid_out, filters).reshape(-1, volume))
    fine_out = live_mask[:, None] * (apply_level(fine_detail, fine_nbr, op_factor[0], term_weight) + fine_back)
    return (fine_out, mid_out)
```

```python
import functools
import math

import jax
import jax.numpy as jnp
import ml_dtypes
import numpy as np
from jax import lax
from jax.experimental import pallas as pl
from jax.experimental.pallas import tpu as pltpu
from jax.sharding import PartitionSpec as P

K = 8
PLANE = 64
TERMS = 32
QUADS = 8
ROWS_W = 640
GONE = 27 * 8
BF16 = jnp.bfloat16
F32 = jnp.float32
VMEM_LIMIT = 40 * 1024 * 1024


def poly_multiply(left, right):
    result = [0.0] * (len(left) + len(right) - 1)
    for first, left_coef in enumerate(left):
        for second, right_coef in enumerate(right):
            result[first + second] += left_coef * right_coef
    return result


def poly_compose(coeffs, factor, offset):
    result = [0.0]
    power_term = [1.0]
    for coef in coeffs:
        padded = result + [0.0] * (len(power_term) - len(result))
        result = [padded[place] + coef * power_term[place] for place in range(len(power_term))]
        power_term = poly_multiply(power_term, [offset, factor])
    return result


def legendre_table(basis_order):
    polys = [[1.0], [0.0, 1.0]]
    for degree in range(1, basis_order):
        upper = [0.0] + [(2 * degree + 1) * coef for coef in polys[degree]]
        lower = [degree * coef for coef in polys[degree - 1]] + [0.0] * (
            len(upper) - len(polys[degree - 1])
        )
        polys.append([(upper[place] - lower[place]) / (degree + 1) for place in range(len(upper))])
    return [
        [math.sqrt(2 * degree + 1) * coef for coef in poly_compose(polys[degree], 2.0, -1.0)]
        for degree in range(basis_order)
    ]


@functools.cache
def two_scale(basis_order):
    shifted = legendre_table(basis_order)
    filters = np.zeros((2, basis_order, basis_order))
    for which_half in range(2):
        for row_at in range(basis_order):
            halved = poly_compose(shifted[row_at], 0.5, 0.5 * which_half)
            for col_at in range(basis_order):
                product = poly_multiply(halved, shifted[col_at])
                total = sum((coef / (place + 1) for place, coef in enumerate(product)))
                filters[which_half, row_at, col_at] = total / math.sqrt(2.0)
    return filters.astype(np.float32).astype(np.float64)


def two_parts(matrix):
    high = matrix.astype(ml_dtypes.bfloat16)
    low = (matrix - high.astype(np.float64)).astype(ml_dtypes.bfloat16)
    return high, low


@functools.cache
def filter_tables():
    h = two_scale(K)
    pair = np.einsum("jqy,lrz->jlqryz", h, h).reshape(4, PLANE, PLANE)
    to_coarse = pair.transpose(0, 2, 1).reshape(4 * PLANE, PLANE)
    comp = np.concatenate(two_parts(to_coarse), axis=1)
    to_fine = pair.transpose(1, 0, 2).reshape(PLANE, 4 * PLANE)
    prol = np.concatenate(two_parts(to_fine), axis=1)
    contrib = np.stack([np.concatenate(two_parts(pair[k].T), axis=1) for k in range(4)])
    single = np.stack([np.concatenate(two_parts(pair[k]), axis=1) for k in range(4)])
    mid = np.zeros((2, PLANE, 4, 2, PLANE))
    for half in range(2):
        mid[half, :, :, half, :] = pair.transpose(1, 0, 2)
    mids = np.concatenate(two_parts(mid.reshape(128, 512)), axis=1)
    rows_c = np.broadcast_to(h.transpose(0, 2, 1).reshape(16, 8)[:, :, None], (16, 8, 128))
    rows_p = np.broadcast_to(h.reshape(16, 8)[:, :, None], (16, 8, 128))
    return dict(
        comp=comp,
        prol=prol,
        contrib=contrib,
        single=single,
        mids=mids,
        rows_c=np.ascontiguousarray(rows_c).astype(np.float32),
        rows_p=np.ascontiguousarray(rows_p).astype(np.float32),
    )


@functools.cache
def select_tables():
    n4 = np.arange(4)
    a = np.arange(8)
    eye4 = (n4[:, None] == n4[None, :]).astype(np.float64)
    eye8 = (a[:, None] == a[None, :]).astype(np.float64)
    one = np.ones(8)
    left = np.einsum("nm,ab,c->nambc", eye4, eye8, one).reshape(32, 256)
    right = np.einsum("nm,ac,b->nambc", eye4, eye8, one).reshape(32, 256)
    return np.concatenate([left, right], axis=1).astype(ml_dtypes.bfloat16)


def split(value):
    high = value.astype(BF16)
    return high, (value - high.astype(F32)).astype(BF16)


def dot(left, right):
    return jnp.dot(left, right, preferred_element_type=F32)


def fine_dot(value, table):
    rows = value.shape[0]
    width = table.shape[1] // 2
    if rows % 16 == 0:
        result = dot(jnp.concatenate(split(value), axis=0), table)
    else:
        high = value.astype(BF16).astype(F32)
        result = dot(jnp.concatenate([high, value - high], axis=0).astype(BF16), table)
    return result[:rows, :width] + result[rows:, :width] + result[:rows, width:]


def low_lanes(shape):
    return lax.broadcasted_iota(jnp.int32, shape, len(shape) - 1) < PLANE


def turned(value):
    return pltpu.roll(value, PLANE, value.ndim - 1)


def row_mix(tables, tile):
    total = None
    for p in range(8):
        term = tables[p] * tile[p : p + 1, :]
        total = term if total is None else total + term
    return total


def two_row_mixes(rows_ref, tile, width):
    return [
        row_mix([rows_ref[i * 8 + p, :, :width] for p in range(8)], tile) for i in range(2)
    ]


def local_cell(near, own, per_device):
    device = near // per_device if per_device == 1 else near >> 3
    step_x = (device >> 6) - (own >> 6) + 1
    step_y = ((device >> 3) & 7) - ((own >> 3) & 7) + 1
    step_z = (device & 7) - (own & 7) + 1
    return step_x * 9 + step_y * 3 + step_z


def build_tables(factors, weighted, select, ab_ref, w_ref):
    left = dot(jnp.concatenate(split(weighted), axis=0), select[:, :256])
    right = dot(jnp.concatenate(split(factors), axis=0), select[:, 256:])
    ab_ref[:, :, :256] = (left[:192] + left[192:]).reshape(8, 24, 256)
    ab_ref[:, :, 256:] = (right[:192] + right[192:]).reshape(8, 24, 256)

    def one_quad(quad, carry):
        inner = [ab_ref[quad, ez * 8 : ez * 8 + 8, 256:512] for ez in range(3)]
        for ey in range(3):
            for pair in range(4):
                at = ey * 8 + 2 * pair
                first = ab_ref[quad, at : at + 1, 0:256]
                second = ab_ref[quad, at + 1 : at + 2, 0:256]
                for ez in range(3):
                    tile = jnp.concatenate([first * inner[ez], second * inner[ez]], axis=0)
                    row = (ey * 3 + ez) * PLANE + pair * 16
                    w_ref[quad, row : row + 16, :] = tile.astype(BF16)
        w_ref[quad, 576:640, :] = jnp.zeros((64, 256), BF16)
        return carry

    lax.fori_loop(0, QUADS, one_quad, 0)


def diagonal_sum(result, rows):
    total = None
    for term in range(4):
        piece = result[term * rows : (term + 1) * rows, term * PLANE : (term + 1) * PLANE]
        total = piece if total is None else total + piece
    return total


def apply_one(sources, x_table, w_ref):
    mixed = dot(x_table, sources).astype(BF16)
    result = None
    for quad in range(QUADS):
        part = dot(mixed[quad * 32 : quad * 32 + 32, :], w_ref[quad])
        result = part if result is None else result + part
    return diagonal_sum(result, 8)


def first_kernel(
    child, parent, refined, fine_nbr, mid_nbr, coarse_nbr, coef, leaf,
    comp, prol, contrib, rows_c, rows_p,
    halo, payload, fine_at, mid_at, coarse_at, source, detail,
):
    near = fine_nbr[...]
    own = near[:, 13:14] >> 3
    cell = local_cell(near, own, 8) * 8 + (near & 7)
    fine_at[:, 0:27] = jnp.where(near >= 0, cell, GONE)
    near_mid = mid_nbr[...]
    own_mid = near_mid[:, 13:14]
    mid_at[:, 0:27] = jnp.where(near_mid >= 0, local_cell(near_mid, own_mid, 1), 27)
    mid_at[:, 27:32] = jnp.full((1, 5), 27, jnp.int32)
    slot = parent[0] >> 3
    octant = parent[0] & 7
    near_coarse = coarse_nbr[pl.ds(slot, 1), :]
    coarse_at[:, 0:27] = jnp.where(near_coarse >= 0, near_coarse, 64)
    coarse_at[:, 27:32] = jnp.full((1, 5), 64, jnp.int32)

    values = coef[...].astype(F32)
    for a in range(8):
        source[:, a, :] = values[:, a * PLANE : (a + 1) * PLANE]
    tiles = [source[child[0, o]] for o in range(8)]
    lhs = jnp.concatenate(
        [jnp.concatenate(tiles[0:4], axis=1), jnp.concatenate(tiles[4:8], axis=1)], axis=0
    ).astype(BF16)
    both = dot(lhs, comp[...])
    partial = both[:, :PLANE] + both[:, PLANE:]
    compressed = None
    for k in range(16):
        term = rows_c[k, :, :PLANE] * partial[k : k + 1, :]
        compressed = term if compressed is None else compressed + term
    leaf_row = leaf[...].astype(F32)
    leaf_tile = jnp.concatenate(
        [leaf_row[:, a * PLANE : (a + 1) * PLANE] for a in range(8)], axis=0
    )
    middle = jnp.where(refined[0] > 0, compressed, leaf_tile).astype(BF16).astype(F32)

    row_at = (octant >> 2) * 8
    inner = row_mix([rows_c[row_at + x, :, :PLANE] for x in range(8)], middle)
    added = fine_dot(inner, contrib[octant & 3])
    low8 = low_lanes((8, 128))
    tag = jnp.full((8, 128), slot, jnp.int32).astype(F32)
    tile = jnp.where(low8, jnp.concatenate([added, added], axis=1), tag).astype(BF16)
    payload[...] = jnp.broadcast_to(tile[None], payload.shape)

    live = jnp.full((8, PLANE), refined[0], jnp.int32).astype(F32)
    upper = jnp.concatenate(two_row_mixes(rows_p, middle, PLANE), axis=0)
    spread = fine_dot(upper, prol[...])
    for o in range(8):
        i, jl = o // 4, o % 4
        part = spread[i * 8 : i * 8 + 8, jl * PLANE : (jl + 1) * PLANE]
        detail[child[0, o]] = live * (tiles[o] - part)
    for group in range(2):
        base = group * 4
        halo[group * 16 : group * 16 + 16, :] = jnp.concatenate(
            [
                jnp.concatenate([detail[base], detail[base + 1]], axis=1),
                jnp.concatenate([detail[base + 2], detail[base + 3]], axis=1),
            ],
            axis=0,
        ).astype(BF16)
    meta = jnp.where(low8, tag, jnp.full((8, 128), octant, jnp.int32).astype(F32))
    halo[32:48, :] = jnp.concatenate(
        [jnp.concatenate([middle, middle], axis=1), meta], axis=0
    ).astype(BF16)


def plane_kernel(arrived, copies):
    rows = arrived[...].astype(F32).reshape(512, 128)
    other = turned(rows)
    low = low_lanes((512, 128))
    value = jnp.where(low, rows, other)
    tag = jnp.where(low, other, rows)
    half = jnp.where(low, 0, 1)
    rhs = jnp.where((tag.astype(jnp.int32) & 1) == half, value, 0.0).astype(BF16)
    pick = jnp.where(lax.broadcasted_iota(jnp.int32, (8, 128), 1) == 0, 1.0, 0.0).astype(BF16)
    along = lax.dot_general(
        pick, tag.astype(BF16), (((1,), (1,)), ((), ())), preferred_element_type=F32
    ).astype(jnp.int32)
    p_of = lax.broadcasted_iota(jnp.int32, (8, 512), 1) & 7
    key = jnp.where(p_of == lax.broadcasted_iota(jnp.int32, (8, 512), 0), along >> 1, -1)
    hot = jnp.concatenate(
        [jnp.where(key == c2, 1.0, 0.0) for c2 in range(32)], axis=0
    ).astype(BF16)
    partial = dot(hot, rhs).astype(BF16)
    copies[...] = jnp.broadcast_to(partial[None], copies.shape)


def fine_kernel(
    fine_at, left, centre, right, factors, weighted, x_table, select,
    direct, mid_tiles, parents, table, mixed, w_ref, ab_ref,
):
    low8 = low_lanes((8, 128))
    lanes = lax.broadcasted_iota(jnp.int32, (1, 128), 1)
    table[GONE] = jnp.zeros((8, 128), F32)
    mid_tiles[27] = jnp.zeros((8, 128), F32)
    names = jnp.full((1, 128), 512, jnp.int32)
    for step_x, ref in enumerate((left, centre, right)):
        for cell in range(9):
            at = (step_x * 9 + cell) * 8
            base = cell * 48
            for group in range(2):
                both = ref[base + group * 16 : base + group * 16 + 16, :].astype(F32)
                for sub in range(2):
                    tile = both[sub * 8 : sub * 8 + 8, :]
                    other = turned(tile)
                    table[at + group * 4 + sub * 2] = jnp.where(low8, tile, other)
                    table[at + group * 4 + sub * 2 + 1] = jnp.where(low8, other, tile)
            last = ref[base + 32 : base + 48, :].astype(F32)
            mid_tiles[step_x * 9 + cell] = last[0:8, :]
            meta = last[8:9, :]
            name = meta * 8.0 + turned(meta)
            name = jnp.where(low8[0:1], name, turned(name)).astype(jnp.int32)
            names = jnp.where(lanes == step_x * 9 + cell, name, names)
    parents[...] = names

    build_tables(factors[...], weighted[...], select[...], ab_ref, w_ref)

    def source(t, ex, e):
        if e > 8:
            return table[GONE]
        return table[fine_at[t, ex * 9 + e]]

    for pair in range(4):
        pieces = []
        for t in (2 * pair, 2 * pair + 1):
            for ep in range(5):
                pieces.append(
                    jnp.concatenate(
                        [
                            jnp.where(low8, source(t, ex, 2 * ep), source(t, ex, 2 * ep + 1))
                            for ex in range(3)
                        ],
                        axis=0,
                    ).astype(BF16)
                )
        product = dot(x_table[...], jnp.concatenate(pieces, axis=1))
        for n in range(TERMS):
            quad, term = n // 4, n % 4
            tile = jnp.concatenate(
                [product[n * 8 : n * 8 + 8, :640], product[n * 8 : n * 8 + 8, 640:]], axis=0
            )
            row = term * PLANE + pair * 16
            mixed[quad, row : row + 16, :] = tile.astype(BF16)
    result = None
    for quad in range(QUADS):
        part = dot(mixed[quad], w_ref[quad])
        result = part if result is None else result + part
    direct[...] = diagonal_sum(result, PLANE).reshape(8, 8, PLANE)


def last_kernel(
    child, parent, refined, mid_at, coarse_at, parents,
    planes, mid_tiles, direct, factors, weighted, x_tables, select, rows_p, prol, single, mids,
    fine_out, mid_out, coarse, back, w_mid, w_coarse, ab_ref,
):
    build_tables(factors[0], weighted[0], select[...], ab_ref, w_mid)
    build_tables(factors[1], weighted[1], select[...], ab_ref, w_coarse)
    low8 = low_lanes((8, 128))
    total = None
    for plane in range(8):
        term = planes[plane].astype(F32)
        total = term if total is None else total + term
    for c2 in range(32):
        tile = total[c2 * 8 : c2 * 8 + 8, :]
        other = turned(tile)
        coarse[2 * c2] = jnp.where(low8, tile, other)
        coarse[2 * c2 + 1] = jnp.where(low8, other, tile)
    coarse[64] = jnp.zeros((8, 128), F32)
    octant = parent[0] & 7

    def coarse_source(ex, e):
        return coarse[coarse_at[0, ex * 9 + e if e < 9 else 27]]

    sources = jnp.concatenate(
        [
            jnp.concatenate(
                [
                    jnp.where(low8, coarse_source(ex, 2 * ep), coarse_source(ex, 2 * ep + 1))
                    for ex in range(3)
                ],
                axis=0,
            ).astype(BF16)
            for ep in range(5)
        ],
        axis=1,
    )
    coarse_result = apply_one(sources, x_tables[1], w_coarse)

    uppers, octants, owns = [], [], []
    for ep in range(5):
        for ex in range(3):
            first = mid_at[0, ex * 9 + 2 * ep]
            second = mid_at[0, ex * 9 + 2 * ep + 1 if ep < 4 else 27]
            name_1, name_2 = parents[0, first], parents[0, second]
            owns.append(jnp.where(low8, mid_tiles[first], mid_tiles[second]))
            both = jnp.where(low8, coarse[name_1 >> 3], coarse[name_2 >> 3])
            named = jnp.where(low8, name_1 & 7, name_2 & 7)
            octants.append(named)
            mix_0, mix_1 = two_row_mixes(rows_p, both, 128)
            uppers.append(jnp.where(named >= 4, mix_1, mix_0))
    stacked = jnp.concatenate(uppers, axis=0)
    high = stacked.astype(BF16).astype(F32)
    spread = dot(jnp.concatenate([high, stacked - high], axis=0).astype(BF16), mids[...])
    spread = spread[:120, :512] + spread[120:, :512] + spread[:120, 512:]
    pieces = []
    for ep in range(5):
        tiles = []
        for ex in range(3):
            at = ep * 3 + ex
            which = octants[at] & 3
            chosen = spread[at * 8 : at * 8 + 8, 0:128]
            for jl in range(1, 4):
                chosen = jnp.where(
                    which == jl, spread[at * 8 : at * 8 + 8, jl * 128 : jl * 128 + 128], chosen
                )
            tiles.append(owns[at] - chosen)
        pieces.append(jnp.concatenate(tiles, axis=0).astype(BF16))
    mid_result = apply_one(jnp.concatenate(pieces, axis=1), x_tables[0], w_mid)

    row_at = (octant >> 2) * 8
    upper = row_mix([rows_p[row_at + p, :, :PLANE] for p in range(8)], coarse_result)
    middle = mid_result + fine_dot(upper, single[octant & 3])
    for a in range(8):
        mid_out[:, a * PLANE : (a + 1) * PLANE] = middle[a : a + 1, :]
    live = jnp.full((8, PLANE), refined[0], jnp.int32).astype(F32)
    upper = jnp.concatenate(two_row_mixes(rows_p, middle, PLANE), axis=0)
    spread = fine_dot(upper, prol[...])
    for o in range(8):
        i, jl = o // 4, o % 4
        slot = child[0, o]
        part = spread[i * 8 : i * 8 + 8, jl * PLANE : (jl + 1) * PLANE]
        back[slot] = live * (direct[slot] + part)
    for a in range(8):
        fine_out[:, a * PLANE : (a + 1) * PLANE] = back[:, a, :]


def call(kernel, kinds, outs, scratch, flops, *args):
    vmem = pl.BlockSpec(memory_space=pltpu.VMEM)
    smem = pl.BlockSpec(memory_space=pltpu.SMEM)
    moved = sum(math.prod(x.shape) * x.dtype.itemsize for x in (*args, *outs))
    return pl.pallas_call(
        kernel,
        out_shape=outs,
        in_specs=[smem if kind == "s" else vmem for kind in kinds],
        out_specs=[vmem] * len(outs),
        scratch_shapes=scratch,
        compiler_params=pltpu.CompilerParams(vmem_limit_bytes=VMEM_LIMIT),
        cost_estimate=pl.CostEstimate(flops=flops, bytes_accessed=moved, transcendentals=0),
        name=kernel.__name__,
    )(*args)


def both_ways(x, axis):
    count = lax.axis_size(axis)
    ends = count - 1
    before = lax.ppermute(x, axis, [(i, i + 1) for i in range(ends)])
    after = lax.ppermute(x, axis, [(i + 1, i) for i in range(ends)])
    return before, after


def shards(
    fine_coef, mid_leaf, mid_child, mid_parent, mid_refined,
    fine_nbr, mid_nbr, coarse_nbr, op_factor, term_weight,
):
    tables = filter_tables()
    select = jnp.asarray(select_tables())
    comp, prol, contrib, single, mids, rows_c, rows_p = (
        jnp.asarray(tables[name])
        for name in ("comp", "prol", "contrib", "single", "mids", "rows_c", "rows_p")
    )
    six = op_factor.reshape(3, QUADS, 4, 3, 8, 8)
    factors = six.transpose(0, 1, 3, 5, 2, 4).reshape(3, QUADS * 24, 32)
    weights = jnp.broadcast_to(
        jnp.repeat(term_weight.reshape(QUADS, 1, 4), 8, axis=2), (QUADS, 24, 32)
    ).reshape(QUADS * 24, 32)
    weighted = factors * weights[None]
    x_tables = op_factor.transpose(0, 1, 3, 2, 4).reshape(3, TERMS * 8, 24).astype(BF16)

    sds = jax.ShapeDtypeStruct
    halo, payload, fine_at, mid_at, coarse_at = call(
        first_kernel,
        "sssvvvvvvvvvv",
        [
            sds((48, 128), BF16),
            sds((64, 8, 128), BF16),
            sds((8, 27), jnp.int32),
            sds((1, 32), jnp.int32),
            sds((1, 32), jnp.int32),
        ],
        [pltpu.VMEM((8, 8, PLANE), F32), pltpu.VMEM((8, 8, PLANE), F32)],
        2_000_000,
        mid_child, mid_parent, mid_refined, fine_nbr, mid_nbr, coarse_nbr, fine_coef, mid_leaf,
        comp, prol, contrib, rows_c, rows_p,
    )
    arrived = lax.all_to_all(payload, ("gy", "gz"), 0, 0, tiled=True)
    before, after = both_ways(halo, "gz")
    line = jnp.concatenate([before, halo, after], axis=0)
    before, after = both_ways(line, "gy")
    sheet = jnp.concatenate([before, line, after], axis=0)
    before, after = both_ways(sheet, "gx")

    (copies,) = call(
        plane_kernel, "v", [sds((8, 256, 128), BF16)], [], 33_000_000, arrived
    )
    planes = lax.all_to_all(copies, "gx", 0, 0, tiled=True)

    direct, mid_tiles, parents = call(
        fine_kernel,
        "svvvvvvv",
        [
            sds((8, 8, PLANE), F32),
            sds((28, 8, 128), F32),
            sds((1, 128), jnp.int32),
        ],
        [
            pltpu.VMEM((GONE + 1, 8, 128), F32),
            pltpu.VMEM((QUADS, 256, ROWS_W), BF16),
            pltpu.VMEM((QUADS, ROWS_W, 256), BF16),
            pltpu.VMEM((QUADS, 24, 512), F32),
        ],
        700_000_000,
        fine_at, before, sheet, after, factors[0], weighted[0], x_tables[0], select,
    )
    fine_out, mid_out = call(
        last_kernel,
        "ssssssvvvvvvvvvvv",
        [sds((8, 512), F32), sds((1, 512), F32)],
        [
            pltpu.VMEM((65, 8, 128), F32),
            pltpu.VMEM((8, 8, PLANE), F32),
            pltpu.VMEM((QUADS, ROWS_W, 256), BF16),
            pltpu.VMEM((QUADS, ROWS_W, 256), BF16),
            pltpu.VMEM((QUADS, 24, 512), F32),
        ],
        200_000_000,
        mid_child, mid_parent, mid_refined, mid_at, coarse_at, parents,
        planes, mid_tiles, direct, factors[1:], weighted[1:], x_tables[1:], select,
        rows_p, prol, single, mids,
    )
    return fine_out, mid_out


def solution(mesh):
    cells = ("gx", "gy", "gz")
    rows = P(cells, None)
    return jax.shard_map(
        shards,
        mesh=mesh,
        in_specs=(rows, rows, rows, P(cells), P(cells), rows, rows, P(), P(), P()),
        out_specs=(rows, rows),
        check_vma=False,
    )
```

```python
import functools
import math

import jax
import jax.numpy as jnp
import ml_dtypes
import numpy as np
from jax import lax
from jax.experimental import pallas as pl
from jax.experimental.pallas import tpu as pltpu
from jax.sharding import PartitionSpec as P

K = 8
PLANE = 64
TERMS = 32
QUADS = 8
ROWS_W = 640
GONE = 27 * 10
BF16 = jnp.bfloat16
F32 = jnp.float32
VMEM_LIMIT = 40 * 1024 * 1024


def poly_multiply(left, right):
    result = [0.0] * (len(left) + len(right) - 1)
    for first, left_coef in enumerate(left):
        for second, right_coef in enumerate(right):
            result[first + second] += left_coef * right_coef
    return result


def poly_compose(coeffs, factor, offset):
    result = [0.0]
    power_term = [1.0]
    for coef in coeffs:
        padded = result + [0.0] * (len(power_term) - len(result))
        result = [padded[place] + coef * power_term[place] for place in range(len(power_term))]
        power_term = poly_multiply(power_term, [offset, factor])
    return result


def legendre_table(basis_order):
    polys = [[1.0], [0.0, 1.0]]
    for degree in range(1, basis_order):
        upper = [0.0] + [(2 * degree + 1) * coef for coef in polys[degree]]
        lower = [degree * coef for coef in polys[degree - 1]] + [0.0] * (
            len(upper) - len(polys[degree - 1])
        )
        polys.append([(upper[place] - lower[place]) / (degree + 1) for place in range(len(upper))])
    return [
        [math.sqrt(2 * degree + 1) * coef for coef in poly_compose(polys[degree], 2.0, -1.0)]
        for degree in range(basis_order)
    ]


@functools.cache
def two_scale(basis_order):
    shifted = legendre_table(basis_order)
    filters = np.zeros((2, basis_order, basis_order))
    for which_half in range(2):
        for row_at in range(basis_order):
            halved = poly_compose(shifted[row_at], 0.5, 0.5 * which_half)
            for col_at in range(basis_order):
                product = poly_multiply(halved, shifted[col_at])
                total = sum((coef / (place + 1) for place, coef in enumerate(product)))
                filters[which_half, row_at, col_at] = total / math.sqrt(2.0)
    return filters.astype(np.float32).astype(np.float64)


def two_parts(matrix):
    high = matrix.astype(ml_dtypes.bfloat16)
    low = (matrix - high.astype(np.float64)).astype(ml_dtypes.bfloat16)
    return high, low


@functools.cache
def filter_tables():
    h = two_scale(K)
    pair = np.einsum("jqy,lrz->jlqryz", h, h).reshape(4, PLANE, PLANE)
    to_coarse = pair.transpose(0, 2, 1).reshape(4 * PLANE, PLANE)
    comp = np.concatenate(two_parts(to_coarse), axis=1)
    to_fine = pair.transpose(1, 0, 2).reshape(PLANE, 4 * PLANE)
    prol = np.concatenate(two_parts(to_fine), axis=1)
    contrib = np.stack([np.concatenate(two_parts(pair[k].T), axis=1) for k in range(4)])
    single = np.stack([np.concatenate(two_parts(pair[k]), axis=1) for k in range(4)])
    mid = np.zeros((2, PLANE, 4, 2, PLANE))
    for half in range(2):
        mid[half, :, :, half, :] = pair.transpose(1, 0, 2)
    mids = np.concatenate(two_parts(mid.reshape(128, 512)), axis=1)
    rows_c = np.broadcast_to(h.transpose(0, 2, 1).reshape(16, 8)[:, :, None], (16, 8, 128))
    rows_p = np.broadcast_to(h.reshape(16, 8)[:, :, None], (16, 8, 128))
    return dict(
        comp=comp,
        prol=prol,
        contrib=contrib,
        single=single,
        mids=mids,
        rows_c=np.ascontiguousarray(rows_c).astype(np.float32),
        rows_p=np.ascontiguousarray(rows_p).astype(np.float32),
    )


@functools.cache
def select_tables():
    out = np.arange(256) // TERMS
    term = np.arange(256) % TERMS
    col = np.arange(256)
    group = term[:, None] % 4 == (col // PLANE)[None, :]
    left = group & (out[:, None] == (col // 8 % 8)[None, :])
    right = group & (out[:, None] == (col % 8)[None, :])
    turn = (term[None, :] == (col // 8)[:, None]) & (out[None, :] == (col % 8)[:, None])
    return np.concatenate([left, right, turn], axis=1).astype(ml_dtypes.bfloat16)


def split(value):
    high = value.astype(BF16)
    return high, (value - high.astype(F32)).astype(BF16)


def dot(left, right):
    return jnp.dot(left, right, preferred_element_type=F32)


def fine_dot(value, table):
    rows = value.shape[0]
    width = table.shape[1] // 2
    if rows % 16 == 0:
        result = dot(jnp.concatenate(split(value), axis=0), table)
    else:
        high = value.astype(BF16).astype(F32)
        result = dot(jnp.concatenate([high, value - high], axis=0).astype(BF16), table)
    return result[:rows, :width] + result[rows:, :width] + result[:rows, width:]


def low_lanes(shape):
    return lax.broadcasted_iota(jnp.int32, shape, len(shape) - 1) < PLANE


def turned(value):
    return pltpu.roll(value, PLANE, value.ndim - 1)


def row_mix(tables, tile):
    total = None
    for p in range(8):
        term = tables[p] * tile[p : p + 1, :]
        total = term if total is None else total + term
    return total


def two_row_mixes(rows_ref, tile, width):
    return [
        row_mix([rows_ref[i * 8 + p, :, :width] for p in range(8)], tile) for i in range(2)
    ]


def local_cell(device, own):
    step_x = (device >> 6) - (own >> 6) + 1
    step_y = ((device >> 3) & 7) - ((own >> 3) & 7) + 1
    step_z = (device & 7) - (own & 7) + 1
    return step_x * 9 + step_y * 3 + step_z


def tables_kernel(factors, weights, select, sheet, w_ref, x_ref, tiles, ab_ref):
    lane = lax.broadcasted_iota(jnp.int32, (24, 256), 1)
    quad_of = (lane & 31) >> 2
    weight = jnp.concatenate([weights[...]] * 8, axis=1)
    weighted, plain = [], []
    for level in range(3):
        rows = []
        for e in range(3):
            rows.append(
                jnp.concatenate(
                    [factors[level, e * 64 + b * 8 : e * 64 + b * 8 + 8, :] for b in range(8)],
                    axis=1,
                )
            )
        values = jnp.concatenate(rows, axis=0)
        scaled = values * weight
        for quad in range(QUADS):
            weighted.append(jnp.where(quad_of == quad, scaled, 0.0))
            plain.append(jnp.where(quad_of == quad, values, 0.0))
        x_ref[level] = lax.dot_general(
            select[:, 512:768],
            values.astype(BF16),
            (((1,), (1,)), ((), ())),
            preferred_element_type=F32,
        ).astype(BF16)
    for which, parts in enumerate((weighted, plain)):
        both = dot(
            jnp.concatenate(split(jnp.concatenate(parts, axis=0)), axis=0),
            select[:, which * 256 : which * 256 + 256],
        )
        ab_ref[which] = (both[:576] + both[576:]).reshape(24, 24, 256)

    def one_quad(at, carry):
        inner = [ab_ref[1, at, ez * 8 : ez * 8 + 8, :] for ez in range(3)]
        for ey in range(3):
            for pair in range(4):
                row = ey * 8 + 2 * pair
                first = ab_ref[0, at, row : row + 1, :]
                second = ab_ref[0, at, row + 1 : row + 2, :]
                for ez in range(3):
                    tile = jnp.concatenate([first * inner[ez], second * inner[ez]], axis=0)
                    to = (ey * 3 + ez) * PLANE + pair * 16
                    w_ref[at, to : to + 16, :] = tile.astype(BF16)
        w_ref[at, 576:640, :] = jnp.zeros((64, 256), BF16)
        return carry

    lax.fori_loop(0, 3 * QUADS, one_quad, 0)
    for cell in range(9):
        spread_cell(sheet, cell, tiles, cell)


def spread_cell(sheet, cell, tiles, to):
    low = low_lanes((8, 128))
    base = cell * 48
    for group in range(2):
        both = sheet[base + group * 16 : base + group * 16 + 16, :].astype(F32)
        for sub in range(2):
            tile = both[sub * 8 : sub * 8 + 8, :]
            other = turned(tile)
            tiles[to * 10 + group * 4 + sub * 2] = jnp.where(low, tile, other)
            tiles[to * 10 + group * 4 + sub * 2 + 1] = jnp.where(low, other, tile)
    last = sheet[base + 32 : base + 48, :].astype(F32)
    tiles[to * 10 + 8] = last[0:8, :]
    tiles[to * 10 + 9] = last[8:16, :]


def diagonal_sum(result, rows):
    total = None
    for term in range(4):
        piece = result[term * rows : (term + 1) * rows, term * PLANE : (term + 1) * PLANE]
        total = piece if total is None else total + piece
    return total


def apply_one(sources, x_table, w_ref, base):
    mixed = dot(x_table, sources).astype(BF16)
    result = None
    for quad in range(QUADS):
        part = dot(mixed[quad * 32 : quad * 32 + 32, :], w_ref[base + quad])
        result = part if result is None else result + part
    return diagonal_sum(result, 8)


def first_kernel(
    child_h, parent_h, refined_h, fine_h, mid_h, coarse_h, coef_h, leaf_h, filters_h, rows_h,
    halo, payload, numbers,
    child, parent, refined, child_v, fine_nbr, mid_nbr, coarse_nbr, coef, leaf, filters, rows,
    source, detail, sems,
):
    copies = [
        pltpu.make_async_copy(there, here, sems.at[at])
        for at, (there, here) in enumerate(
            (
                (coef_h, coef),
                (filters_h, filters),
                (rows_h, rows),
                (child_h, child),
                (parent_h, parent),
                (refined_h, refined),
                (leaf_h, leaf),
                (child_h, child_v),
                (fine_h, fine_nbr),
                (mid_h, mid_nbr),
                (coarse_h, coarse_nbr),
            )
        )
    ]
    for copy in copies:
        copy.start()
    for copy in copies:
        copy.wait()
    comp = filters[0:256, :]
    prol = jnp.concatenate([filters[256 + 64 * k : 320 + 64 * k, :] for k in range(4)], axis=1)
    slot = parent[0] >> 3
    octant = parent[0] & 7
    near = fine_nbr[...]
    own = near[:, 13:14] >> 3
    cell = local_cell(near >> 3, own) * 10 + (near & 7)
    numbers[0:8, 0:27] = jnp.where(near >= 0, cell, GONE)
    near_mid = mid_nbr[...]
    own_mid = near_mid[:, 13:14]
    numbers[8:9, 0:27] = jnp.where(near_mid >= 0, local_cell(near_mid, own_mid), 27)
    numbers[8:9, 27:28] = jnp.full((1, 1), 27, jnp.int32)
    hot = jnp.where(lax.broadcasted_iota(jnp.int32, (8, 64), 1) == slot, 1.0, 0.0).astype(BF16)
    near_coarse = lax.dot_general(
        hot,
        coarse_nbr[...].astype(F32).astype(BF16),
        (((1,), (1,)), ((), ())),
        preferred_element_type=F32,
    )[0:1].astype(jnp.int32)
    numbers[9:10, 0:27] = jnp.where(near_coarse >= 0, near_coarse, 64)
    numbers[9:10, 27:28] = jnp.full((1, 1), 64, jnp.int32)
    numbers[10:11, 0:8] = child_v[...]
    numbers[10:11, 8:9] = jnp.full((1, 1), parent[0], jnp.int32)
    numbers[10:11, 9:10] = jnp.full((1, 1), refined[0], jnp.int32)

    values = coef[...].astype(F32)
    for a in range(8):
        source[:, a, :] = values[:, a * PLANE : (a + 1) * PLANE]
    tiles = [source[child[0, o]] for o in range(8)]
    lhs = jnp.concatenate(
        [jnp.concatenate(tiles[0:4], axis=1), jnp.concatenate(tiles[4:8], axis=1)], axis=0
    ).astype(BF16)
    both = dot(lhs, comp)
    partial = both[:, :PLANE] + both[:, PLANE:]
    compressed = None
    for k in range(16):
        term = rows[k, :, :PLANE] * partial[k : k + 1, :]
        compressed = term if compressed is None else compressed + term
    leaf_row = leaf[...].astype(F32)
    leaf_tile = jnp.concatenate(
        [leaf_row[:, a * PLANE : (a + 1) * PLANE] for a in range(8)], axis=0
    )
    middle = jnp.where(refined[0] > 0, compressed, leaf_tile).astype(BF16).astype(F32)

    row_at = (octant >> 2) * 8
    inner = row_mix([rows[row_at + x, :, :PLANE] for x in range(8)], middle)
    table = filters[pl.ds(pl.multiple_of(512 + (octant & 3) * 64, 64), 64), :]
    added = fine_dot(inner, table)
    low8 = low_lanes((8, 128))
    tag = jnp.full((8, 128), slot, jnp.int32).astype(F32)
    tile = jnp.where(low8, jnp.concatenate([added, added], axis=1), tag).astype(BF16)
    payload[...] = jnp.broadcast_to(tile[None], payload.shape)

    live = jnp.full((8, PLANE), refined[0], jnp.int32).astype(F32)
    upper = jnp.concatenate(two_row_mixes(rows.at[16:32], middle, PLANE), axis=0)
    spread = fine_dot(upper, prol)
    for o in range(8):
        i, jl = o // 4, o % 4
        part = spread[i * 8 : i * 8 + 8, jl * PLANE : (jl + 1) * PLANE]
        detail[child[0, o]] = live * (tiles[o] - part)
    for group in range(2):
        base = group * 4
        halo[group * 16 : group * 16 + 16, :] = jnp.concatenate(
            [
                jnp.concatenate([detail[base], detail[base + 1]], axis=1),
                jnp.concatenate([detail[base + 2], detail[base + 3]], axis=1),
            ],
            axis=0,
        ).astype(BF16)
    meta = jnp.where(low8, tag, jnp.full((8, 128), octant, jnp.int32).astype(F32))
    halo[32:48, :] = jnp.concatenate(
        [jnp.concatenate([middle, middle], axis=1), meta], axis=0
    ).astype(BF16)


def plane_kernel(arrived, copies):
    rows = arrived[...].astype(F32).reshape(512, 128)
    other = turned(rows)
    low = low_lanes((512, 128))
    value = jnp.where(low, rows, other)
    tag = jnp.where(low, other, rows)
    half = jnp.where(low, 0, 1)
    rhs = jnp.where((tag.astype(jnp.int32) & 1) == half, value, 0.0).astype(BF16)
    pick = jnp.where(lax.broadcasted_iota(jnp.int32, (8, 128), 1) == 0, 1.0, 0.0).astype(BF16)
    along = lax.dot_general(
        pick, tag.astype(BF16), (((1,), (1,)), ((), ())), preferred_element_type=F32
    ).astype(jnp.int32)
    p_of = lax.broadcasted_iota(jnp.int32, (8, 512), 1) & 7
    key = jnp.where(p_of == lax.broadcasted_iota(jnp.int32, (8, 512), 0), along >> 1, -1)
    hot = jnp.concatenate(
        [jnp.where(key == c2, 1.0, 0.0) for c2 in range(32)], axis=0
    ).astype(BF16)
    partial = dot(hot, rhs).astype(BF16)
    copies[...] = jnp.broadcast_to(partial[None], copies.shape)


def pair_of(first, second):
    return jnp.where(low_lanes((8, 128)), first, second)


def last_kernel(
    numbers, left, centre, right, planes, w_ref, x_ref, rows_p, filters, mids,
    fine_out, mid_out,
    table, mixed, coarse, back, names_v, names_s, sem,
):
    lanes = lax.broadcasted_iota(jnp.int32, (1, 128), 1)
    low8 = low_lanes((8, 128))
    table[GONE] = jnp.zeros((8, 128), F32)
    table[GONE + 8] = jnp.zeros((8, 128), F32)
    for cell in range(9):
        spread_cell(left, cell, table, cell)
        spread_cell(right, cell, table, 18 + cell)
    for at in range(90):
        table[90 + at] = centre[at]
    names = jnp.full((1, 128), 512, jnp.int32)
    for cell in range(27):
        meta = table[cell * 10 + 9, 0:1, :]
        other = turned(meta)
        name = jnp.where(low8[0:1], meta * 8.0 + other, other * 8.0 + meta).astype(jnp.int32)
        names = jnp.where(lanes == cell, name, names)
    names_v[...] = names
    fetch = pltpu.make_async_copy(names_v, names_s, sem)
    fetch.start()

    def source(t, ex, e):
        if e > 8:
            return table[GONE]
        return table[numbers[t, ex * 9 + e]]

    for pair in range(4):
        pieces = []
        for t in (2 * pair, 2 * pair + 1):
            for ep in range(5):
                pieces.append(
                    jnp.concatenate(
                        [
                            pair_of(source(t, ex, 2 * ep), source(t, ex, 2 * ep + 1))
                            for ex in range(3)
                        ],
                        axis=0,
                    ).astype(BF16)
                )
        product = dot(x_ref[0], jnp.concatenate(pieces, axis=1))
        for n in range(TERMS):
            quad, term = n // 4, n % 4
            tile = jnp.concatenate(
                [product[n * 8 : n * 8 + 8, :640], product[n * 8 : n * 8 + 8, 640:]], axis=0
            )
            row = term * PLANE + pair * 16
            mixed[quad, row : row + 16, :] = tile.astype(BF16)
    result = None
    for quad in range(QUADS):
        part = dot(mixed[quad], w_ref[quad])
        result = part if result is None else result + part
    direct = diagonal_sum(result, PLANE)

    total = None
    for plane in range(8):
        term = planes[plane].astype(F32)
        total = term if total is None else total + term
    for c2 in range(32):
        tile = total[c2 * 8 : c2 * 8 + 8, :]
        other = turned(tile)
        coarse[2 * c2] = jnp.where(low8, tile, other)
        coarse[2 * c2 + 1] = jnp.where(low8, other, tile)
    coarse[64] = jnp.zeros((8, 128), F32)
    octant = numbers[10, 8] & 7

    def coarse_source(ex, e):
        return coarse[numbers[9, ex * 9 + e if e < 9 else 27]]

    sources = jnp.concatenate(
        [
            jnp.concatenate(
                [
                    pair_of(coarse_source(ex, 2 * ep), coarse_source(ex, 2 * ep + 1))
                    for ex in range(3)
                ],
                axis=0,
            ).astype(BF16)
            for ep in range(5)
        ],
        axis=1,
    )
    coarse_result = apply_one(sources, x_ref[2], w_ref, 16)

    fetch.wait()
    uppers, octants, owns = [], [], []
    for ep in range(5):
        for ex in range(3):
            first = numbers[8, ex * 9 + 2 * ep]
            second = numbers[8, ex * 9 + 2 * ep + 1 if ep < 4 else 27]
            name_1, name_2 = names_s[0, first], names_s[0, second]
            owns.append(pair_of(table[first * 10 + 8], table[second * 10 + 8]))
            both = pair_of(coarse[name_1 >> 3], coarse[name_2 >> 3])
            named = jnp.where(low8, name_1 & 7, name_2 & 7)
            octants.append(named)
            mix_0, mix_1 = two_row_mixes(rows_p, both, 128)
            uppers.append(jnp.where(named >= 4, mix_1, mix_0))
    stacked = jnp.concatenate(uppers, axis=0)
    high = stacked.astype(BF16).astype(F32)
    spread = dot(jnp.concatenate([high, stacked - high], axis=0).astype(BF16), mids[...])
    spread = spread[:120, :512] + spread[120:, :512] + spread[:120, 512:]
    pieces = []
    for ep in range(5):
        tiles = []
        for ex in range(3):
            at = ep * 3 + ex
            which = octants[at] & 3
            chosen = spread[at * 8 : at * 8 + 8, 0:128]
            for jl in range(1, 4):
                chosen = jnp.where(
                    which == jl, spread[at * 8 : at * 8 + 8, jl * 128 : jl * 128 + 128], chosen
                )
            tiles.append(owns[at] - chosen)
        pieces.append(jnp.concatenate(tiles, axis=0).astype(BF16))
    mid_result = apply_one(jnp.concatenate(pieces, axis=1), x_ref[1], w_ref, 8)

    row_at = (octant >> 2) * 8
    upper = row_mix([rows_p[row_at + p, :, :PLANE] for p in range(8)], coarse_result)
    single = filters[pl.ds(pl.multiple_of(256 + (octant & 3) * 64, 64), 64), :]
    middle = mid_result + fine_dot(upper, single)
    for a in range(8):
        mid_out[:, a * PLANE : (a + 1) * PLANE] = middle[a : a + 1, :]
    live = jnp.full((8, PLANE), numbers[10, 9], jnp.int32).astype(F32)
    upper = jnp.concatenate(two_row_mixes(rows_p, middle, PLANE), axis=0)
    prol = jnp.concatenate([filters[64 * k : 64 * k + 64, :] for k in range(4)], axis=1)
    spread = fine_dot(upper, prol)
    for t in range(8):
        back[t] = direct[t * 8 : t * 8 + 8, :]
    for o in range(8):
        i, jl = o // 4, o % 4
        slot = numbers[10, o]
        part = spread[i * 8 : i * 8 + 8, jl * PLANE : (jl + 1) * PLANE]
        back[slot] = live * (back[slot] + part)
    for a in range(8):
        fine_out[:, a * PLANE : (a + 1) * PLANE] = back[:, a, :]


def call(kernel, kinds, outs, scratch, flops, *args):
    spaces = {
        "s": pltpu.SMEM,
        "v": pltpu.VMEM,
        "h": pltpu.HBM,
    }
    moved = sum(math.prod(x.shape) * x.dtype.itemsize for x in (*args, *outs))
    return pl.pallas_call(
        kernel,
        out_shape=outs,
        in_specs=[pl.BlockSpec(memory_space=spaces[kind]) for kind in kinds],
        out_specs=[pl.BlockSpec(memory_space=pltpu.VMEM)] * len(outs),
        scratch_shapes=scratch,
        compiler_params=pltpu.CompilerParams(vmem_limit_bytes=VMEM_LIMIT),
        cost_estimate=pl.CostEstimate(flops=flops, bytes_accessed=moved, transcendentals=0),
        name=kernel.__name__,
    )(*args)


def both_ways(x, axis):
    count = lax.axis_size(axis)
    ends = count - 1
    before = lax.ppermute(x, axis, [(i, i + 1) for i in range(ends)])
    after = lax.ppermute(x, axis, [(i + 1, i) for i in range(ends)])
    return before, after


def shards(
    fine_coef, mid_leaf, mid_child, mid_parent, mid_refined,
    fine_nbr, mid_nbr, coarse_nbr, op_factor, term_weight,
):
    tables = filter_tables()
    select = jnp.asarray(select_tables())
    prol_rows = np.concatenate(np.split(tables["prol"], 4, axis=1), axis=0)
    single_rows = tables["single"].reshape(256, 128)
    first_filters = jnp.asarray(
        np.concatenate([tables["comp"], prol_rows, tables["contrib"].reshape(256, 128)])
    )
    last_filters = jnp.asarray(np.concatenate([prol_rows, single_rows]))
    rows_both = jnp.asarray(np.concatenate([tables["rows_c"], tables["rows_p"]]))
    rows_p = jnp.asarray(tables["rows_p"])
    mids = jnp.asarray(tables["mids"])
    factors = op_factor.transpose(0, 2, 3, 4, 1).reshape(3, 192, TERMS)

    sds = jax.ShapeDtypeStruct
    vmem, smem = pltpu.VMEM, pltpu.SMEM
    i32 = jnp.int32
    halo, payload, numbers = call(
        first_kernel,
        "hhhhhhhhhh",
        [sds((48, 128), BF16), sds((64, 8, 128), BF16), sds((16, 128), i32)],
        [
            smem((1, 8), i32),
            smem((1,), i32),
            smem((1,), i32),
            vmem((1, 8), i32),
            vmem((8, 27), i32),
            vmem((1, 27), i32),
            vmem((27, 64), i32),
            vmem((8, 512), BF16),
            vmem((1, 512), BF16),
            vmem((768, 128), BF16),
            vmem((32, 8, 128), F32),
            vmem((8, 8, PLANE), F32),
            vmem((8, 8, PLANE), F32),
            pltpu.SemaphoreType.DMA((11,)),
        ],
        2_000_000,
        mid_child, mid_parent, mid_refined, fine_nbr, mid_nbr, coarse_nbr.T, fine_coef, mid_leaf,
        first_filters, rows_both,
    )
    arrived = lax.all_to_all(payload, ("gy", "gz"), 0, 0, tiled=True)
    before, after = both_ways(halo, "gz")
    line = jnp.concatenate([before, halo, after], axis=0)
    before, after = both_ways(line, "gy")
    sheet = jnp.concatenate([before, line, after], axis=0)
    before, after = both_ways(sheet, "gx")

    (copies,) = call(
        plane_kernel, "v", [sds((8, 256, 128), BF16)], [], 33_000_000, arrived
    )
    planes = lax.all_to_all(copies, "gx", 0, 0, tiled=True)

    w_tables, x_tables, centre = call(
        tables_kernel,
        "vvvv",
        [
            pltpu.VMEM((3 * QUADS, ROWS_W, 256), BF16),
            pltpu.VMEM((3, 256, 24), BF16),
            pltpu.VMEM((90, 8, 128), F32),
        ],
        [vmem((2, 24, 24, 256), F32)],
        600_000_000,
        factors, term_weight.reshape(1, TERMS), select, sheet,
    )
    fine_out, mid_out = call(
        last_kernel,
        "svvvvvvvvv",
        [sds((8, 512), F32), sds((1, 512), F32)],
        [
            vmem((GONE + 9, 8, 128), F32),
            vmem((QUADS, 256, ROWS_W), BF16),
            vmem((65, 8, 128), F32),
            vmem((8, 8, PLANE), F32),
            vmem((1, 128), i32),
            smem((1, 128), i32),
            pltpu.SemaphoreType.DMA,
        ],
        900_000_000,
        numbers, before, centre, after, planes, w_tables, x_tables, rows_p, last_filters, mids,
    )
    return fine_out, mid_out


def solution(mesh):
    cells = ("gx", "gy", "gz")
    rows = P(cells, None)
    return jax.shard_map(
        shards,
        mesh=mesh,
        in_specs=(rows, rows, rows, P(cells), P(cells), rows, rows, P(), P(), P()),
        out_specs=(rows, rows),
        check_vma=False,
    )
```

```python
import functools
import math

import jax
import jax.numpy as jnp
import ml_dtypes
import numpy as np
from jax import lax
from jax.experimental import pallas as pl
from jax.experimental.pallas import tpu as pltpu
from jax.sharding import PartitionSpec as P

K = 8
PLANE = 64
TERMS = 32
QUADS = 8
ROWS_W = 640
GONE = 27 * 10
BF16 = jnp.bfloat16
F32 = jnp.float32
VMEM_LIMIT = 32 * 1024 * 1024


def poly_multiply(left, right):
    result = [0.0] * (len(left) + len(right) - 1)
    for first, left_coef in enumerate(left):
        for second, right_coef in enumerate(right):
            result[first + second] += left_coef * right_coef
    return result


def poly_compose(coeffs, factor, offset):
    result = [0.0]
    power_term = [1.0]
    for coef in coeffs:
        padded = result + [0.0] * (len(power_term) - len(result))
        result = [padded[place] + coef * power_term[place] for place in range(len(power_term))]
        power_term = poly_multiply(power_term, [offset, factor])
    return result


def legendre_table(basis_order):
    polys = [[1.0], [0.0, 1.0]]
    for degree in range(1, basis_order):
        upper = [0.0] + [(2 * degree + 1) * coef for coef in polys[degree]]
        lower = [degree * coef for coef in polys[degree - 1]] + [0.0] * (
            len(upper) - len(polys[degree - 1])
        )
        polys.append([(upper[place] - lower[place]) / (degree + 1) for place in range(len(upper))])
    return [
        [math.sqrt(2 * degree + 1) * coef for coef in poly_compose(polys[degree], 2.0, -1.0)]
        for degree in range(basis_order)
    ]


@functools.cache
def two_scale(basis_order):
    shifted = legendre_table(basis_order)
    filters = np.zeros((2, basis_order, basis_order))
    for which_half in range(2):
        for row_at in range(basis_order):
            halved = poly_compose(shifted[row_at], 0.5, 0.5 * which_half)
            for col_at in range(basis_order):
                product = poly_multiply(halved, shifted[col_at])
                total = sum((coef / (place + 1) for place, coef in enumerate(product)))
                filters[which_half, row_at, col_at] = total / math.sqrt(2.0)
    return filters.astype(np.float32).astype(np.float64)


def two_parts(matrix):
    high = matrix.astype(ml_dtypes.bfloat16)
    low = (matrix - high.astype(np.float64)).astype(ml_dtypes.bfloat16)
    return high, low


@functools.cache
def filter_tables():
    h = two_scale(K)
    pair = np.einsum("jqy,lrz->jlqryz", h, h).reshape(4, PLANE, PLANE)
    to_coarse = pair.transpose(0, 2, 1).reshape(4 * PLANE, PLANE)
    comp = np.concatenate(two_parts(to_coarse), axis=1)
    to_fine = pair.transpose(1, 0, 2).reshape(PLANE, 4 * PLANE)
    prol = np.concatenate(two_parts(to_fine), axis=1)
    contrib = np.stack([np.concatenate(two_parts(pair[k].T), axis=1) for k in range(4)])
    single = np.stack([np.concatenate(two_parts(pair[k]), axis=1) for k in range(4)])
    mid = np.zeros((2, PLANE, 4, 2, PLANE))
    for half in range(2):
        mid[half, :, :, half, :] = pair.transpose(1, 0, 2)
    mids = np.concatenate(two_parts(mid.reshape(128, 512)), axis=1)
    rows_c = np.broadcast_to(h.transpose(0, 2, 1).reshape(16, 8)[:, :, None], (16, 8, 128))
    rows_p = np.broadcast_to(h.reshape(16, 8)[:, :, None], (16, 8, 128))
    return dict(
        comp=comp,
        prol=prol,
        contrib=contrib,
        single=single,
        mids=mids,
        rows_c=np.ascontiguousarray(rows_c).astype(np.float32),
        rows_p=np.ascontiguousarray(rows_p).astype(np.float32),
    )


@functools.cache
def select_tables():
    out = np.arange(256) // TERMS
    term = np.arange(256) % TERMS
    col = np.arange(256)
    group = term[:, None] % 4 == (col // PLANE)[None, :]
    left = group & (out[:, None] == (col // 8 % 8)[None, :])
    right = group & (out[:, None] == (col % 8)[None, :])
    turn = (term[None, :] == (col // 8)[:, None]) & (out[None, :] == (col % 8)[:, None])
    return np.concatenate([left, right, turn], axis=1).astype(ml_dtypes.bfloat16)


def split(value):
    high = value.astype(BF16)
    return high, (value - high.astype(F32)).astype(BF16)


def dot(left, right):
    return jnp.dot(left, right, preferred_element_type=F32)


def fine_dot(value, table):
    rows = value.shape[0]
    width = table.shape[1] // 2
    if rows % 16 == 0:
        result = dot(jnp.concatenate(split(value), axis=0), table)
    else:
        high = value.astype(BF16).astype(F32)
        result = dot(jnp.concatenate([high, value - high], axis=0).astype(BF16), table)
    return result[:rows, :width] + result[rows:, :width] + result[:rows, width:]


def low_lanes(shape):
    return lax.broadcasted_iota(jnp.int32, shape, len(shape) - 1) < PLANE


def turned(value):
    return pltpu.roll(value, PLANE, value.ndim - 1)


def row_mix(tables, tile):
    total = None
    for p in range(8):
        term = tables[p] * tile[p : p + 1, :]
        total = term if total is None else total + term
    return total


def two_row_mixes(rows_ref, tile, width):
    return [
        row_mix([rows_ref[i * 8 + p, :, :width] for p in range(8)], tile) for i in range(2)
    ]


def fetches(sems, *pairs):
    copies = [
        pltpu.make_async_copy(there, here, sems.at[at]) for at, (there, here) in enumerate(pairs)
    ]
    for copy in copies:
        copy.start()
    return copies


def local_cell(device, own):
    step_x = (device >> 6) - (own >> 6) + 1
    step_y = ((device >> 3) & 7) - ((own >> 3) & 7) + 1
    step_z = (device & 7) - (own & 7) + 1
    return step_x * 9 + step_y * 3 + step_z


def tables_kernel(
    factors_h, weights_h, select_h, sheet,
    w_hbm, x_ref, tiles,
    ab_ref, factors, weights, select, sems, w_ref, w_sems,
):
    copies = fetches(sems, (factors_h, factors), (weights_h, weights), (select_h, select))
    for cell in range(9):
        spread_cell(sheet, cell, tiles, cell)
    for copy in copies:
        copy.wait()
    lane = lax.broadcasted_iota(jnp.int32, (24, 256), 1)
    quad_of = (lane & 31) >> 2
    weight = jnp.concatenate([weights[...]] * 8, axis=1)
    weighted, plain = [], []
    for level in range(3):
        rows = []
        for e in range(3):
            rows.append(
                jnp.concatenate(
                    [factors[level, e * 64 + b * 8 : e * 64 + b * 8 + 8, :] for b in range(8)],
                    axis=1,
                )
            )
        values = jnp.concatenate(rows, axis=0)
        scaled = values * weight
        for quad in range(QUADS):
            weighted.append(jnp.where(quad_of == quad, scaled, 0.0))
            plain.append(jnp.where(quad_of == quad, values, 0.0))
        x_ref[level] = lax.dot_general(
            select[:, 512:768],
            values.astype(BF16),
            (((1,), (1,)), ((), ())),
            preferred_element_type=F32,
        ).astype(BF16)
    for which, parts in enumerate((weighted, plain)):
        both = dot(
            jnp.concatenate(split(jnp.concatenate(parts, axis=0)), axis=0),
            select[:, which * 256 : which * 256 + 256],
        )
        ab_ref[which] = (both[:576] + both[576:]).reshape(24, 24, 256)

    def one_quad(at, carry):
        inner = [ab_ref[1, at, ez * 8 : ez * 8 + 8, :] for ez in range(3)]
        for ey in range(3):
            for pair in range(4):
                row = ey * 8 + 2 * pair
                first = ab_ref[0, at, row : row + 1, :]
                second = ab_ref[0, at, row + 1 : row + 2, :]
                for ez in range(3):
                    tile = jnp.concatenate([first * inner[ez], second * inner[ez]], axis=0)
                    to = (ey * 3 + ez) * PLANE + pair * 16
                    w_ref[at, to : to + 16, :] = tile.astype(BF16)
        return carry

    copies = []
    for level in range(3):
        lax.fori_loop(level * QUADS, (level + 1) * QUADS, one_quad, 0)
        some = pl.ds(level * QUADS, QUADS)
        copies.append(pltpu.make_async_copy(w_ref.at[some], w_hbm.at[some], w_sems.at[level]))
        copies[-1].start()
    for copy in copies:
        copy.wait()


def spread_cell(sheet, cell, tiles, to):
    low = low_lanes((8, 128))
    base = cell * 48
    for group in range(2):
        both = sheet[base + group * 16 : base + group * 16 + 16, :].astype(F32)
        for sub in range(2):
            tile = both[sub * 8 : sub * 8 + 8, :]
            other = turned(tile)
            tiles[to * 10 + group * 4 + sub * 2] = jnp.where(low, tile, other)
            tiles[to * 10 + group * 4 + sub * 2 + 1] = jnp.where(low, other, tile)
    last = sheet[base + 32 : base + 48, :].astype(F32)
    tiles[to * 10 + 8] = last[0:8, :]
    tiles[to * 10 + 9] = last[8:16, :]


def diagonal_sum(result, rows):
    total = None
    for term in range(4):
        piece = result[term * rows : (term + 1) * rows, term * PLANE : (term + 1) * PLANE]
        total = piece if total is None else total + piece
    return total


def apply_one(sources, x_table, w_ref):
    mixed = dot(x_table, sources).astype(BF16)
    result = None
    for quad in range(QUADS):
        part = dot(mixed[quad * 32 : quad * 32 + 32, :576], w_ref[quad])
        result = part if result is None else result + part
    return diagonal_sum(result, 8)


def first_kernel(
    small_h, fine_h, mid_h, coarse_h, coef_h, leaf_h, filters_h, rows_h,
    halo, payload, numbers,
    small, small_v, fine_nbr, mid_nbr, coarse_nbr, coef, leaf, filters, rows,
    source, detail, sems,
):
    copies = fetches(
        sems,
        (coef_h, coef),
        (filters_h, filters),
        (rows_h, rows),
        (small_h, small),
        (leaf_h, leaf),
        (small_h, small_v),
        (fine_h, fine_nbr),
        (mid_h, mid_nbr),
        (coarse_h, coarse_nbr),
    )
    for copy in copies:
        copy.wait()
    comp = filters[0:256, :]
    prol = jnp.concatenate([filters[256 + 64 * k : 320 + 64 * k, :] for k in range(4)], axis=1)
    slot = small[0, 8] >> 3
    octant = small[0, 8] & 7
    near = fine_nbr[...]
    own = near[:, 13:14] >> 3
    cell = local_cell(near >> 3, own) * 10 + (near & 7)
    numbers[0:8, 0:27] = jnp.where(near >= 0, cell, GONE)
    near_mid = mid_nbr[...]
    own_mid = near_mid[:, 13:14]
    numbers[8:9, 0:27] = jnp.where(near_mid >= 0, local_cell(near_mid, own_mid), 27)
    numbers[8:9, 27:28] = jnp.full((1, 1), 27, jnp.int32)
    hot = jnp.where(lax.broadcasted_iota(jnp.int32, (8, 64), 1) == slot, 1.0, 0.0).astype(BF16)
    near_coarse = lax.dot_general(
        hot,
        coarse_nbr[...].astype(F32).astype(BF16),
        (((1,), (1,)), ((), ())),
        preferred_element_type=F32,
    )[0:1].astype(jnp.int32)
    numbers[9:10, 0:27] = jnp.where(near_coarse >= 0, near_coarse, 64)
    numbers[9:10, 27:28] = jnp.full((1, 1), 64, jnp.int32)
    numbers[10:11, 0:10] = small_v[...]

    values = coef[...].astype(F32)
    for a in range(8):
        source[:, a, :] = values[:, a * PLANE : (a + 1) * PLANE]
    tiles = [source[small[0, o]] for o in range(8)]
    lhs = jnp.concatenate(
        [jnp.concatenate(tiles[0:4], axis=1), jnp.concatenate(tiles[4:8], axis=1)], axis=0
    ).astype(BF16)
    both = dot(lhs, comp)
    partial = both[:, :PLANE] + both[:, PLANE:]
    compressed = None
    for k in range(16):
        term = rows[k, :, :PLANE] * partial[k : k + 1, :]
        compressed = term if compressed is None else compressed + term
    leaf_row = leaf[...].astype(F32)
    leaf_tile = jnp.concatenate(
        [leaf_row[:, a * PLANE : (a + 1) * PLANE] for a in range(8)], axis=0
    )
    middle = jnp.where(small[0, 9] > 0, compressed, leaf_tile).astype(BF16).astype(F32)

    row_at = (octant >> 2) * 8
    inner = row_mix([rows[row_at + x, :, :PLANE] for x in range(8)], middle)
    table = filters[pl.ds(pl.multiple_of(512 + (octant & 3) * 64, 64), 64), :]
    added = fine_dot(inner, table)
    low8 = low_lanes((8, 128))
    tag = jnp.full((8, 128), slot, jnp.int32).astype(F32)
    tile = jnp.where(low8, jnp.concatenate([added, added], axis=1), tag).astype(BF16)
    payload[...] = jnp.broadcast_to(tile[None], payload.shape)

    live = jnp.full((8, PLANE), small[0, 9], jnp.int32).astype(F32)
    upper = jnp.concatenate(two_row_mixes(rows.at[16:32], middle, PLANE), axis=0)
    spread = fine_dot(upper, prol)
    for o in range(8):
        i, jl = o // 4, o % 4
        part = spread[i * 8 : i * 8 + 8, jl * PLANE : (jl + 1) * PLANE]
        detail[small[0, o]] = live * (tiles[o] - part)
    for group in range(2):
        base = group * 4
        halo[group * 16 : group * 16 + 16, :] = jnp.concatenate(
            [
                jnp.concatenate([detail[base], detail[base + 1]], axis=1),
                jnp.concatenate([detail[base + 2], detail[base + 3]], axis=1),
            ],
            axis=0,
        ).astype(BF16)
    meta = jnp.where(low8, tag, jnp.full((8, 128), octant, jnp.int32).astype(F32))
    halo[32:48, :] = jnp.concatenate(
        [jnp.concatenate([middle, middle], axis=1), meta], axis=0
    ).astype(BF16)


def plane_kernel(arrived, copies):
    rows = arrived[...].astype(F32).reshape(512, 128)
    other = turned(rows)
    low = low_lanes((512, 128))
    value = jnp.where(low, rows, other)
    tag = jnp.where(low, other, rows)
    half = jnp.where(low, 0, 1)
    rhs = jnp.where((tag.astype(jnp.int32) & 1) == half, value, 0.0).astype(BF16)
    pick = jnp.where(lax.broadcasted_iota(jnp.int32, (8, 128), 1) == 0, 1.0, 0.0).astype(BF16)
    along = lax.dot_general(
        pick, tag.astype(BF16), (((1,), (1,)), ((), ())), preferred_element_type=F32
    ).astype(jnp.int32)
    p_of = lax.broadcasted_iota(jnp.int32, (8, 512), 1) & 7
    key = jnp.where(p_of == lax.broadcasted_iota(jnp.int32, (8, 512), 0), along >> 1, -1)
    hot = jnp.concatenate(
        [jnp.where(key == c2, 1.0, 0.0) for c2 in range(32)], axis=0
    ).astype(BF16)
    partial = dot(hot, rhs).astype(BF16)
    copies[...] = jnp.broadcast_to(partial[None], copies.shape)


def pair_of(first, second):
    return jnp.where(low_lanes((8, 128)), first, second)


def last_kernel(
    numbers, left, centre, right, planes, w_hbm, x_ref, rows_h, filters_h, mids_h,
    fine_out, mid_out,
    table, mixed, coarse, back, names_v, names_s, sem, rows_p, filters, mids, sems,
    w_ref, w_sems,
):
    levels = [pl.ds(level * QUADS, QUADS) for level in range(3)]
    w_copies = fetches(w_sems, *((w_hbm.at[some], w_ref.at[some]) for some in levels))
    copies = fetches(sems, (rows_h, rows_p), (filters_h, filters), (mids_h, mids))
    lanes = lax.broadcasted_iota(jnp.int32, (1, 128), 1)
    low8 = low_lanes((8, 128))
    table[GONE] = jnp.zeros((8, 128), F32)
    table[GONE + 8] = jnp.zeros((8, 128), F32)
    for cell in range(9):
        spread_cell(left, cell, table, cell)
        spread_cell(right, cell, table, 18 + cell)
    for at in range(90):
        table[90 + at] = centre[at]
    names = jnp.full((1, 128), 512, jnp.int32)
    for cell in range(27):
        meta = table[cell * 10 + 9, 0:1, :]
        other = turned(meta)
        name = jnp.where(low8[0:1], meta * 8.0 + other, other * 8.0 + meta).astype(jnp.int32)
        names = jnp.where(lanes == cell, name, names)
    names_v[...] = names
    fetch = pltpu.make_async_copy(names_v, names_s, sem)
    fetch.start()

    def source(t, ex, e):
        if e > 8:
            return table[GONE]
        return table[numbers[t, ex * 9 + e]]

    for pair in range(4):
        pieces = []
        for t in (2 * pair, 2 * pair + 1):
            for ep in range(5):
                pieces.append(
                    jnp.concatenate(
                        [
                            pair_of(source(t, ex, 2 * ep), source(t, ex, 2 * ep + 1))
                            for ex in range(3)
                        ],
                        axis=0,
                    ).astype(BF16)
                )
        product = dot(x_ref[0], jnp.concatenate(pieces, axis=1))
        for n in range(TERMS):
            quad, term = n // 4, n % 4
            tile = jnp.concatenate(
                [product[n * 8 : n * 8 + 8, :640], product[n * 8 : n * 8 + 8, 640:]], axis=0
            )
            row = term * PLANE + pair * 16
            mixed[quad, row : row + 16, :] = tile.astype(BF16)
    w_copies[0].wait()
    result = None
    for quad in range(QUADS):
        part = dot(mixed[quad, :, :576], w_ref[quad])
        result = part if result is None else result + part
    direct = diagonal_sum(result, PLANE)

    total = None
    for plane in range(8):
        term = planes[plane].astype(F32)
        total = term if total is None else total + term
    for c2 in range(32):
        tile = total[c2 * 8 : c2 * 8 + 8, :]
        other = turned(tile)
        coarse[2 * c2] = jnp.where(low8, tile, other)
        coarse[2 * c2 + 1] = jnp.where(low8, other, tile)
    coarse[64] = jnp.zeros((8, 128), F32)
    octant = numbers[10, 8] & 7

    def coarse_source(ex, e):
        return coarse[numbers[9, ex * 9 + e if e < 9 else 27]]

    sources = jnp.concatenate(
        [
            jnp.concatenate(
                [
                    pair_of(coarse_source(ex, 2 * ep), coarse_source(ex, 2 * ep + 1))
                    for ex in range(3)
                ],
                axis=0,
            ).astype(BF16)
            for ep in range(5)
        ],
        axis=1,
    )
    w_copies[2].wait()
    coarse_result = apply_one(sources, x_ref[2], w_ref.at[16:24])

    fetch.wait()
    for copy in copies:
        copy.wait()
    uppers, octants, owns = [], [], []
    for ep in range(5):
        for ex in range(3):
            first = numbers[8, ex * 9 + 2 * ep]
            second = numbers[8, ex * 9 + 2 * ep + 1 if ep < 4 else 27]
            name_1, name_2 = names_s[0, first], names_s[0, second]
            owns.append(pair_of(table[first * 10 + 8], table[second * 10 + 8]))
            both = pair_of(coarse[name_1 >> 3], coarse[name_2 >> 3])
            named = jnp.where(low8, name_1 & 7, name_2 & 7)
            octants.append(named)
            mix_0, mix_1 = two_row_mixes(rows_p, both, 128)
            uppers.append(jnp.where(named >= 4, mix_1, mix_0))
    stacked = jnp.concatenate(uppers, axis=0)
    high = stacked.astype(BF16).astype(F32)
    spread = dot(jnp.concatenate([high, stacked - high], axis=0).astype(BF16), mids[...])
    spread = spread[:120, :512] + spread[120:, :512] + spread[:120, 512:]
    pieces = []
    for ep in range(5):
        tiles = []
        for ex in range(3):
            at = ep * 3 + ex
            which = octants[at] & 3
            chosen = spread[at * 8 : at * 8 + 8, 0:128]
            for jl in range(1, 4):
                chosen = jnp.where(
                    which == jl, spread[at * 8 : at * 8 + 8, jl * 128 : jl * 128 + 128], chosen
                )
            tiles.append(owns[at] - chosen)
        pieces.append(jnp.concatenate(tiles, axis=0).astype(BF16))
    w_copies[1].wait()
    mid_result = apply_one(jnp.concatenate(pieces, axis=1), x_ref[1], w_ref.at[8:16])

    row_at = (octant >> 2) * 8
    upper = row_mix([rows_p[row_at + p, :, :PLANE] for p in range(8)], coarse_result)
    single = filters[pl.ds(pl.multiple_of(256 + (octant & 3) * 64, 64), 64), :]
    middle = mid_result + fine_dot(upper, single)
    for a in range(8):
        mid_out[:, a * PLANE : (a + 1) * PLANE] = middle[a : a + 1, :]
    live = jnp.full((8, PLANE), numbers[10, 9], jnp.int32).astype(F32)
    upper = jnp.concatenate(two_row_mixes(rows_p, middle, PLANE), axis=0)
    prol = jnp.concatenate([filters[64 * k : 64 * k + 64, :] for k in range(4)], axis=1)
    spread = fine_dot(upper, prol)
    for t in range(8):
        back[t] = direct[t * 8 : t * 8 + 8, :]
    for o in range(8):
        i, jl = o // 4, o % 4
        slot = numbers[10, o]
        part = spread[i * 8 : i * 8 + 8, jl * PLANE : (jl + 1) * PLANE]
        back[slot] = live * (back[slot] + part)
    for a in range(8):
        fine_out[:, a * PLANE : (a + 1) * PLANE] = back[:, a, :]


def call(kernel, kinds, outs, scratch, flops, *args):
    any_space = pl.BlockSpec(memory_space=pl.ANY)
    vmem = pl.BlockSpec(memory_space=pltpu.VMEM)
    specs = dict(s=pl.BlockSpec(memory_space=pltpu.SMEM), v=vmem, w=vmem, h=any_space)
    moved = sum(math.prod(x.shape) * x.dtype.itemsize for x in (*args, *outs))
    spaces = dict(w=pltpu.VMEM, h=pltpu.HBM)
    args = [
        pltpu.with_memory_space_constraint(x, spaces[kind]) if kind in spaces else x
        for kind, x in zip(kinds, args, strict=True)
    ]
    return pl.pallas_call(
        kernel,
        out_shape=outs,
        in_specs=[specs[kind] for kind in kinds],
        out_specs=[any_space if getattr(x, "memory_space", None) == pltpu.HBM else vmem for x in outs],
        scratch_shapes=scratch,
        compiler_params=pltpu.CompilerParams(vmem_limit_bytes=VMEM_LIMIT),
        cost_estimate=pl.CostEstimate(flops=flops, bytes_accessed=moved, transcendentals=0),
        name=kernel.__name__,
    )(*args)


def both_ways(x, axis):
    count = lax.axis_size(axis)
    ends = count - 1
    before = lax.ppermute(x, axis, [(i, i + 1) for i in range(ends)])
    after = lax.ppermute(x, axis, [(i + 1, i) for i in range(ends)])
    return before, after


def shards(
    fine_coef, mid_leaf, mid_child, mid_parent, mid_refined,
    fine_nbr, mid_nbr, coarse_nbr, op_factor, term_weight,
):
    tables = filter_tables()
    select = jnp.asarray(select_tables())
    prol_rows = np.concatenate(np.split(tables["prol"], 4, axis=1), axis=0)
    single_rows = tables["single"].reshape(256, 128)
    first_filters = jnp.asarray(
        np.concatenate([tables["comp"], prol_rows, tables["contrib"].reshape(256, 128)])
    )
    last_filters = jnp.asarray(np.concatenate([prol_rows, single_rows]))
    rows_both = jnp.asarray(np.concatenate([tables["rows_c"], tables["rows_p"]]))
    rows_p = jnp.asarray(tables["rows_p"])
    mids = jnp.asarray(tables["mids"])
    factors = op_factor.transpose(0, 2, 3, 4, 1).reshape(3, 192, TERMS)

    sds = jax.ShapeDtypeStruct
    vmem, smem = pltpu.VMEM, pltpu.SMEM
    i32 = jnp.int32
    at = lax.broadcasted_iota(jnp.int32, (1, 10), 1)
    named = jnp.where(at == 8, jnp.broadcast_to(mid_parent, (1, 10)), jnp.broadcast_to(mid_refined, (1, 10)))
    small = jnp.where(at < 8, jnp.pad(mid_child, ((0, 0), (0, 2))), named)
    halo, payload, numbers = call(
        first_kernel,
        "hhhhhhhh",
        [sds((48, 128), BF16), sds((64, 8, 128), BF16), sds((16, 128), i32)],
        [
            smem((1, 10), i32),
            vmem((1, 10), i32),
            vmem((8, 27), i32),
            vmem((1, 27), i32),
            vmem((27, 64), i32),
            vmem((8, 512), BF16),
            vmem((1, 512), BF16),
            vmem((768, 128), BF16),
            vmem((32, 8, 128), F32),
            vmem((8, 8, PLANE), F32),
            vmem((8, 8, PLANE), F32),
            pltpu.SemaphoreType.DMA((9,)),
        ],
        2_000_000,
        small, fine_nbr, mid_nbr, coarse_nbr.T, fine_coef, mid_leaf,
        first_filters, rows_both,
    )
    arrived = lax.all_to_all(payload, ("gy", "gz"), 0, 0, tiled=True)
    before, after = both_ways(halo, "gz")
    line = jnp.concatenate([before, halo, after], axis=0)
    before, after = both_ways(line, "gy")
    sheet = jnp.concatenate([before, line, after], axis=0)
    before, after = both_ways(sheet, "gx")

    (copies,) = call(
        plane_kernel, "v", [sds((8, 256, 128), BF16)], [], 33_000_000, arrived
    )
    planes = lax.all_to_all(copies, "gx", 0, 0, tiled=True)

    w_tables, x_tables, centre = call(
        tables_kernel,
        "hhhv",
        [
            pltpu.HBM((3 * QUADS, 576, 256), BF16),
            pltpu.VMEM((3, 256, 24), BF16),
            pltpu.VMEM((90, 8, 128), F32),
        ],
        [
            vmem((2, 24, 24, 256), F32),
            vmem((3, 192, TERMS), F32),
            vmem((1, TERMS), F32),
            vmem((256, 768), BF16),
            pltpu.SemaphoreType.DMA((3,)),
            vmem((3 * QUADS, 576, 256), BF16),
            pltpu.SemaphoreType.DMA((3,)),
        ],
        600_000_000,
        factors, term_weight.reshape(1, TERMS), select, sheet,
    )
    fine_out, mid_out = call(
        last_kernel,
        "svwvvhwhhh",
        [sds((8, 512), F32), sds((1, 512), F32)],
        [
            vmem((GONE + 9, 8, 128), F32),
            vmem((QUADS, 256, ROWS_W), BF16),
            vmem((65, 8, 128), F32),
            vmem((8, 8, PLANE), F32),
            vmem((1, 128), i32),
            smem((1, 128), i32),
            pltpu.SemaphoreType.DMA,
            vmem((16, 8, 128), F32),
            vmem((512, 128), BF16),
            vmem((128, 1024), BF16),
            pltpu.SemaphoreType.DMA((3,)),
            vmem((3 * QUADS, 576, 256), BF16),
            pltpu.SemaphoreType.DMA((3,)),
        ],
        900_000_000,
        numbers, before, centre, after, planes, w_tables, x_tables, rows_p, last_filters, mids,
    )
    return fine_out, mid_out


def solution(mesh):
    cells = ("gx", "gy", "gz")
    rows = P(cells, None)
    return jax.shard_map(
        shards,
        mesh=mesh,
        in_specs=(rows, rows, rows, P(cells), P(cells), rows, rows, P(), P(), P()),
        out_specs=(rows, rows),
        check_vma=False,
    )
```

```python
import functools
import math

import jax
import jax.numpy as jnp
import ml_dtypes
import numpy as np
from jax import lax
from jax.experimental import pallas as pl
from jax.experimental.pallas import tpu as pltpu
from jax.sharding import PartitionSpec as P

K = 8
PLANE = 64
TERMS = 32
QUADS = 8
ROWS_W = 640
GONE = 27 * 10
BF16 = jnp.bfloat16
F32 = jnp.float32
VMEM_LIMIT = 32 * 1024 * 1024


def poly_multiply(left, right):
    result = [0.0] * (len(left) + len(right) - 1)
    for first, left_coef in enumerate(left):
        for second, right_coef in enumerate(right):
            result[first + second] += left_coef * right_coef
    return result


def poly_compose(coeffs, factor, offset):
    result = [0.0]
    power_term = [1.0]
    for coef in coeffs:
        padded = result + [0.0] * (len(power_term) - len(result))
        result = [padded[place] + coef * power_term[place] for place in range(len(power_term))]
        power_term = poly_multiply(power_term, [offset, factor])
    return result


def legendre_table(basis_order):
    polys = [[1.0], [0.0, 1.0]]
    for degree in range(1, basis_order):
        upper = [0.0] + [(2 * degree + 1) * coef for coef in polys[degree]]
        lower = [degree * coef for coef in polys[degree - 1]] + [0.0] * (
            len(upper) - len(polys[degree - 1])
        )
        polys.append([(upper[place] - lower[place]) / (degree + 1) for place in range(len(upper))])
    return [
        [math.sqrt(2 * degree + 1) * coef for coef in poly_compose(polys[degree], 2.0, -1.0)]
        for degree in range(basis_order)
    ]


@functools.cache
def two_scale(basis_order):
    shifted = legendre_table(basis_order)
    filters = np.zeros((2, basis_order, basis_order))
    for which_half in range(2):
        for row_at in range(basis_order):
            halved = poly_compose(shifted[row_at], 0.5, 0.5 * which_half)
            for col_at in range(basis_order):
                product = poly_multiply(halved, shifted[col_at])
                total = sum((coef / (place + 1) for place, coef in enumerate(product)))
                filters[which_half, row_at, col_at] = total / math.sqrt(2.0)
    return filters.astype(np.float32).astype(np.float64)


def two_parts(matrix):
    high = matrix.astype(ml_dtypes.bfloat16)
    low = (matrix - high.astype(np.float64)).astype(ml_dtypes.bfloat16)
    return high, low


@functools.cache
def filter_tables():
    h = two_scale(K)
    pair = np.einsum("jqy,lrz->jlqryz", h, h).reshape(4, PLANE, PLANE)
    to_coarse = pair.transpose(0, 2, 1).reshape(4 * PLANE, PLANE)
    comp = np.concatenate(two_parts(to_coarse), axis=1)
    to_fine = pair.transpose(1, 0, 2).reshape(PLANE, 4 * PLANE)
    prol = np.concatenate(two_parts(to_fine), axis=1)
    contrib = np.stack([np.concatenate(two_parts(pair[k].T), axis=1) for k in range(4)])
    single = np.stack([np.concatenate(two_parts(pair[k]), axis=1) for k in range(4)])
    mid = np.zeros((2, PLANE, 4, 2, PLANE))
    for half in range(2):
        mid[half, :, :, half, :] = pair.transpose(1, 0, 2)
    mids = np.concatenate(two_parts(mid.reshape(128, 512)), axis=1)
    rows_c = np.broadcast_to(h.transpose(0, 2, 1).reshape(16, 8)[:, :, None], (16, 8, 128))
    rows_p = np.broadcast_to(h.reshape(16, 8)[:, :, None], (16, 8, 128))
    return dict(
        comp=comp,
        prol=prol,
        contrib=contrib,
        single=single,
        mids=mids,
        rows_c=np.ascontiguousarray(rows_c).astype(np.float32),
        rows_p=np.ascontiguousarray(rows_p).astype(np.float32),
    )


@functools.cache
def select_tables():
    out = np.arange(256) // TERMS
    term = np.arange(256) % TERMS
    col = np.arange(256)
    group = term[:, None] % 4 == (col // PLANE)[None, :]
    left = group & (out[:, None] == (col // 8 % 8)[None, :])
    right = group & (out[:, None] == (col % 8)[None, :])
    turn = (term[None, :] == (col // 8)[:, None]) & (out[None, :] == (col % 8)[:, None])
    return np.concatenate([left, right, turn], axis=1).astype(ml_dtypes.bfloat16)


def split(value):
    high = value.astype(BF16)
    return high, (value - high.astype(F32)).astype(BF16)


def dot(left, right):
    return jnp.dot(left, right, preferred_element_type=F32)


def fine_dot(value, table):
    rows = value.shape[0]
    width = table.shape[1] // 2
    if rows % 16 == 0:
        result = dot(jnp.concatenate(split(value), axis=0), table)
    else:
        high = value.astype(BF16).astype(F32)
        result = dot(jnp.concatenate([high, value - high], axis=0).astype(BF16), table)
    return result[:rows, :width] + result[rows:, :width] + result[:rows, width:]


def low_lanes(shape):
    return lax.broadcasted_iota(jnp.int32, shape, len(shape) - 1) < PLANE


def turned(value):
    return pltpu.roll(value, PLANE, value.ndim - 1)


def row_mix(tables, tile):
    total = None
    for p in range(8):
        term = tables[p] * tile[p : p + 1, :]
        total = term if total is None else total + term
    return total


def two_row_mixes(rows_ref, tile, width):
    return [
        row_mix([rows_ref[i * 8 + p, :, :width] for p in range(8)], tile) for i in range(2)
    ]


def fetches(sems, *pairs):
    copies = [
        pltpu.make_async_copy(there, here, sems.at[at]) for at, (there, here) in enumerate(pairs)
    ]
    for copy in copies:
        copy.start()
    return copies


def local_cell(device, own):
    step_x = (device >> 6) - (own >> 6) + 1
    step_y = ((device >> 3) & 7) - ((own >> 3) & 7) + 1
    step_z = (device & 7) - (own & 7) + 1
    return step_x * 9 + step_y * 3 + step_z


def tables_kernel(
    factors_h, weights_h, select_h, sheet,
    w_hbm, x_ref, tiles,
    ab_ref, factors, weights, select, sems, w_ref, w_sems,
):
    copies = fetches(sems, (factors_h, factors), (weights_h, weights), (select_h, select))
    for cell in range(9):
        spread_cell(sheet, cell, tiles, cell)
    for copy in copies:
        copy.wait()
    lane = lax.broadcasted_iota(jnp.int32, (24, 256), 1)
    quad_of = (lane & 31) >> 2
    weight = jnp.concatenate([weights[...]] * 8, axis=1)
    weighted, plain = [], []
    for level in range(3):
        rows = []
        for e in range(3):
            rows.append(
                jnp.concatenate(
                    [factors[level, e * 64 + b * 8 : e * 64 + b * 8 + 8, :] for b in range(8)],
                    axis=1,
                )
            )
        values = jnp.concatenate(rows, axis=0)
        scaled = values * weight
        for quad in range(QUADS):
            weighted.append(jnp.where(quad_of == quad, scaled, 0.0))
            plain.append(jnp.where(quad_of == quad, values, 0.0))
        x_ref[level] = lax.dot_general(
            select[:, 512:768],
            values.astype(BF16),
            (((1,), (1,)), ((), ())),
            preferred_element_type=F32,
        ).astype(BF16)
    for which, parts in enumerate((weighted, plain)):
        both = dot(
            jnp.concatenate(split(jnp.concatenate(parts, axis=0)), axis=0),
            select[:, which * 256 : which * 256 + 256],
        )
        ab_ref[which] = (both[:576] + both[576:]).reshape(24, 24, 256)

    def one_quad(at, carry):
        inner = [ab_ref[1, at, ez * 8 : ez * 8 + 8, :] for ez in range(3)]
        for ey in range(3):
            for pair in range(4):
                row = ey * 8 + 2 * pair
                first = ab_ref[0, at, row : row + 1, :]
                second = ab_ref[0, at, row + 1 : row + 2, :]
                for ez in range(3):
                    tile = jnp.concatenate([first * inner[ez], second * inner[ez]], axis=0)
                    to = (ey * 3 + ez) * PLANE + pair * 16
                    w_ref[at, to : to + 16, :] = tile.astype(BF16)
        return carry

    copies = []
    for level in range(3):
        lax.fori_loop(level * QUADS, (level + 1) * QUADS, one_quad, 0)
        some = pl.ds(level * QUADS, QUADS)
        copies.append(pltpu.make_async_copy(w_ref.at[some], w_hbm.at[some], w_sems.at[level]))
        copies[-1].start()
    for copy in copies:
        copy.wait()


def spread_cell(sheet, cell, tiles, to):
    low = low_lanes((8, 128))
    base = cell * 48
    for group in range(2):
        both = sheet[base + group * 16 : base + group * 16 + 16, :].astype(F32)
        for sub in range(2):
            tile = both[sub * 8 : sub * 8 + 8, :]
            other = turned(tile)
            tiles[to * 10 + group * 4 + sub * 2] = jnp.where(low, tile, other)
            tiles[to * 10 + group * 4 + sub * 2 + 1] = jnp.where(low, other, tile)
    last = sheet[base + 32 : base + 48, :].astype(F32)
    tiles[to * 10 + 8] = last[0:8, :]
    tiles[to * 10 + 9] = last[8:16, :]


def diagonal_sum(result, rows):
    total = None
    for term in range(4):
        piece = result[term * rows : (term + 1) * rows, term * PLANE : (term + 1) * PLANE]
        total = piece if total is None else total + piece
    return total


def apply_one(sources, x_table, w_ref):
    mixed = dot(x_table, sources).astype(BF16)
    result = None
    for quad in range(QUADS):
        part = dot(mixed[quad * 32 : quad * 32 + 32, :576], w_ref[quad])
        result = part if result is None else result + part
    return diagonal_sum(result, 8)


def first_kernel(
    parent, refined, child_h, fine_h, mid_h, coarse_h, coef_h, leaf_h, filters_h, rows_h,
    halo, payload, numbers,
    child, child_v, fine_nbr, mid_nbr, coarse_nbr, coef, leaf, filters, rows,
    source, detail, sems,
):
    copies = fetches(
        sems,
        (coef_h, coef),
        (filters_h, filters),
        (rows_h, rows),
        (child_h, child),
        (leaf_h, leaf),
        (child_h, child_v),
        (fine_h, fine_nbr),
        (mid_h, mid_nbr),
        (coarse_h, coarse_nbr),
    )
    for copy in copies:
        copy.wait()
    comp = filters[0:256, :]
    prol = jnp.concatenate([filters[256 + 64 * k : 320 + 64 * k, :] for k in range(4)], axis=1)
    slot = parent[0] >> 3
    octant = parent[0] & 7
    near = fine_nbr[...]
    own = near[:, 13:14] >> 3
    cell = local_cell(near >> 3, own) * 10 + (near & 7)
    numbers[0:8, 0:27] = jnp.where(near >= 0, cell, GONE)
    near_mid = mid_nbr[...]
    own_mid = near_mid[:, 13:14]
    numbers[8:9, 0:27] = jnp.where(near_mid >= 0, local_cell(near_mid, own_mid), 27)
    numbers[8:9, 27:28] = jnp.full((1, 1), 27, jnp.int32)
    hot = jnp.where(lax.broadcasted_iota(jnp.int32, (8, 64), 1) == slot, 1.0, 0.0).astype(BF16)
    near_coarse = lax.dot_general(
        hot,
        coarse_nbr[...].astype(F32).astype(BF16),
        (((1,), (1,)), ((), ())),
        preferred_element_type=F32,
    )[0:1].astype(jnp.int32)
    numbers[9:10, 0:27] = jnp.where(near_coarse >= 0, near_coarse, 64)
    numbers[9:10, 27:28] = jnp.full((1, 1), 64, jnp.int32)
    numbers[10:11, 0:8] = child_v[...]
    numbers[10:11, 8:9] = jnp.full((1, 1), parent[0], jnp.int32)
    numbers[10:11, 9:10] = jnp.full((1, 1), refined[0], jnp.int32)

    values = coef[...].astype(F32)
    for a in range(8):
        source[:, a, :] = values[:, a * PLANE : (a + 1) * PLANE]
    tiles = [source[child[0, o]] for o in range(8)]
    lhs = jnp.concatenate(
        [jnp.concatenate(tiles[0:4], axis=1), jnp.concatenate(tiles[4:8], axis=1)], axis=0
    ).astype(BF16)
    both = dot(lhs, comp)
    partial = both[:, :PLANE] + both[:, PLANE:]
    compressed = None
    for k in range(16):
        term = rows[k, :, :PLANE] * partial[k : k + 1, :]
        compressed = term if compressed is None else compressed + term
    leaf_row = leaf[...].astype(F32)
    leaf_tile = jnp.concatenate(
        [leaf_row[:, a * PLANE : (a + 1) * PLANE] for a in range(8)], axis=0
    )
    middle = jnp.where(refined[0] > 0, compressed, leaf_tile).astype(BF16).astype(F32)

    row_at = (octant >> 2) * 8
    inner = row_mix([rows[row_at + x, :, :PLANE] for x in range(8)], middle)
    table = filters[pl.ds(pl.multiple_of(512 + (octant & 3) * 64, 64), 64), :]
    added = fine_dot(inner, table)
    low8 = low_lanes((8, 128))
    tag = jnp.full((8, 128), slot, jnp.int32).astype(F32)
    tile = jnp.where(low8, jnp.concatenate([added, added], axis=1), tag).astype(BF16)
    payload[...] = jnp.broadcast_to(tile[None], payload.shape)

    live = jnp.full((8, PLANE), refined[0], jnp.int32).astype(F32)
    upper = jnp.concatenate(two_row_mixes(rows.at[16:32], middle, PLANE), axis=0)
    spread = fine_dot(upper, prol)
    for o in range(8):
        i, jl = o // 4, o % 4
        part = spread[i * 8 : i * 8 + 8, jl * PLANE : (jl + 1) * PLANE]
        detail[child[0, o]] = live * (tiles[o] - part)
    for group in range(2):
        base = group * 4
        halo[group * 16 : group * 16 + 16, :] = jnp.concatenate(
            [
                jnp.concatenate([detail[base], detail[base + 1]], axis=1),
                jnp.concatenate([detail[base + 2], detail[base + 3]], axis=1),
            ],
            axis=0,
        ).astype(BF16)
    meta = jnp.where(low8, tag, jnp.full((8, 128), octant, jnp.int32).astype(F32))
    halo[32:48, :] = jnp.concatenate(
        [jnp.concatenate([middle, middle], axis=1), meta], axis=0
    ).astype(BF16)


def plane_kernel(arrived, copies):
    rows = arrived[...].astype(F32).reshape(512, 128)
    other = turned(rows)
    low = low_lanes((512, 128))
    value = jnp.where(low, rows, other)
    tag = jnp.where(low, other, rows)
    half = jnp.where(low, 0, 1)
    rhs = jnp.where((tag.astype(jnp.int32) & 1) == half, value, 0.0).astype(BF16)
    pick = jnp.where(lax.broadcasted_iota(jnp.int32, (8, 128), 1) == 0, 1.0, 0.0).astype(BF16)
    along = lax.dot_general(
        pick, tag.astype(BF16), (((1,), (1,)), ((), ())), preferred_element_type=F32
    ).astype(jnp.int32)
    p_of = lax.broadcasted_iota(jnp.int32, (8, 512), 1) & 7
    key = jnp.where(p_of == lax.broadcasted_iota(jnp.int32, (8, 512), 0), along >> 1, -1)
    hot = jnp.concatenate(
        [jnp.where(key == c2, 1.0, 0.0) for c2 in range(32)], axis=0
    ).astype(BF16)
    partial = dot(hot, rhs).astype(BF16)
    copies[...] = jnp.broadcast_to(partial[None], copies.shape)


def pair_of(first, second):
    return jnp.where(low_lanes((8, 128)), first, second)


def fine_kernel(
    numbers, left, centre, right, w_hbm, x_ref,
    direct, mid_tiles, names_ref,
    table, mixed, w_ref, sems,
):
    copies = fetches(sems, (w_hbm.at[pl.ds(0, QUADS)], w_ref))
    lanes = lax.broadcasted_iota(jnp.int32, (1, 128), 1)
    low8 = low_lanes((8, 128))
    table[GONE] = jnp.zeros((8, 128), F32)
    table[GONE + 8] = jnp.zeros((8, 128), F32)
    for cell in range(9):
        spread_cell(left, cell, table, cell)
        spread_cell(right, cell, table, 18 + cell)
    for at in range(90):
        table[90 + at] = centre[at]
    names = jnp.full((1, 128), 512, jnp.int32)
    for cell in range(27):
        meta = table[cell * 10 + 9, 0:1, :]
        other = turned(meta)
        name = jnp.where(low8[0:1], meta * 8.0 + other, other * 8.0 + meta).astype(jnp.int32)
        names = jnp.where(lanes == cell, name, names)
    names_ref[...] = names
    for cell in range(28):
        mid_tiles[cell] = table[cell * 10 + 8]

    def source(t, ex, e):
        if e > 8:
            return table[GONE]
        return table[numbers[t, ex * 9 + e]]

    for pair in range(4):
        pieces = []
        for t in (2 * pair, 2 * pair + 1):
            for ep in range(5):
                pieces.append(
                    jnp.concatenate(
                        [
                            pair_of(source(t, ex, 2 * ep), source(t, ex, 2 * ep + 1))
                            for ex in range(3)
                        ],
                        axis=0,
                    ).astype(BF16)
                )
        product = dot(x_ref[0], jnp.concatenate(pieces, axis=1))
        for n in range(TERMS):
            quad, term = n // 4, n % 4
            tile = jnp.concatenate(
                [product[n * 8 : n * 8 + 8, :640], product[n * 8 : n * 8 + 8, 640:]], axis=0
            )
            row = term * PLANE + pair * 16
            mixed[quad, row : row + 16, :] = tile.astype(BF16)
    for copy in copies:
        copy.wait()
    result = None
    for quad in range(QUADS):
        part = dot(mixed[quad, :, :576], w_ref[quad])
        result = part if result is None else result + part
    direct[...] = diagonal_sum(result, PLANE).reshape(8, 8, PLANE)


def last_kernel(
    numbers, names, planes, mid_tiles, direct, w_hbm, x_ref, rows_h, filters_h, mids_h,
    fine_out, mid_out,
    coarse, back, rows_p, filters, mids, sems, w_ref, w_sems,
):
    levels = [pl.ds((level + 1) * QUADS, QUADS) for level in range(2)]
    homes = [pl.ds(level * QUADS, QUADS) for level in range(2)]
    copies = fetches(sems, (rows_h, rows_p), (filters_h, filters), (mids_h, mids))
    w_copies = fetches(
        w_sems,
        *((w_hbm.at[levels[level]], w_ref.at[homes[level]]) for level in range(2)),
    )
    low8 = low_lanes((8, 128))

    total = None
    for plane in range(8):
        term = planes[plane].astype(F32)
        total = term if total is None else total + term
    for c2 in range(32):
        tile = total[c2 * 8 : c2 * 8 + 8, :]
        other = turned(tile)
        coarse[2 * c2] = jnp.where(low8, tile, other)
        coarse[2 * c2 + 1] = jnp.where(low8, other, tile)
    coarse[64] = jnp.zeros((8, 128), F32)
    octant = numbers[10, 8] & 7

    def coarse_source(ex, e):
        return coarse[numbers[9, ex * 9 + e if e < 9 else 27]]

    sources = jnp.concatenate(
        [
            jnp.concatenate(
                [
                    pair_of(coarse_source(ex, 2 * ep), coarse_source(ex, 2 * ep + 1))
                    for ex in range(3)
                ],
                axis=0,
            ).astype(BF16)
            for ep in range(5)
        ],
        axis=1,
    )
    w_copies[1].wait()
    coarse_result = apply_one(sources, x_ref[2], w_ref.at[8:16])

    for copy in copies:
        copy.wait()
    uppers, octants, owns = [], [], []
    for ep in range(5):
        for ex in range(3):
            first = numbers[8, ex * 9 + 2 * ep]
            second = numbers[8, ex * 9 + 2 * ep + 1 if ep < 4 else 27]
            name_1, name_2 = names[0, first], names[0, second]
            owns.append(pair_of(mid_tiles[first], mid_tiles[second]))
            both = pair_of(coarse[name_1 >> 3], coarse[name_2 >> 3])
            named = jnp.where(low8, name_1 & 7, name_2 & 7)
            octants.append(named)
            mix_0, mix_1 = two_row_mixes(rows_p, both, 128)
            uppers.append(jnp.where(named >= 4, mix_1, mix_0))
    stacked = jnp.concatenate(uppers, axis=0)
    high = stacked.astype(BF16).astype(F32)
    spread = dot(jnp.concatenate([high, stacked - high], axis=0).astype(BF16), mids[...])
    spread = spread[:120, :512] + spread[120:, :512] + spread[:120, 512:]
    pieces = []
    for ep in range(5):
        tiles = []
        for ex in range(3):
            at = ep * 3 + ex
            which = octants[at] & 3
            chosen = spread[at * 8 : at * 8 + 8, 0:128]
            for jl in range(1, 4):
                chosen = jnp.where(
                    which == jl, spread[at * 8 : at * 8 + 8, jl * 128 : jl * 128 + 128], chosen
                )
            tiles.append(owns[at] - chosen)
        pieces.append(jnp.concatenate(tiles, axis=0).astype(BF16))
    w_copies[0].wait()
    mid_result = apply_one(jnp.concatenate(pieces, axis=1), x_ref[1], w_ref.at[0:8])

    row_at = (octant >> 2) * 8
    upper = row_mix([rows_p[row_at + p, :, :PLANE] for p in range(8)], coarse_result)
    single = filters[pl.ds(pl.multiple_of(256 + (octant & 3) * 64, 64), 64), :]
    middle = mid_result + fine_dot(upper, single)
    for a in range(8):
        mid_out[:, a * PLANE : (a + 1) * PLANE] = middle[a : a + 1, :]
    live = jnp.full((8, PLANE), numbers[10, 9], jnp.int32).astype(F32)
    upper = jnp.concatenate(two_row_mixes(rows_p, middle, PLANE), axis=0)
    prol = jnp.concatenate([filters[64 * k : 64 * k + 64, :] for k in range(4)], axis=1)
    spread = fine_dot(upper, prol)
    for o in range(8):
        i, jl = o // 4, o % 4
        slot = numbers[10, o]
        part = spread[i * 8 : i * 8 + 8, jl * PLANE : (jl + 1) * PLANE]
        back[slot] = live * (direct[slot] + part)
    for a in range(8):
        fine_out[:, a * PLANE : (a + 1) * PLANE] = back[:, a, :]


def call(kernel, kinds, outs, scratch, flops, *args):
    any_space = pl.BlockSpec(memory_space=pl.ANY)
    vmem = pl.BlockSpec(memory_space=pltpu.VMEM)
    specs = dict(s=pl.BlockSpec(memory_space=pltpu.SMEM), v=vmem, w=vmem, h=any_space)
    moved = sum(math.prod(x.shape) * x.dtype.itemsize for x in (*args, *outs))
    spaces = dict(w=pltpu.VMEM, h=pltpu.HBM)
    args = [
        pltpu.with_memory_space_constraint(x, spaces[kind]) if kind in spaces else x
        for kind, x in zip(kinds, args, strict=True)
    ]
    return pl.pallas_call(
        kernel,
        out_shape=outs,
        in_specs=[specs[kind] for kind in kinds],
        out_specs=[any_space if getattr(x, "memory_space", None) == pltpu.HBM else vmem for x in outs],
        scratch_shapes=scratch,
        compiler_params=pltpu.CompilerParams(vmem_limit_bytes=VMEM_LIMIT),
        cost_estimate=pl.CostEstimate(flops=flops, bytes_accessed=moved, transcendentals=0),
        name=kernel.__name__,
    )(*args)


def both_ways(x, axis):
    count = lax.axis_size(axis)
    ends = count - 1
    before = lax.ppermute(x, axis, [(i, i + 1) for i in range(ends)])
    after = lax.ppermute(x, axis, [(i + 1, i) for i in range(ends)])
    return before, after


def shards(
    fine_coef, mid_leaf, mid_child, mid_parent, mid_refined,
    fine_nbr, mid_nbr, coarse_nbr, op_factor, term_weight,
):
    tables = filter_tables()
    select = jnp.asarray(select_tables())
    prol_rows = np.concatenate(np.split(tables["prol"], 4, axis=1), axis=0)
    single_rows = tables["single"].reshape(256, 128)
    first_filters = jnp.asarray(
        np.concatenate([tables["comp"], prol_rows, tables["contrib"].reshape(256, 128)])
    )
    last_filters = jnp.asarray(np.concatenate([prol_rows, single_rows]))
    rows_both = jnp.asarray(np.concatenate([tables["rows_c"], tables["rows_p"]]))
    rows_p = jnp.asarray(tables["rows_p"])
    mids = jnp.asarray(tables["mids"])
    factors = op_factor.transpose(0, 2, 3, 4, 1).reshape(3, 192, TERMS)

    sds = jax.ShapeDtypeStruct
    vmem, smem = pltpu.VMEM, pltpu.SMEM
    i32 = jnp.int32
    halo, payload, numbers = call(
        first_kernel,
        "sshhhhhhhh",
        [sds((48, 128), BF16), sds((64, 8, 128), BF16), sds((16, 128), i32)],
        [
            smem((1, 8), i32),
            vmem((1, 8), i32),
            vmem((8, 27), i32),
            vmem((1, 27), i32),
            vmem((27, 64), i32),
            vmem((8, 512), BF16),
            vmem((1, 512), BF16),
            vmem((768, 128), BF16),
            vmem((32, 8, 128), F32),
            vmem((8, 8, PLANE), F32),
            vmem((8, 8, PLANE), F32),
            pltpu.SemaphoreType.DMA((9,)),
        ],
        2_000_000,
        mid_parent, mid_refined, mid_child, fine_nbr, mid_nbr, coarse_nbr.T, fine_coef, mid_leaf,
        first_filters, rows_both,
    )
    arrived = lax.all_to_all(payload, ("gy", "gz"), 0, 0, tiled=True)
    before, after = both_ways(halo, "gz")
    line = jnp.concatenate([before, halo, after], axis=0)
    before, after = both_ways(line, "gy")
    sheet = jnp.concatenate([before, line, after], axis=0)
    before, after = both_ways(sheet, "gx")

    (copies,) = call(
        plane_kernel, "v", [sds((8, 256, 128), BF16)], [], 33_000_000, arrived
    )
    planes = lax.all_to_all(copies, "gx", 0, 0, tiled=True)

    w_tables, x_tables, centre = call(
        tables_kernel,
        "hhhv",
        [
            pltpu.HBM((3 * QUADS, 576, 256), BF16),
            pltpu.VMEM((3, 256, 24), BF16),
            pltpu.VMEM((90, 8, 128), F32),
        ],
        [
            vmem((2, 24, 24, 256), F32),
            vmem((3, 192, TERMS), F32),
            vmem((1, TERMS), F32),
            vmem((256, 768), BF16),
            pltpu.SemaphoreType.DMA((3,)),
            vmem((3 * QUADS, 576, 256), BF16),
            pltpu.SemaphoreType.DMA((3,)),
        ],
        600_000_000,
        factors, term_weight.reshape(1, TERMS), select, sheet,
    )
    direct, mid_tiles, names = call(
        fine_kernel,
        "svvvhw",
        [sds((8, 8, PLANE), F32), sds((28, 8, 128), F32), sds((1, 128), i32)],
        [
            vmem((GONE + 9, 8, 128), F32),
            vmem((QUADS, 256, ROWS_W), BF16),
            vmem((QUADS, 576, 256), BF16),
            pltpu.SemaphoreType.DMA((1,)),
        ],
        100_000_000,
        numbers, before, centre, after, w_tables, x_tables,
    )
    fine_out, mid_out = call(
        last_kernel,
        "ssvvvhwhhh",
        [sds((8, 512), F32), sds((1, 512), F32)],
        [
            vmem((65, 8, 128), F32),
            vmem((8, 8, PLANE), F32),
            vmem((16, 8, 128), F32),
            vmem((512, 128), BF16),
            vmem((128, 1024), BF16),
            pltpu.SemaphoreType.DMA((3,)),
            vmem((2 * QUADS, 576, 256), BF16),
            pltpu.SemaphoreType.DMA((2,)),
        ],
        200_000_000,
        numbers, names, planes, mid_tiles, direct, w_tables, x_tables,
        rows_p, last_filters, mids,
    )
    return fine_out, mid_out


def solution(mesh):
    cells = ("gx", "gy", "gz")
    rows = P(cells, None)
    return jax.shard_map(
        shards,
        mesh=mesh,
        in_specs=(rows, rows, rows, P(cells), P(cells), rows, rows, P(), P(), P()),
        out_specs=(rows, rows),
        check_vma=False,
    )
```

```python
import functools
import math

import jax
import jax.numpy as jnp
import ml_dtypes
import numpy as np
from jax import lax
from jax.experimental import pallas as pl
from jax.experimental.pallas import tpu as pltpu
from jax.sharding import PartitionSpec as P

K = 8
PLANE = 64
TERMS = 32
QUADS = 8
ROWS_W = 640
GONE = 27 * 10
BF16 = jnp.bfloat16
F32 = jnp.float32
VMEM_LIMIT = 32 * 1024 * 1024


def poly_multiply(left, right):
    result = [0.0] * (len(left) + len(right) - 1)
    for first, left_coef in enumerate(left):
        for second, right_coef in enumerate(right):
            result[first + second] += left_coef * right_coef
    return result


def poly_compose(coeffs, factor, offset):
    result = [0.0]
    power_term = [1.0]
    for coef in coeffs:
        padded = result + [0.0] * (len(power_term) - len(result))
        result = [padded[place] + coef * power_term[place] for place in range(len(power_term))]
        power_term = poly_multiply(power_term, [offset, factor])
    return result


def legendre_table(basis_order):
    polys = [[1.0], [0.0, 1.0]]
    for degree in range(1, basis_order):
        upper = [0.0] + [(2 * degree + 1) * coef for coef in polys[degree]]
        lower = [degree * coef for coef in polys[degree - 1]] + [0.0] * (
            len(upper) - len(polys[degree - 1])
        )
        polys.append([(upper[place] - lower[place]) / (degree + 1) for place in range(len(upper))])
    return [
        [math.sqrt(2 * degree + 1) * coef for coef in poly_compose(polys[degree], 2.0, -1.0)]
        for degree in range(basis_order)
    ]


@functools.cache
def two_scale(basis_order):
    shifted = legendre_table(basis_order)
    filters = np.zeros((2, basis_order, basis_order))
    for which_half in range(2):
        for row_at in range(basis_order):
            halved = poly_compose(shifted[row_at], 0.5, 0.5 * which_half)
            for col_at in range(basis_order):
                product = poly_multiply(halved, shifted[col_at])
                total = sum((coef / (place + 1) for place, coef in enumerate(product)))
                filters[which_half, row_at, col_at] = total / math.sqrt(2.0)
    return filters.astype(np.float32).astype(np.float64)


def two_parts(matrix):
    high = matrix.astype(ml_dtypes.bfloat16)
    low = (matrix - high.astype(np.float64)).astype(ml_dtypes.bfloat16)
    return high, low


@functools.cache
def filter_tables():
    h = two_scale(K)
    pair = np.einsum("jqy,lrz->jlqryz", h, h).reshape(4, PLANE, PLANE)
    to_coarse = pair.transpose(0, 2, 1).reshape(4 * PLANE, PLANE)
    comp = np.concatenate(two_parts(to_coarse), axis=1)
    to_fine = pair.transpose(1, 0, 2).reshape(PLANE, 4 * PLANE)
    prol = np.concatenate(two_parts(to_fine), axis=1)
    contrib = np.stack([np.concatenate(two_parts(pair[k].T), axis=1) for k in range(4)])
    single = np.stack([np.concatenate(two_parts(pair[k]), axis=1) for k in range(4)])
    mid = np.zeros((2, PLANE, 4, 2, PLANE))
    for half in range(2):
        mid[half, :, :, half, :] = pair.transpose(1, 0, 2)
    mids = np.concatenate(two_parts(mid.reshape(128, 512)), axis=1)
    rows_c = np.broadcast_to(h.transpose(0, 2, 1).reshape(16, 8)[:, :, None], (16, 8, 128))
    rows_p = np.broadcast_to(h.reshape(16, 8)[:, :, None], (16, 8, 128))
    return dict(
        comp=comp,
        prol=prol,
        contrib=contrib,
        single=single,
        mids=mids,
        rows_c=np.ascontiguousarray(rows_c).astype(np.float32),
        rows_p=np.ascontiguousarray(rows_p).astype(np.float32),
    )


@functools.cache
def select_tables():
    out = np.arange(256) // TERMS
    term = np.arange(256) % TERMS
    col = np.arange(256)
    group = term[:, None] % 4 == (col // PLANE)[None, :]
    left = group & (out[:, None] == (col // 8 % 8)[None, :])
    right = group & (out[:, None] == (col % 8)[None, :])
    turn = (term[None, :] == (col // 8)[:, None]) & (out[None, :] == (col % 8)[:, None])
    return np.concatenate([left, right, turn], axis=1).astype(ml_dtypes.bfloat16)


def split(value):
    high = value.astype(BF16)
    return high, (value - high.astype(F32)).astype(BF16)


def dot(left, right):
    return jnp.dot(left, right, preferred_element_type=F32)


def fine_dot(value, table):
    rows = value.shape[0]
    width = table.shape[1] // 2
    if rows % 16 == 0:
        result = dot(jnp.concatenate(split(value), axis=0), table)
    else:
        high = value.astype(BF16).astype(F32)
        result = dot(jnp.concatenate([high, value - high], axis=0).astype(BF16), table)
    return result[:rows, :width] + result[rows:, :width] + result[:rows, width:]


def low_lanes(shape):
    return lax.broadcasted_iota(jnp.int32, shape, len(shape) - 1) < PLANE


def turned(value):
    return pltpu.roll(value, PLANE, value.ndim - 1)


def row_mix(tables, tile):
    total = None
    for p in range(8):
        term = tables[p] * tile[p : p + 1, :]
        total = term if total is None else total + term
    return total


def two_row_mixes(rows_ref, tile, width):
    return [
        row_mix([rows_ref[i * 8 + p, :, :width] for p in range(8)], tile) for i in range(2)
    ]


def fetches(sems, *pairs):
    copies = [
        pltpu.make_async_copy(there, here, sems.at[at]) for at, (there, here) in enumerate(pairs)
    ]
    for copy in copies:
        copy.start()
    return copies


def local_cell(device, own):
    step_x = (device >> 6) - (own >> 6) + 1
    step_y = ((device >> 3) & 7) - ((own >> 3) & 7) + 1
    step_z = (device & 7) - (own & 7) + 1
    return step_x * 9 + step_y * 3 + step_z


def tables_kernel(
    factors_h, weights_h, select_h, sheet,
    ab_ref, x_ref, tiles,
    factors, weights, select, sems,
):
    copies = fetches(sems, (factors_h, factors), (weights_h, weights), (select_h, select))
    for cell in range(9):
        spread_cell(sheet, cell, tiles, cell)
    for copy in copies:
        copy.wait()
    lane = lax.broadcasted_iota(jnp.int32, (24, 256), 1)
    quad_of = (lane & 31) >> 2
    weight = jnp.concatenate([weights[...]] * 8, axis=1)
    weighted, plain = [], []
    for level in range(3):
        rows = []
        for e in range(3):
            rows.append(
                jnp.concatenate(
                    [factors[level, e * 64 + b * 8 : e * 64 + b * 8 + 8, :] for b in range(8)],
                    axis=1,
                )
            )
        values = jnp.concatenate(rows, axis=0)
        scaled = values * weight
        for quad in range(QUADS):
            weighted.append(jnp.where(quad_of == quad, scaled, 0.0))
            plain.append(jnp.where(quad_of == quad, values, 0.0))
        x_ref[level] = lax.dot_general(
            select[:, 512:768],
            values.astype(BF16),
            (((1,), (1,)), ((), ())),
            preferred_element_type=F32,
        ).astype(BF16)
    for which, parts in enumerate((weighted, plain)):
        both = dot(
            jnp.concatenate(split(jnp.concatenate(parts, axis=0)), axis=0),
            select[:, which * 256 : which * 256 + 256],
        )
        ab_ref[which] = (both[:576] + both[576:]).reshape(24, 24, 256)


def build_w(ab_ref, level, w_ref):
    def one_quad(quad, carry):
        at = level * QUADS + quad
        inner = [ab_ref[1, at, ez * 8 : ez * 8 + 8, :] for ez in range(3)]
        for ey in range(3):
            for pair in range(4):
                row = ey * 8 + 2 * pair
                first = ab_ref[0, at, row : row + 1, :]
                second = ab_ref[0, at, row + 1 : row + 2, :]
                for ez in range(3):
                    tile = jnp.concatenate([first * inner[ez], second * inner[ez]], axis=0)
                    to = (ey * 3 + ez) * PLANE + pair * 16
                    w_ref[quad, to : to + 16, :] = tile.astype(BF16)
        return carry

    lax.fori_loop(0, QUADS, one_quad, 0)


def spread_cell(sheet, cell, tiles, to):
    low = low_lanes((8, 128))
    base = cell * 48
    for group in range(2):
        both = sheet[base + group * 16 : base + group * 16 + 16, :].astype(F32)
        for sub in range(2):
            tile = both[sub * 8 : sub * 8 + 8, :]
            other = turned(tile)
            tiles[to * 10 + group * 4 + sub * 2] = jnp.where(low, tile, other)
            tiles[to * 10 + group * 4 + sub * 2 + 1] = jnp.where(low, other, tile)
    last = sheet[base + 32 : base + 48, :].astype(F32)
    tiles[to * 10 + 8] = last[0:8, :]
    tiles[to * 10 + 9] = last[8:16, :]


def diagonal_sum(result, rows):
    total = None
    for term in range(4):
        piece = result[term * rows : (term + 1) * rows, term * PLANE : (term + 1) * PLANE]
        total = piece if total is None else total + piece
    return total


def apply_one(sources, x_table, w_ref):
    mixed = dot(x_table, sources).astype(BF16)
    result = None
    for quad in range(QUADS):
        part = dot(mixed[quad * 32 : quad * 32 + 32, :576], w_ref[quad])
        result = part if result is None else result + part
    return diagonal_sum(result, 8)


def first_kernel(
    parent, refined, child_h, fine_h, mid_h, coarse_h, coef_h, leaf_h, filters_h, rows_h,
    halo, payload, numbers,
    child, child_v, fine_nbr, mid_nbr, coarse_nbr, coef, leaf, filters, rows,
    source, detail, sems,
):
    copies = fetches(
        sems,
        (coef_h, coef),
        (filters_h, filters),
        (rows_h, rows),
        (child_h, child),
        (leaf_h, leaf),
        (child_h, child_v),
        (fine_h, fine_nbr),
        (mid_h, mid_nbr),
        (coarse_h, coarse_nbr),
    )
    for copy in copies:
        copy.wait()
    comp = filters[0:256, :]
    prol = jnp.concatenate([filters[256 + 64 * k : 320 + 64 * k, :] for k in range(4)], axis=1)
    slot = parent[0] >> 3
    octant = parent[0] & 7
    near = fine_nbr[...]
    own = near[:, 13:14] >> 3
    cell = local_cell(near >> 3, own) * 10 + (near & 7)
    numbers[0:8, 0:27] = jnp.where(near >= 0, cell, GONE)
    near_mid = mid_nbr[...]
    own_mid = near_mid[:, 13:14]
    numbers[8:9, 0:27] = jnp.where(near_mid >= 0, local_cell(near_mid, own_mid), 27)
    numbers[8:9, 27:28] = jnp.full((1, 1), 27, jnp.int32)
    hot = jnp.where(lax.broadcasted_iota(jnp.int32, (8, 64), 1) == slot, 1.0, 0.0).astype(BF16)
    near_coarse = lax.dot_general(
        hot,
        coarse_nbr[...].astype(F32).astype(BF16),
        (((1,), (1,)), ((), ())),
        preferred_element_type=F32,
    )[0:1].astype(jnp.int32)
    numbers[9:10, 0:27] = jnp.where(near_coarse >= 0, near_coarse, 64)
    numbers[9:10, 27:28] = jnp.full((1, 1), 64, jnp.int32)
    numbers[10:11, 0:8] = child_v[...]
    numbers[10:11, 8:9] = jnp.full((1, 1), parent[0], jnp.int32)
    numbers[10:11, 9:10] = jnp.full((1, 1), refined[0], jnp.int32)

    values = coef[...].astype(F32)
    for a in range(8):
        source[:, a, :] = values[:, a * PLANE : (a + 1) * PLANE]
    tiles = [source[child[0, o]] for o in range(8)]
    lhs = jnp.concatenate(
        [jnp.concatenate(tiles[0:4], axis=1), jnp.concatenate(tiles[4:8], axis=1)], axis=0
    ).astype(BF16)
    both = dot(lhs, comp)
    partial = both[:, :PLANE] + both[:, PLANE:]
    compressed = None
    for k in range(16):
        term = rows[k, :, :PLANE] * partial[k : k + 1, :]
        compressed = term if compressed is None else compressed + term
    leaf_row = leaf[...].astype(F32)
    leaf_tile = jnp.concatenate(
        [leaf_row[:, a * PLANE : (a + 1) * PLANE] for a in range(8)], axis=0
    )
    middle = jnp.where(refined[0] > 0, compressed, leaf_tile).astype(BF16).astype(F32)

    row_at = (octant >> 2) * 8
    inner = row_mix([rows[row_at + x, :, :PLANE] for x in range(8)], middle)
    table = filters[pl.ds(pl.multiple_of(512 + (octant & 3) * 64, 64), 64), :]
    added = fine_dot(inner, table)
    low8 = low_lanes((8, 128))
    tag = jnp.full((8, 128), slot, jnp.int32).astype(F32)
    tile = jnp.where(low8, jnp.concatenate([added, added], axis=1), tag).astype(BF16)
    payload[...] = jnp.broadcast_to(tile[None], payload.shape)

    live = jnp.full((8, PLANE), refined[0], jnp.int32).astype(F32)
    upper = jnp.concatenate(two_row_mixes(rows.at[16:32], middle, PLANE), axis=0)
    spread = fine_dot(upper, prol)
    for o in range(8):
        i, jl = o // 4, o % 4
        part = spread[i * 8 : i * 8 + 8, jl * PLANE : (jl + 1) * PLANE]
        detail[child[0, o]] = live * (tiles[o] - part)
    for group in range(2):
        base = group * 4
        halo[group * 16 : group * 16 + 16, :] = jnp.concatenate(
            [
                jnp.concatenate([detail[base], detail[base + 1]], axis=1),
                jnp.concatenate([detail[base + 2], detail[base + 3]], axis=1),
            ],
            axis=0,
        ).astype(BF16)
    meta = jnp.where(low8, tag, jnp.full((8, 128), octant, jnp.int32).astype(F32))
    halo[32:48, :] = jnp.concatenate(
        [jnp.concatenate([middle, middle], axis=1), meta], axis=0
    ).astype(BF16)


def plane_kernel(arrived, copies):
    rows = arrived[...].astype(F32).reshape(512, 128)
    other = turned(rows)
    low = low_lanes((512, 128))
    value = jnp.where(low, rows, other)
    tag = jnp.where(low, other, rows)
    half = jnp.where(low, 0, 1)
    rhs = jnp.where((tag.astype(jnp.int32) & 1) == half, value, 0.0).astype(BF16)
    pick = jnp.where(lax.broadcasted_iota(jnp.int32, (8, 128), 1) == 0, 1.0, 0.0).astype(BF16)
    along = lax.dot_general(
        pick, tag.astype(BF16), (((1,), (1,)), ((), ())), preferred_element_type=F32
    ).astype(jnp.int32)
    p_of = lax.broadcasted_iota(jnp.int32, (8, 512), 1) & 7
    key = jnp.where(p_of == lax.broadcasted_iota(jnp.int32, (8, 512), 0), along >> 1, -1)
    hot = jnp.concatenate(
        [jnp.where(key == c2, 1.0, 0.0) for c2 in range(32)], axis=0
    ).astype(BF16)
    partial = dot(hot, rhs).astype(BF16)
    copies[...] = jnp.broadcast_to(partial[None], copies.shape)


def pair_of(first, second):
    return jnp.where(low_lanes((8, 128)), first, second)


def fine_kernel(
    numbers, left, centre, right, ab_ref, x_ref,
    direct, mid_tiles, names_ref,
    table, mixed, w_ref,
):
    build_w(ab_ref, 0, w_ref)
    lanes = lax.broadcasted_iota(jnp.int32, (1, 128), 1)
    low8 = low_lanes((8, 128))
    table[GONE] = jnp.zeros((8, 128), F32)
    table[GONE + 8] = jnp.zeros((8, 128), F32)
    for cell in range(9):
        spread_cell(left, cell, table, cell)
        spread_cell(right, cell, table, 18 + cell)
    for at in range(90):
        table[90 + at] = centre[at]
    names = jnp.full((1, 128), 512, jnp.int32)
    for cell in range(27):
        meta = table[cell * 10 + 9, 0:1, :]
        other = turned(meta)
        name = jnp.where(low8[0:1], meta * 8.0 + other, other * 8.0 + meta).astype(jnp.int32)
        names = jnp.where(lanes == cell, name, names)
    names_ref[...] = names
    for cell in range(28):
        mid_tiles[cell] = table[cell * 10 + 8]

    def source(t, ex, e):
        if e > 8:
            return table[GONE]
        return table[numbers[t, ex * 9 + e]]

    for pair in range(4):
        pieces = []
        for t in (2 * pair, 2 * pair + 1):
            for ep in range(5):
                pieces.append(
                    jnp.concatenate(
                        [
                            pair_of(source(t, ex, 2 * ep), source(t, ex, 2 * ep + 1))
                            for ex in range(3)
                        ],
                        axis=0,
                    ).astype(BF16)
                )
        product = dot(x_ref[0], jnp.concatenate(pieces, axis=1))
        for n in range(TERMS):
            quad, term = n // 4, n % 4
            tile = jnp.concatenate(
                [product[n * 8 : n * 8 + 8, :640], product[n * 8 : n * 8 + 8, 640:]], axis=0
            )
            row = term * PLANE + pair * 16
            mixed[quad, row : row + 16, :] = tile.astype(BF16)
    result = None
    for quad in range(QUADS):
        part = dot(mixed[quad, :, :576], w_ref[quad])
        result = part if result is None else result + part
    direct[...] = diagonal_sum(result, PLANE).reshape(8, 8, PLANE)


def last_kernel(
    numbers, names, planes, mid_tiles, direct, ab_ref, x_ref, rows_h, filters_h, mids_h,
    fine_out, mid_out,
    coarse, back, rows_p, filters, mids, sems, w_mid, w_coarse,
):
    copies = fetches(sems, (rows_h, rows_p), (filters_h, filters), (mids_h, mids))
    build_w(ab_ref, 1, w_mid)
    build_w(ab_ref, 2, w_coarse)
    low8 = low_lanes((8, 128))

    total = None
    for plane in range(8):
        term = planes[plane].astype(F32)
        total = term if total is None else total + term
    for c2 in range(32):
        tile = total[c2 * 8 : c2 * 8 + 8, :]
        other = turned(tile)
        coarse[2 * c2] = jnp.where(low8, tile, other)
        coarse[2 * c2 + 1] = jnp.where(low8, other, tile)
    coarse[64] = jnp.zeros((8, 128), F32)
    octant = numbers[10, 8] & 7

    def coarse_source(ex, e):
        return coarse[numbers[9, ex * 9 + e if e < 9 else 27]]

    sources = jnp.concatenate(
        [
            jnp.concatenate(
                [
                    pair_of(coarse_source(ex, 2 * ep), coarse_source(ex, 2 * ep + 1))
                    for ex in range(3)
                ],
                axis=0,
            ).astype(BF16)
            for ep in range(5)
        ],
        axis=1,
    )
    coarse_result = apply_one(sources, x_ref[2], w_coarse)

    for copy in copies:
        copy.wait()
    uppers, octants, owns = [], [], []
    for ep in range(5):
        for ex in range(3):
            first = numbers[8, ex * 9 + 2 * ep]
            second = numbers[8, ex * 9 + 2 * ep + 1 if ep < 4 else 27]
            name_1, name_2 = names[0, first], names[0, second]
            owns.append(pair_of(mid_tiles[first], mid_tiles[second]))
            both = pair_of(coarse[name_1 >> 3], coarse[name_2 >> 3])
            named = jnp.where(low8, name_1 & 7, name_2 & 7)
            octants.append(named)
            mix_0, mix_1 = two_row_mixes(rows_p, both, 128)
            uppers.append(jnp.where(named >= 4, mix_1, mix_0))
    stacked = jnp.concatenate(uppers, axis=0)
    high = stacked.astype(BF16).astype(F32)
    spread = dot(jnp.concatenate([high, stacked - high], axis=0).astype(BF16), mids[...])
    spread = spread[:120, :512] + spread[120:, :512] + spread[:120, 512:]
    pieces = []
    for ep in range(5):
        tiles = []
        for ex in range(3):
            at = ep * 3 + ex
            which = octants[at] & 3
            chosen = spread[at * 8 : at * 8 + 8, 0:128]
            for jl in range(1, 4):
                chosen = jnp.where(
                    which == jl, spread[at * 8 : at * 8 + 8, jl * 128 : jl * 128 + 128], chosen
                )
            tiles.append(owns[at] - chosen)
        pieces.append(jnp.concatenate(tiles, axis=0).astype(BF16))
    mid_result = apply_one(jnp.concatenate(pieces, axis=1), x_ref[1], w_mid)

    row_at = (octant >> 2) * 8
    upper = row_mix([rows_p[row_at + p, :, :PLANE] for p in range(8)], coarse_result)
    single = filters[pl.ds(pl.multiple_of(256 + (octant & 3) * 64, 64), 64), :]
    middle = mid_result + fine_dot(upper, single)
    for a in range(8):
        mid_out[:, a * PLANE : (a + 1) * PLANE] = middle[a : a + 1, :]
    live = jnp.full((8, PLANE), numbers[10, 9], jnp.int32).astype(F32)
    upper = jnp.concatenate(two_row_mixes(rows_p, middle, PLANE), axis=0)
    prol = jnp.concatenate([filters[64 * k : 64 * k + 64, :] for k in range(4)], axis=1)
    spread = fine_dot(upper, prol)
    for o in range(8):
        i, jl = o // 4, o % 4
        slot = numbers[10, o]
        part = spread[i * 8 : i * 8 + 8, jl * PLANE : (jl + 1) * PLANE]
        back[slot] = live * (direct[slot] + part)
    for a in range(8):
        fine_out[:, a * PLANE : (a + 1) * PLANE] = back[:, a, :]


def call(kernel, kinds, outs, scratch, flops, *args):
    any_space = pl.BlockSpec(memory_space=pl.ANY)
    vmem = pl.BlockSpec(memory_space=pltpu.VMEM)
    specs = dict(s=pl.BlockSpec(memory_space=pltpu.SMEM), v=vmem, w=vmem, h=any_space)
    moved = sum(math.prod(x.shape) * x.dtype.itemsize for x in (*args, *outs))
    spaces = dict(w=pltpu.VMEM, h=pltpu.HBM)
    args = [
        pltpu.with_memory_space_constraint(x, spaces[kind]) if kind in spaces else x
        for kind, x in zip(kinds, args, strict=True)
    ]
    return pl.pallas_call(
        kernel,
        out_shape=outs,
        in_specs=[specs[kind] for kind in kinds],
        out_specs=[any_space if getattr(x, "memory_space", None) == pltpu.HBM else vmem for x in outs],
        scratch_shapes=scratch,
        compiler_params=pltpu.CompilerParams(vmem_limit_bytes=VMEM_LIMIT),
        cost_estimate=pl.CostEstimate(flops=flops, bytes_accessed=moved, transcendentals=0),
        name=kernel.__name__,
    )(*args)


def both_ways(x, axis):
    count = lax.axis_size(axis)
    ends = count - 1
    before = lax.ppermute(x, axis, [(i, i + 1) for i in range(ends)])
    after = lax.ppermute(x, axis, [(i + 1, i) for i in range(ends)])
    return before, after


def shards(
    fine_coef, mid_leaf, mid_child, mid_parent, mid_refined,
    fine_nbr, mid_nbr, coarse_nbr, op_factor, term_weight,
):
    tables = filter_tables()
    select = jnp.asarray(select_tables())
    prol_rows = np.concatenate(np.split(tables["prol"], 4, axis=1), axis=0)
    single_rows = tables["single"].reshape(256, 128)
    first_filters = jnp.asarray(
        np.concatenate([tables["comp"], prol_rows, tables["contrib"].reshape(256, 128)])
    )
    last_filters = jnp.asarray(np.concatenate([prol_rows, single_rows]))
    rows_both = jnp.asarray(np.concatenate([tables["rows_c"], tables["rows_p"]]))
    rows_p = jnp.asarray(tables["rows_p"])
    mids = jnp.asarray(tables["mids"])
    factors = op_factor.transpose(0, 2, 3, 4, 1).reshape(3, 192, TERMS)

    sds = jax.ShapeDtypeStruct
    vmem, smem = pltpu.VMEM, pltpu.SMEM
    i32 = jnp.int32
    halo, payload, numbers = call(
        first_kernel,
        "sshhhhhhhh",
        [sds((48, 128), BF16), sds((64, 8, 128), BF16), sds((16, 128), i32)],
        [
            smem((1, 8), i32),
            vmem((1, 8), i32),
            vmem((8, 27), i32),
            vmem((1, 27), i32),
            vmem((27, 64), i32),
            vmem((8, 512), BF16),
            vmem((1, 512), BF16),
            vmem((768, 128), BF16),
            vmem((32, 8, 128), F32),
            vmem((8, 8, PLANE), F32),
            vmem((8, 8, PLANE), F32),
            pltpu.SemaphoreType.DMA((9,)),
        ],
        2_000_000,
        mid_parent, mid_refined, mid_child, fine_nbr, mid_nbr, coarse_nbr.T, fine_coef, mid_leaf,
        first_filters, rows_both,
    )
    arrived = lax.all_to_all(payload, ("gy", "gz"), 0, 0, tiled=True)
    before, after = both_ways(halo, "gz")
    line = jnp.concatenate([before, halo, after], axis=0)
    before, after = both_ways(line, "gy")
    sheet = jnp.concatenate([before, line, after], axis=0)
    before, after = both_ways(sheet, "gx")

    (copies,) = call(
        plane_kernel, "v", [sds((8, 256, 128), BF16)], [], 33_000_000, arrived
    )
    planes = lax.all_to_all(copies, "gx", 0, 0, tiled=True)

    w_factors, x_tables, centre = call(
        tables_kernel,
        "hhhv",
        [
            pltpu.VMEM((2, 3 * QUADS, 24, 256), F32),
            pltpu.VMEM((3, 256, 24), BF16),
            pltpu.VMEM((90, 8, 128), F32),
        ],
        [
            vmem((3, 192, TERMS), F32),
            vmem((1, TERMS), F32),
            vmem((256, 768), BF16),
            pltpu.SemaphoreType.DMA((3,)),
        ],
        600_000_000,
        factors, term_weight.reshape(1, TERMS), select, sheet,
    )
    direct, mid_tiles, names = call(
        fine_kernel,
        "svvvww",
        [sds((8, 8, PLANE), F32), sds((28, 8, 128), F32), sds((1, 128), i32)],
        [
            vmem((GONE + 9, 8, 128), F32),
            vmem((QUADS, 256, ROWS_W), BF16),
            vmem((QUADS, 576, 256), BF16),
        ],
        100_000_000,
        numbers, before, centre, after, w_factors, x_tables,
    )
    fine_out, mid_out = call(
        last_kernel,
        "ssvvvwwhhh",
        [sds((8, 512), F32), sds((1, 512), F32)],
        [
            vmem((65, 8, 128), F32),
            vmem((8, 8, PLANE), F32),
            vmem((16, 8, 128), F32),
            vmem((512, 128), BF16),
            vmem((128, 1024), BF16),
            pltpu.SemaphoreType.DMA((3,)),
            vmem((QUADS, 576, 256), BF16),
            vmem((QUADS, 576, 256), BF16),
        ],
        200_000_000,
        numbers, names, planes, mid_tiles, direct, w_factors, x_tables,
        rows_p, last_filters, mids,
    )
    return fine_out, mid_out


def solution(mesh):
    cells = ("gx", "gy", "gz")
    rows = P(cells, None)
    return jax.shard_map(
        shards,
        mesh=mesh,
        in_specs=(rows, rows, rows, P(cells), P(cells), rows, rows, P(), P(), P()),
        out_specs=(rows, rows),
        check_vma=False,
    )
```

```python
import functools
import math

import jax
import jax.numpy as jnp
import ml_dtypes
import numpy as np
from jax import lax
from jax.experimental import pallas as pl
from jax.experimental.pallas import tpu as pltpu
from jax.sharding import PartitionSpec as P

K = 8
PLANE = 64
TERMS = 32
QUADS = 8
ROWS_W = 4608
GONE = 27 * 10
BF16 = jnp.bfloat16
F32 = jnp.float32
VMEM_LIMIT = 32 * 1024 * 1024


def poly_multiply(left, right):
    result = [0.0] * (len(left) + len(right) - 1)
    for first, left_coef in enumerate(left):
        for second, right_coef in enumerate(right):
            result[first + second] += left_coef * right_coef
    return result


def poly_compose(coeffs, factor, offset):
    result = [0.0]
    power_term = [1.0]
    for coef in coeffs:
        padded = result + [0.0] * (len(power_term) - len(result))
        result = [padded[place] + coef * power_term[place] for place in range(len(power_term))]
        power_term = poly_multiply(power_term, [offset, factor])
    return result


def legendre_table(basis_order):
    polys = [[1.0], [0.0, 1.0]]
    for degree in range(1, basis_order):
        upper = [0.0] + [(2 * degree + 1) * coef for coef in polys[degree]]
        lower = [degree * coef for coef in polys[degree - 1]] + [0.0] * (
            len(upper) - len(polys[degree - 1])
        )
        polys.append([(upper[place] - lower[place]) / (degree + 1) for place in range(len(upper))])
    return [
        [math.sqrt(2 * degree + 1) * coef for coef in poly_compose(polys[degree], 2.0, -1.0)]
        for degree in range(basis_order)
    ]


@functools.cache
def two_scale(basis_order):
    shifted = legendre_table(basis_order)
    filters = np.zeros((2, basis_order, basis_order))
    for which_half in range(2):
        for row_at in range(basis_order):
            halved = poly_compose(shifted[row_at], 0.5, 0.5 * which_half)
            for col_at in range(basis_order):
                product = poly_multiply(halved, shifted[col_at])
                total = sum((coef / (place + 1) for place, coef in enumerate(product)))
                filters[which_half, row_at, col_at] = total / math.sqrt(2.0)
    return filters.astype(np.float32).astype(np.float64)


def two_parts(matrix):
    high = matrix.astype(ml_dtypes.bfloat16)
    low = (matrix - high.astype(np.float64)).astype(ml_dtypes.bfloat16)
    return high, low


@functools.cache
def filter_tables():
    h = two_scale(K)
    pair = np.einsum("jqy,lrz->jlqryz", h, h).reshape(4, PLANE, PLANE)
    to_coarse = pair.transpose(0, 2, 1).reshape(4 * PLANE, PLANE)
    comp = np.concatenate(two_parts(to_coarse), axis=1)
    to_fine = pair.transpose(1, 0, 2).reshape(PLANE, 4 * PLANE)
    prol = np.concatenate(two_parts(to_fine), axis=1)
    contrib = np.stack([np.concatenate(two_parts(pair[k].T), axis=1) for k in range(4)])
    single = np.stack([np.concatenate(two_parts(pair[k]), axis=1) for k in range(4)])
    mid = np.zeros((2, PLANE, 4, 2, PLANE))
    for half in range(2):
        mid[half, :, :, half, :] = pair.transpose(1, 0, 2)
    mids = np.concatenate(two_parts(mid.reshape(128, 512)), axis=1)
    rows_c = np.broadcast_to(h.transpose(0, 2, 1).reshape(16, 8)[:, :, None], (16, 8, 128))
    rows_p = np.broadcast_to(h.reshape(16, 8)[:, :, None], (16, 8, 128))
    return dict(
        comp=comp,
        prol=prol,
        contrib=contrib,
        single=single,
        mids=mids,
        rows_c=np.ascontiguousarray(rows_c).astype(np.float32),
        rows_p=np.ascontiguousarray(rows_p).astype(np.float32),
    )


@functools.cache
def select_tables():
    out = np.arange(256) // TERMS
    term = np.arange(256) % TERMS
    col = np.arange(256)
    group = term[:, None] % 4 == (col // PLANE)[None, :]
    left = group & (out[:, None] == (col // 8 % 8)[None, :])
    right = group & (out[:, None] == (col % 8)[None, :])
    turn = (term[None, :] == (col // 8)[:, None]) & (out[None, :] == (col % 8)[:, None])
    return np.concatenate([left, right, turn], axis=1).astype(ml_dtypes.bfloat16)


def split(value):
    high = value.astype(BF16)
    return high, (value - high.astype(F32)).astype(BF16)


def dot(left, right):
    return jnp.dot(left, right, preferred_element_type=F32)


def fine_dot(value, table):
    rows = value.shape[0]
    width = table.shape[1] // 2
    if rows % 16 == 0:
        result = dot(jnp.concatenate(split(value), axis=0), table)
    else:
        high = value.astype(BF16).astype(F32)
        result = dot(jnp.concatenate([high, value - high], axis=0).astype(BF16), table)
    return result[:rows, :width] + result[rows:, :width] + result[:rows, width:]


def low_lanes(shape):
    return lax.broadcasted_iota(jnp.int32, shape, len(shape) - 1) < PLANE


def turned(value):
    return pltpu.roll(value, PLANE, value.ndim - 1)


def row_mix(tables, tile):
    total = None
    for p in range(8):
        term = tables[p] * tile[p : p + 1, :]
        total = term if total is None else total + term
    return total


def two_row_mixes(rows_ref, tile, width):
    return [
        row_mix([rows_ref[i * 8 + p, :, :width] for p in range(8)], tile) for i in range(2)
    ]


def fetches(sems, *pairs):
    copies = [
        pltpu.make_async_copy(there, here, sems.at[at]) for at, (there, here) in enumerate(pairs)
    ]
    for copy in copies:
        copy.start()
    return copies


def local_cell(device, own):
    step_x = (device >> 6) - (own >> 6) + 1
    step_y = ((device >> 3) & 7) - ((own >> 3) & 7) + 1
    step_z = (device & 7) - (own & 7) + 1
    return step_x * 9 + step_y * 3 + step_z


def tables_kernel(
    factors_h, weights_h, select_h, sheet,
    ab_ref, x_ref, tiles,
    factors, weights, select, sems,
):
    copies = fetches(sems, (factors_h, factors), (weights_h, weights), (select_h, select))
    for cell in range(9):
        spread_cell(sheet, cell, tiles, cell)
    for copy in copies:
        copy.wait()
    lane = lax.broadcasted_iota(jnp.int32, (24, 256), 1)
    quad_of = (lane & 31) >> 2
    weight = jnp.concatenate([weights[...]] * 8, axis=1)
    weighted, plain = [], []
    for level in range(3):
        rows = []
        for e in range(3):
            rows.append(
                jnp.concatenate(
                    [factors[level, e * 64 + b * 8 : e * 64 + b * 8 + 8, :] for b in range(8)],
                    axis=1,
                )
            )
        values = jnp.concatenate(rows, axis=0)
        scaled = values * weight
        for quad in range(QUADS):
            weighted.append(jnp.where(quad_of == quad, scaled, 0.0))
            plain.append(jnp.where(quad_of == quad, values, 0.0))
        x_ref[level] = lax.dot_general(
            select[:, 512:768],
            values.astype(BF16),
            (((1,), (1,)), ((), ())),
            preferred_element_type=F32,
        ).astype(BF16)
    for which, parts in enumerate((weighted, plain)):
        both = dot(
            jnp.concatenate(split(jnp.concatenate(parts, axis=0)), axis=0),
            select[:, which * 256 : which * 256 + 256],
        )
        ab_ref[which] = (both[:576] + both[576:]).reshape(24, 24, 256)


def build_w(ab_ref, level, w_ref):
    def one_quad(quad, carry):
        at = level * QUADS + quad
        inner = [ab_ref[1, at, ez * 8 : ez * 8 + 8, :] for ez in range(3)]
        for ey in range(3):
            for pair in range(4):
                row = ey * 8 + 2 * pair
                first = ab_ref[0, at, row : row + 1, :]
                second = ab_ref[0, at, row + 1 : row + 2, :]
                for ez in range(3):
                    tile = jnp.concatenate([first * inner[ez], second * inner[ez]], axis=0)
                    e = ey * 3 + ez
                    to = quad * 512 + e * PLANE if e < 8 else 4096 + quad * PLANE
                    to = pl.multiple_of(to + pair * 16, 16)
                    w_ref[pl.ds(to, 16), :] = tile.astype(BF16)
        return carry

    lax.fori_loop(0, QUADS, one_quad, 0)


def spread_cell(sheet, cell, tiles, to):
    low = low_lanes((8, 128))
    base = cell * 48
    for group in range(2):
        both = sheet[base + group * 16 : base + group * 16 + 16, :].astype(F32)
        for sub in range(2):
            tile = both[sub * 8 : sub * 8 + 8, :]
            other = turned(tile)
            tiles[to * 10 + group * 4 + sub * 2] = jnp.where(low, tile, other)
            tiles[to * 10 + group * 4 + sub * 2 + 1] = jnp.where(low, other, tile)
    last = sheet[base + 32 : base + 48, :].astype(F32)
    tiles[to * 10 + 8] = last[0:8, :]
    tiles[to * 10 + 9] = last[8:16, :]


def diagonal_sum(result, rows):
    total = None
    for term in range(4):
        piece = result[term * rows : (term + 1) * rows, term * PLANE : (term + 1) * PLANE]
        total = piece if total is None else total + piece
    return total


def apply_one(sources, x_table, w_ref):
    product = dot(x_table, sources)
    low = low_lanes((32, 128))
    groups = [product[quad * 32 : quad * 32 + 32, :] for quad in range(QUADS)]
    pieces = [group[:, :512].astype(BF16) for group in groups]
    for quad in range(0, QUADS, 2):
        both = jnp.where(low, groups[quad][:, 512:], groups[quad + 1][:, 512:])
        pieces.append(both.astype(BF16))
    result = dot(jnp.concatenate(pieces, axis=1), w_ref[...])
    return diagonal_sum(result, 8)


def first_kernel(
    parent, refined, child_h, fine_h, mid_h, coarse_h, coef_h, leaf_h, filters_h, rows_h,
    halo, payload, numbers,
    child, child_v, fine_nbr, mid_nbr, coarse_nbr, coef, leaf, filters, rows,
    source, detail, sems,
):
    copies = fetches(
        sems,
        (coef_h, coef),
        (filters_h, filters),
        (rows_h, rows),
        (child_h, child),
        (leaf_h, leaf),
        (child_h, child_v),
        (fine_h, fine_nbr),
        (mid_h, mid_nbr),
        (coarse_h, coarse_nbr),
    )
    for copy in copies:
        copy.wait()
    comp = filters[0:256, :]
    prol = jnp.concatenate([filters[256 + 64 * k : 320 + 64 * k, :] for k in range(4)], axis=1)
    slot = parent[0] >> 3
    octant = parent[0] & 7
    near = fine_nbr[...]
    own = near[:, 13:14] >> 3
    cell = local_cell(near >> 3, own) * 10 + (near & 7)
    numbers[0:8, 0:27] = jnp.where(near >= 0, cell, GONE)
    near_mid = mid_nbr[...]
    own_mid = near_mid[:, 13:14]
    numbers[8:9, 0:27] = jnp.where(near_mid >= 0, local_cell(near_mid, own_mid), 27)
    numbers[8:9, 27:28] = jnp.full((1, 1), 27, jnp.int32)
    hot = jnp.where(lax.broadcasted_iota(jnp.int32, (8, 64), 1) == slot, 1.0, 0.0).astype(BF16)
    near_coarse = lax.dot_general(
        hot,
        coarse_nbr[...].astype(F32).astype(BF16),
        (((1,), (1,)), ((), ())),
        preferred_element_type=F32,
    )[0:1].astype(jnp.int32)
    numbers[9:10, 0:27] = jnp.where(near_coarse >= 0, near_coarse, 64)
    numbers[9:10, 27:28] = jnp.full((1, 1), 64, jnp.int32)
    numbers[10:11, 0:8] = child_v[...]
    numbers[10:11, 8:9] = jnp.full((1, 1), parent[0], jnp.int32)
    numbers[10:11, 9:10] = jnp.full((1, 1), refined[0], jnp.int32)

    values = coef[...].astype(F32)
    for a in range(8):
        source[:, a, :] = values[:, a * PLANE : (a + 1) * PLANE]
    tiles = [source[child[0, o]] for o in range(8)]
    lhs = jnp.concatenate(
        [jnp.concatenate(tiles[0:4], axis=1), jnp.concatenate(tiles[4:8], axis=1)], axis=0
    ).astype(BF16)
    both = dot(lhs, comp)
    partial = both[:, :PLANE] + both[:, PLANE:]
    compressed = None
    for k in range(16):
        term = rows[k, :, :PLANE] * partial[k : k + 1, :]
        compressed = term if compressed is None else compressed + term
    leaf_row = leaf[...].astype(F32)
    leaf_tile = jnp.concatenate(
        [leaf_row[:, a * PLANE : (a + 1) * PLANE] for a in range(8)], axis=0
    )
    middle = jnp.where(refined[0] > 0, compressed, leaf_tile).astype(BF16).astype(F32)

    row_at = (octant >> 2) * 8
    inner = row_mix([rows[row_at + x, :, :PLANE] for x in range(8)], middle)
    table = filters[pl.ds(pl.multiple_of(512 + (octant & 3) * 64, 64), 64), :]
    added = fine_dot(inner, table)
    low8 = low_lanes((8, 128))
    tag = jnp.full((8, 128), slot, jnp.int32).astype(F32)
    tile = jnp.where(low8, jnp.concatenate([added, added], axis=1), tag).astype(BF16)
    payload[...] = jnp.broadcast_to(tile[None], payload.shape)

    live = jnp.full((8, PLANE), refined[0], jnp.int32).astype(F32)
    upper = jnp.concatenate(two_row_mixes(rows.at[16:32], middle, PLANE), axis=0)
    spread = fine_dot(upper, prol)
    for o in range(8):
        i, jl = o // 4, o % 4
        part = spread[i * 8 : i * 8 + 8, jl * PLANE : (jl + 1) * PLANE]
        detail[child[0, o]] = live * (tiles[o] - part)
    for group in range(2):
        base = group * 4
        halo[group * 16 : group * 16 + 16, :] = jnp.concatenate(
            [
                jnp.concatenate([detail[base], detail[base + 1]], axis=1),
                jnp.concatenate([detail[base + 2], detail[base + 3]], axis=1),
            ],
            axis=0,
        ).astype(BF16)
    meta = jnp.where(low8, tag, jnp.full((8, 128), octant, jnp.int32).astype(F32))
    halo[32:48, :] = jnp.concatenate(
        [jnp.concatenate([middle, middle], axis=1), meta], axis=0
    ).astype(BF16)


def plane_kernel(arrived, copies):
    rows = arrived[...].astype(F32).reshape(512, 128)
    other = turned(rows)
    low = low_lanes((512, 128))
    value = jnp.where(low, rows, other)
    tag = jnp.where(low, other, rows)
    half = jnp.where(low, 0, 1)
    rhs = jnp.where((tag.astype(jnp.int32) & 1) == half, value, 0.0).astype(BF16)
    pick = jnp.where(lax.broadcasted_iota(jnp.int32, (8, 128), 1) == 0, 1.0, 0.0).astype(BF16)
    along = lax.dot_general(
        pick, tag.astype(BF16), (((1,), (1,)), ((), ())), preferred_element_type=F32
    ).astype(jnp.int32)
    p_of = lax.broadcasted_iota(jnp.int32, (8, 512), 1) & 7
    key = jnp.where(p_of == lax.broadcasted_iota(jnp.int32, (8, 512), 0), along >> 1, -1)
    hot = jnp.concatenate(
        [jnp.where(key == c2, 1.0, 0.0) for c2 in range(32)], axis=0
    ).astype(BF16)
    partial = dot(hot, rhs).astype(BF16)
    copies[...] = jnp.broadcast_to(partial[None], copies.shape)


def pair_of(first, second):
    return jnp.where(low_lanes((8, 128)), first, second)


def fine_kernel(
    numbers, left, centre, right, ab_ref, x_ref,
    direct, mid_tiles, names_ref,
    table, mixed, w_ref,
):
    build_w(ab_ref, 0, w_ref)
    lanes = lax.broadcasted_iota(jnp.int32, (1, 128), 1)
    low8 = low_lanes((8, 128))
    table[GONE] = jnp.zeros((8, 128), F32)
    table[GONE + 8] = jnp.zeros((8, 128), F32)
    for cell in range(9):
        spread_cell(left, cell, table, cell)
        spread_cell(right, cell, table, 18 + cell)
    for at in range(90):
        table[90 + at] = centre[at]
    names = jnp.full((1, 128), 512, jnp.int32)
    for cell in range(27):
        meta = table[cell * 10 + 9, 0:1, :]
        other = turned(meta)
        name = jnp.where(low8[0:1], meta * 8.0 + other, other * 8.0 + meta).astype(jnp.int32)
        names = jnp.where(lanes == cell, name, names)
    names_ref[...] = names
    for cell in range(28):
        mid_tiles[cell] = table[cell * 10 + 8]

    def source(t, ex, e):
        return table[numbers[t, ex * 9 + e]]

    for pair in range(4):
        pieces = []
        for t in (2 * pair, 2 * pair + 1):
            for ep in range(5):
                pieces.append(
                    jnp.concatenate(
                        [
                            pair_of(source(t, ex, 2 * ep), source(t, ex, min(2 * ep + 1, 8)))
                            for ex in range(3)
                        ],
                        axis=0,
                    ).astype(BF16)
                )
        product = dot(x_ref[0], jnp.concatenate(pieces, axis=1))
        for term in range(4):
            row = term * PLANE + pair * 16
            last = None
            for quad in range(QUADS):
                at = (quad * 4 + term) * 8
                tile = jnp.concatenate(
                    [product[at : at + 8, :512], product[at : at + 8, 640:1152]], axis=0
                )
                mixed[row : row + 16, quad * 512 : quad * 512 + 512] = tile.astype(BF16)
                tile = jnp.concatenate(
                    [product[at : at + 8, 512:640], product[at : at + 8, 1152:1280]], axis=0
                )
                if quad % 2 == 0:
                    last = tile
                else:
                    to = 4096 + quad // 2 * 128
                    tile = jnp.where(low_lanes((16, 128)), last, tile)
                    mixed[row : row + 16, to : to + 128] = tile.astype(BF16)
    result = None
    for half in range(2):
        total = None
        own = slice(half * 128, half * 128 + 128)
        for part in range(9):
            some = slice(part * 512, part * 512 + 512)
            term = dot(mixed[own, some], w_ref[some, own])
            total = term if total is None else total + term
        for term in range(2):
            rows = slice(term * PLANE, term * PLANE + PLANE)
            result = total[rows, rows] if result is None else result + total[rows, rows]
    direct[...] = result.reshape(8, 8, PLANE)


def last_kernel(
    numbers, names, planes, mid_tiles, direct, ab_ref, x_ref, rows_h, filters_h, mids_h,
    fine_out, mid_out,
    coarse, back, rows_p, filters, mids, sems, w_mid, w_coarse,
):
    copies = fetches(sems, (rows_h, rows_p), (filters_h, filters), (mids_h, mids))
    build_w(ab_ref, 1, w_mid)
    build_w(ab_ref, 2, w_coarse)
    low8 = low_lanes((8, 128))

    total = None
    for plane in range(8):
        term = planes[plane].astype(F32)
        total = term if total is None else total + term
    for c2 in range(32):
        tile = total[c2 * 8 : c2 * 8 + 8, :]
        other = turned(tile)
        coarse[2 * c2] = jnp.where(low8, tile, other)
        coarse[2 * c2 + 1] = jnp.where(low8, other, tile)
    coarse[64] = jnp.zeros((8, 128), F32)
    octant = numbers[10, 8] & 7

    def coarse_source(ex, e):
        return coarse[numbers[9, ex * 9 + e]]

    sources = jnp.concatenate(
        [
            jnp.concatenate(
                [
                    pair_of(coarse_source(ex, 2 * ep), coarse_source(ex, min(2 * ep + 1, 8)))
                    for ex in range(3)
                ],
                axis=0,
            ).astype(BF16)
            for ep in range(5)
        ],
        axis=1,
    )
    coarse_result = apply_one(sources, x_ref[2], w_coarse)

    for copy in copies:
        copy.wait()
    uppers, octants, owns = [], [], []
    for ep in range(5):
        for ex in range(3):
            first = numbers[8, ex * 9 + 2 * ep]
            second = numbers[8, ex * 9 + min(2 * ep + 1, 8)]
            name_1, name_2 = names[0, first], names[0, second]
            owns.append(pair_of(mid_tiles[first], mid_tiles[second]))
            both = pair_of(coarse[name_1 >> 3], coarse[name_2 >> 3])
            named = jnp.where(low8, name_1 & 7, name_2 & 7)
            octants.append(named)
            mix_0, mix_1 = two_row_mixes(rows_p, both, 128)
            uppers.append(jnp.where(named >= 4, mix_1, mix_0))
    stacked = jnp.concatenate(uppers, axis=0)
    high = stacked.astype(BF16).astype(F32)
    spread = dot(jnp.concatenate([high, stacked - high], axis=0).astype(BF16), mids[...])
    spread = spread[:120, :512] + spread[120:, :512] + spread[:120, 512:]
    pieces = []
    for ep in range(5):
        tiles = []
        for ex in range(3):
            at = ep * 3 + ex
            which = octants[at] & 3
            chosen = spread[at * 8 : at * 8 + 8, 0:128]
            for jl in range(1, 4):
                chosen = jnp.where(
                    which == jl, spread[at * 8 : at * 8 + 8, jl * 128 : jl * 128 + 128], chosen
                )
            tiles.append(owns[at] - chosen)
        pieces.append(jnp.concatenate(tiles, axis=0).astype(BF16))
    mid_result = apply_one(jnp.concatenate(pieces, axis=1), x_ref[1], w_mid)

    row_at = (octant >> 2) * 8
    upper = row_mix([rows_p[row_at + p, :, :PLANE] for p in range(8)], coarse_result)
    single = filters[pl.ds(pl.multiple_of(256 + (octant & 3) * 64, 64), 64), :]
    middle = mid_result + fine_dot(upper, single)
    for a in range(8):
        mid_out[:, a * PLANE : (a + 1) * PLANE] = middle[a : a + 1, :]
    live = jnp.full((8, PLANE), numbers[10, 9], jnp.int32).astype(F32)
    upper = jnp.concatenate(two_row_mixes(rows_p, middle, PLANE), axis=0)
    prol = jnp.concatenate([filters[64 * k : 64 * k + 64, :] for k in range(4)], axis=1)
    spread = fine_dot(upper, prol)
    for o in range(8):
        i, jl = o // 4, o % 4
        slot = numbers[10, o]
        part = spread[i * 8 : i * 8 + 8, jl * PLANE : (jl + 1) * PLANE]
        back[slot] = live * (direct[slot] + part)
    for a in range(8):
        fine_out[:, a * PLANE : (a + 1) * PLANE] = back[:, a, :]


def call(kernel, kinds, outs, scratch, flops, *args):
    any_space = pl.BlockSpec(memory_space=pl.ANY)
    vmem = pl.BlockSpec(memory_space=pltpu.VMEM)
    specs = dict(s=pl.BlockSpec(memory_space=pltpu.SMEM), v=vmem, w=vmem, h=any_space)
    moved = sum(math.prod(x.shape) * x.dtype.itemsize for x in (*args, *outs))
    spaces = dict(w=pltpu.VMEM, h=pltpu.HBM)
    args = [
        pltpu.with_memory_space_constraint(x, spaces[kind]) if kind in spaces else x
        for kind, x in zip(kinds, args, strict=True)
    ]
    return pl.pallas_call(
        kernel,
        out_shape=outs,
        in_specs=[specs[kind] for kind in kinds],
        out_specs=[any_space if getattr(x, "memory_space", None) == pltpu.HBM else vmem for x in outs],
        scratch_shapes=scratch,
        compiler_params=pltpu.CompilerParams(vmem_limit_bytes=VMEM_LIMIT),
        cost_estimate=pl.CostEstimate(flops=flops, bytes_accessed=moved, transcendentals=0),
        name=kernel.__name__,
    )(*args)


def both_ways(x, axis):
    count = lax.axis_size(axis)
    ends = count - 1
    before = lax.ppermute(x, axis, [(i, i + 1) for i in range(ends)])
    after = lax.ppermute(x, axis, [(i + 1, i) for i in range(ends)])
    return before, after


def shards(
    fine_coef, mid_leaf, mid_child, mid_parent, mid_refined,
    fine_nbr, mid_nbr, coarse_nbr, op_factor, term_weight,
):
    tables = filter_tables()
    select = jnp.asarray(select_tables())
    prol_rows = np.concatenate(np.split(tables["prol"], 4, axis=1), axis=0)
    single_rows = tables["single"].reshape(256, 128)
    first_filters = jnp.asarray(
        np.concatenate([tables["comp"], prol_rows, tables["contrib"].reshape(256, 128)])
    )
    last_filters = jnp.asarray(np.concatenate([prol_rows, single_rows]))
    rows_both = jnp.asarray(np.concatenate([tables["rows_c"], tables["rows_p"]]))
    rows_p = jnp.asarray(tables["rows_p"])
    mids = jnp.asarray(tables["mids"])
    factors = op_factor.transpose(0, 2, 3, 4, 1).reshape(3, 192, TERMS)

    sds = jax.ShapeDtypeStruct
    vmem, smem = pltpu.VMEM, pltpu.SMEM
    i32 = jnp.int32
    halo, payload, numbers = call(
        first_kernel,
        "sshhhhhhhh",
        [sds((48, 128), BF16), sds((64, 8, 128), BF16), sds((16, 128), i32)],
        [
            smem((1, 8), i32),
            vmem((1, 8), i32),
            vmem((8, 27), i32),
            vmem((1, 27), i32),
            vmem((27, 64), i32),
            vmem((8, 512), BF16),
            vmem((1, 512), BF16),
            vmem((768, 128), BF16),
            vmem((32, 8, 128), F32),
            vmem((8, 8, PLANE), F32),
            vmem((8, 8, PLANE), F32),
            pltpu.SemaphoreType.DMA((9,)),
        ],
        2_000_000,
        mid_parent, mid_refined, mid_child, fine_nbr, mid_nbr, coarse_nbr.T, fine_coef, mid_leaf,
        first_filters, rows_both,
    )
    arrived = lax.all_to_all(payload, ("gy", "gz"), 0, 0, tiled=True)
    before, after = both_ways(halo, "gz")
    line = jnp.concatenate([before, halo, after], axis=0)
    before, after = both_ways(line, "gy")
    sheet = jnp.concatenate([before, line, after], axis=0)
    before, after = both_ways(sheet, "gx")

    (copies,) = call(
        plane_kernel, "v", [sds((8, 256, 128), BF16)], [], 33_000_000, arrived
    )
    planes = lax.all_to_all(copies, "gx", 0, 0, tiled=True)

    w_factors, x_tables, centre = call(
        tables_kernel,
        "hhhv",
        [
            pltpu.VMEM((2, 3 * QUADS, 24, 256), F32),
            pltpu.VMEM((3, 256, 24), BF16),
            pltpu.VMEM((90, 8, 128), F32),
        ],
        [
            vmem((3, 192, TERMS), F32),
            vmem((1, TERMS), F32),
            vmem((256, 768), BF16),
            pltpu.SemaphoreType.DMA((3,)),
        ],
        600_000_000,
        factors, term_weight.reshape(1, TERMS), select, sheet,
    )
    direct, mid_tiles, names = call(
        fine_kernel,
        "svvvww",
        [sds((8, 8, PLANE), F32), sds((28, 8, 128), F32), sds((1, 128), i32)],
        [
            vmem((GONE + 9, 8, 128), F32),
            vmem((256, ROWS_W), BF16),
            vmem((ROWS_W, 256), BF16),
        ],
        100_000_000,
        numbers, before, centre, after, w_factors, x_tables,
    )
    fine_out, mid_out = call(
        last_kernel,
        "ssvvvwwhhh",
        [sds((8, 512), F32), sds((1, 512), F32)],
        [
            vmem((65, 8, 128), F32),
            vmem((8, 8, PLANE), F32),
            vmem((16, 8, 128), F32),
            vmem((512, 128), BF16),
            vmem((128, 1024), BF16),
            pltpu.SemaphoreType.DMA((3,)),
            vmem((ROWS_W, 256), BF16),
            vmem((ROWS_W, 256), BF16),
        ],
        200_000_000,
        numbers, names, planes, mid_tiles, direct, w_factors, x_tables,
        rows_p, last_filters, mids,
    )
    return fine_out, mid_out


def solution(mesh):
    cells = ("gx", "gy", "gz")
    rows = P(cells, None)
    return jax.shard_map(
        shards,
        mesh=mesh,
        in_specs=(rows, rows, rows, P(cells), P(cells), rows, rows, P(), P(), P()),
        out_specs=(rows, rows),
        check_vma=False,
    )
```

```python
import functools
import math

import jax
import jax.numpy as jnp
import ml_dtypes
import numpy as np
from jax import lax
from jax.experimental import pallas as pl
from jax.experimental.pallas import tpu as pltpu
from jax.sharding import PartitionSpec as P

K = 8
PLANE = 64
TERMS = 32
QUADS = 8
ROWS_W = 4608
GONE = 27 * 10
BF16 = jnp.bfloat16
F32 = jnp.float32
VMEM_LIMIT = 32 * 1024 * 1024


def poly_multiply(left, right):
    result = [0.0] * (len(left) + len(right) - 1)
    for first, left_coef in enumerate(left):
        for second, right_coef in enumerate(right):
            result[first + second] += left_coef * right_coef
    return result


def poly_compose(coeffs, factor, offset):
    result = [0.0]
    power_term = [1.0]
    for coef in coeffs:
        padded = result + [0.0] * (len(power_term) - len(result))
        result = [padded[place] + coef * power_term[place] for place in range(len(power_term))]
        power_term = poly_multiply(power_term, [offset, factor])
    return result


def legendre_table(basis_order):
    polys = [[1.0], [0.0, 1.0]]
    for degree in range(1, basis_order):
        upper = [0.0] + [(2 * degree + 1) * coef for coef in polys[degree]]
        lower = [degree * coef for coef in polys[degree - 1]] + [0.0] * (
            len(upper) - len(polys[degree - 1])
        )
        polys.append([(upper[place] - lower[place]) / (degree + 1) for place in range(len(upper))])
    return [
        [math.sqrt(2 * degree + 1) * coef for coef in poly_compose(polys[degree], 2.0, -1.0)]
        for degree in range(basis_order)
    ]


@functools.cache
def two_scale(basis_order):
    shifted = legendre_table(basis_order)
    filters = np.zeros((2, basis_order, basis_order))
    for which_half in range(2):
        for row_at in range(basis_order):
            halved = poly_compose(shifted[row_at], 0.5, 0.5 * which_half)
            for col_at in range(basis_order):
                product = poly_multiply(halved, shifted[col_at])
                total = sum((coef / (place + 1) for place, coef in enumerate(product)))
                filters[which_half, row_at, col_at] = total / math.sqrt(2.0)
    return filters.astype(np.float32).astype(np.float64)


def two_parts(matrix):
    high = matrix.astype(ml_dtypes.bfloat16)
    low = (matrix - high.astype(np.float64)).astype(ml_dtypes.bfloat16)
    return high, low


@functools.cache
def filter_tables():
    h = two_scale(K)
    pair = np.einsum("jqy,lrz->jlqryz", h, h).reshape(4, PLANE, PLANE)
    to_coarse = pair.transpose(0, 2, 1).reshape(4 * PLANE, PLANE)
    comp = np.concatenate(two_parts(to_coarse), axis=1)
    to_fine = pair.transpose(1, 0, 2).reshape(PLANE, 4 * PLANE)
    prol = np.concatenate(two_parts(to_fine), axis=1)
    contrib = np.stack([np.concatenate(two_parts(pair[k].T), axis=1) for k in range(4)])
    single = np.stack([np.concatenate(two_parts(pair[k]), axis=1) for k in range(4)])
    mid = np.zeros((2, PLANE, 4, 2, PLANE))
    for half in range(2):
        mid[half, :, :, half, :] = pair.transpose(1, 0, 2)
    mids = np.concatenate(two_parts(mid.reshape(128, 512)), axis=1)
    rows_c = np.broadcast_to(h.transpose(0, 2, 1).reshape(16, 8)[:, :, None], (16, 8, 128))
    rows_p = np.broadcast_to(h.reshape(16, 8)[:, :, None], (16, 8, 128))
    return dict(
        comp=comp,
        prol=prol,
        contrib=contrib,
        single=single,
        mids=mids,
        rows_c=np.ascontiguousarray(rows_c).astype(np.float32),
        rows_p=np.ascontiguousarray(rows_p).astype(np.float32),
    )


@functools.cache
def select_tables():
    out = np.arange(256) // TERMS
    term = np.arange(256) % TERMS
    col = np.arange(256)
    group = term[:, None] % 4 == (col // PLANE)[None, :]
    left = group & (out[:, None] == (col // 8 % 8)[None, :])
    right = group & (out[:, None] == (col % 8)[None, :])
    turn = (term[None, :] == (col // 8)[:, None]) & (out[None, :] == (col % 8)[:, None])
    return np.concatenate([left, right, turn], axis=1).astype(ml_dtypes.bfloat16)


def split(value):
    high = value.astype(BF16)
    return high, (value - high.astype(F32)).astype(BF16)


def dot(left, right):
    return jnp.dot(left, right, preferred_element_type=F32)


def fine_dot(value, table):
    rows = value.shape[0]
    width = table.shape[1] // 2
    if rows % 16 == 0:
        result = dot(jnp.concatenate(split(value), axis=0), table)
    else:
        high = value.astype(BF16).astype(F32)
        result = dot(jnp.concatenate([high, value - high], axis=0).astype(BF16), table)
    return result[:rows, :width] + result[rows:, :width] + result[:rows, width:]


def low_lanes(shape):
    return lax.broadcasted_iota(jnp.int32, shape, len(shape) - 1) < PLANE


def turned(value):
    return pltpu.roll(value, PLANE, value.ndim - 1)


def row_mix(tables, tile):
    total = None
    for p in range(8):
        term = tables[p] * tile[p : p + 1, :]
        total = term if total is None else total + term
    return total


def two_row_mixes(rows_ref, tile, width):
    return [
        row_mix([rows_ref[i * 8 + p, :, :width] for p in range(8)], tile) for i in range(2)
    ]


def fetches(sems, *pairs):
    copies = [
        pltpu.make_async_copy(there, here, sems.at[at]) for at, (there, here) in enumerate(pairs)
    ]
    for copy in copies:
        copy.start()
    return copies


def local_cell(device, own):
    step_x = (device >> 6) - (own >> 6) + 1
    step_y = ((device >> 3) & 7) - ((own >> 3) & 7) + 1
    step_z = (device & 7) - (own & 7) + 1
    return step_x * 9 + step_y * 3 + step_z


def tables_kernel(
    factors_h, weights_h, select_h, sheet,
    ab_ref, x_ref, tiles,
    factors, weights, select, sems,
):
    copies = fetches(sems, (factors_h, factors), (weights_h, weights), (select_h, select))
    for cell in range(9):
        spread_cell(sheet, cell, tiles, cell)
    for copy in copies:
        copy.wait()
    lane = lax.broadcasted_iota(jnp.int32, (24, 256), 1)
    quad_of = (lane & 31) >> 2
    weight = jnp.concatenate([weights[...]] * 8, axis=1)
    weighted, plain = [], []
    for level in range(3):
        rows = []
        for e in range(3):
            rows.append(
                jnp.concatenate(
                    [factors[level, e * 64 + b * 8 : e * 64 + b * 8 + 8, :] for b in range(8)],
                    axis=1,
                )
            )
        values = jnp.concatenate(rows, axis=0)
        scaled = values * weight
        for quad in range(QUADS):
            weighted.append(jnp.where(quad_of == quad, scaled, 0.0))
            plain.append(jnp.where(quad_of == quad, values, 0.0))
        x_ref[level] = lax.dot_general(
            select[:, 512:768],
            values.astype(BF16),
            (((1,), (1,)), ((), ())),
            preferred_element_type=F32,
        ).astype(BF16)
    for which, parts in enumerate((weighted, plain)):
        both = dot(
            jnp.concatenate(split(jnp.concatenate(parts, axis=0)), axis=0),
            select[:, which * 256 : which * 256 + 256],
        )
        ab_ref[which] = (both[:576] + both[576:]).reshape(24, 24, 256)


def build_w(ab_ref, level, w_ref):
    def one_quad(quad, carry):
        at = level * QUADS + quad
        inner = [ab_ref[1, at, ez * 8 : ez * 8 + 8, :] for ez in range(3)]
        for ey in range(3):
            for pair in range(4):
                row = ey * 8 + 2 * pair
                first = ab_ref[0, at, row : row + 1, :]
                second = ab_ref[0, at, row + 1 : row + 2, :]
                for ez in range(3):
                    tile = jnp.concatenate([first * inner[ez], second * inner[ez]], axis=0)
                    e = ey * 3 + ez
                    to = quad * 512 + e * PLANE if e < 8 else 4096 + quad * PLANE
                    to = pl.multiple_of(to + pair * 16, 16)
                    w_ref[pl.ds(to, 16), :] = tile.astype(BF16)
        return carry

    lax.fori_loop(0, QUADS, one_quad, 0)


def spread_cell(sheet, cell, tiles, to):
    low = low_lanes((8, 128))
    base = cell * 48
    for group in range(2):
        both = sheet[base + group * 16 : base + group * 16 + 16, :].astype(F32)
        for sub in range(2):
            tile = both[sub * 8 : sub * 8 + 8, :]
            other = turned(tile)
            tiles[to * 10 + group * 4 + sub * 2] = jnp.where(low, tile, other)
            tiles[to * 10 + group * 4 + sub * 2 + 1] = jnp.where(low, other, tile)
    last = sheet[base + 32 : base + 48, :].astype(F32)
    tiles[to * 10 + 8] = last[0:8, :]
    tiles[to * 10 + 9] = last[8:16, :]


def diagonal_sum(result, rows):
    total = None
    for term in range(4):
        piece = result[term * rows : (term + 1) * rows, term * PLANE : (term + 1) * PLANE]
        total = piece if total is None else total + piece
    return total


def apply_one(sources, x_table, w_ref):
    product = dot(x_table, sources)
    low = low_lanes((32, 128))
    groups = [product[quad * 32 : quad * 32 + 32, :] for quad in range(QUADS)]
    pieces = [group[:, :512].astype(BF16) for group in groups]
    for quad in range(0, QUADS, 2):
        both = jnp.where(low, groups[quad][:, 512:], groups[quad + 1][:, 512:])
        pieces.append(both.astype(BF16))
    result = dot(jnp.concatenate(pieces, axis=1), w_ref[...])
    return diagonal_sum(result, 8)


def first_kernel(
    parent, refined, child_h, fine_h, mid_h, coarse_h, coef_h, leaf_h, filters_h, rows_h,
    halo, payload, numbers,
    child, child_v, fine_nbr, mid_nbr, coarse_nbr, coef, leaf, filters, rows,
    source, detail, sems, payload_v, payload_sem,
):
    copies = fetches(
        sems,
        (child_h, child),
        (coef_h, coef),
        (filters_h, filters),
        (rows_h, rows),
        (leaf_h, leaf),
        (child_h, child_v),
        (fine_h, fine_nbr),
        (mid_h, mid_nbr),
        (coarse_h, coarse_nbr),
    )
    for copy in copies[:5]:
        copy.wait()
    comp = filters[0:256, :]
    prol = jnp.concatenate([filters[256 + 64 * k : 320 + 64 * k, :] for k in range(4)], axis=1)
    slot = parent[0] >> 3
    octant = parent[0] & 7

    values = coef[...].astype(F32)
    for a in range(8):
        source[:, a, :] = values[:, a * PLANE : (a + 1) * PLANE]
    tiles = [source[child[0, o]] for o in range(8)]
    lhs = jnp.concatenate(
        [jnp.concatenate(tiles[0:4], axis=1), jnp.concatenate(tiles[4:8], axis=1)], axis=0
    ).astype(BF16)
    both = dot(lhs, comp)
    partial = both[:, :PLANE] + both[:, PLANE:]
    compressed = None
    for k in range(16):
        term = rows[k, :, :PLANE] * partial[k : k + 1, :]
        compressed = term if compressed is None else compressed + term
    leaf_row = leaf[...].astype(F32)
    leaf_tile = jnp.concatenate(
        [leaf_row[:, a * PLANE : (a + 1) * PLANE] for a in range(8)], axis=0
    )
    middle = jnp.where(refined[0] > 0, compressed, leaf_tile).astype(BF16).astype(F32)

    row_at = (octant >> 2) * 8
    inner = row_mix([rows[row_at + x, :, :PLANE] for x in range(8)], middle)
    table = filters[pl.ds(pl.multiple_of(512 + (octant & 3) * 64, 64), 64), :]
    added = fine_dot(inner, table)
    low8 = low_lanes((8, 128))
    tag = jnp.full((8, 128), slot, jnp.int32).astype(F32)
    tile = jnp.where(low8, jnp.concatenate([added, added], axis=1), tag).astype(BF16)
    payload_v[...] = jnp.broadcast_to(tile[None], payload_v.shape)
    send = pltpu.make_async_copy(payload_v, payload, payload_sem)
    send.start()

    live = jnp.full((8, PLANE), refined[0], jnp.int32).astype(F32)
    upper = jnp.concatenate(two_row_mixes(rows.at[16:32], middle, PLANE), axis=0)
    spread = fine_dot(upper, prol)
    for o in range(8):
        i, jl = o // 4, o % 4
        part = spread[i * 8 : i * 8 + 8, jl * PLANE : (jl + 1) * PLANE]
        detail[child[0, o]] = live * (tiles[o] - part)
    for group in range(2):
        base = group * 4
        halo[group * 16 : group * 16 + 16, :] = jnp.concatenate(
            [
                jnp.concatenate([detail[base], detail[base + 1]], axis=1),
                jnp.concatenate([detail[base + 2], detail[base + 3]], axis=1),
            ],
            axis=0,
        ).astype(BF16)
    meta = jnp.where(low8, tag, jnp.full((8, 128), octant, jnp.int32).astype(F32))
    halo[32:48, :] = jnp.concatenate(
        [jnp.concatenate([middle, middle], axis=1), meta], axis=0
    ).astype(BF16)

    for copy in copies[5:]:
        copy.wait()
    near = fine_nbr[...]
    own = near[:, 13:14] >> 3
    cell = local_cell(near >> 3, own) * 10 + (near & 7)
    numbers[0:8, 0:27] = jnp.where(near >= 0, cell, GONE)
    near_mid = mid_nbr[...]
    own_mid = near_mid[:, 13:14]
    numbers[8:9, 0:27] = jnp.where(near_mid >= 0, local_cell(near_mid, own_mid), 27)
    numbers[8:9, 27:28] = jnp.full((1, 1), 27, jnp.int32)
    hot = jnp.where(lax.broadcasted_iota(jnp.int32, (8, 64), 1) == slot, 1.0, 0.0).astype(BF16)
    near_coarse = lax.dot_general(
        hot,
        coarse_nbr[...].astype(F32).astype(BF16),
        (((1,), (1,)), ((), ())),
        preferred_element_type=F32,
    )[0:1].astype(jnp.int32)
    numbers[9:10, 0:27] = jnp.where(near_coarse >= 0, near_coarse, 64)
    numbers[9:10, 27:28] = jnp.full((1, 1), 64, jnp.int32)
    numbers[10:11, 0:8] = child_v[...]
    numbers[10:11, 8:9] = jnp.full((1, 1), parent[0], jnp.int32)
    numbers[10:11, 9:10] = jnp.full((1, 1), refined[0], jnp.int32)
    send.wait()


def plane_kernel(arrived, copies, partial, sems):
    rows = arrived[...].astype(F32).reshape(512, 128)
    other = turned(rows)
    low = low_lanes((512, 128))
    value = jnp.where(low, rows, other)
    tag = jnp.where(low, other, rows)
    half = jnp.where(low, 0, 1)
    rhs = jnp.where((tag.astype(jnp.int32) & 1) == half, value, 0.0).astype(BF16)
    pick = jnp.where(lax.broadcasted_iota(jnp.int32, (8, 128), 1) == 0, 1.0, 0.0).astype(BF16)
    along = lax.dot_general(
        pick, tag.astype(BF16), (((1,), (1,)), ((), ())), preferred_element_type=F32
    ).astype(jnp.int32)
    p_of = lax.broadcasted_iota(jnp.int32, (8, 512), 1) & 7
    key = jnp.where(p_of == lax.broadcasted_iota(jnp.int32, (8, 512), 0), along >> 1, -1)
    hot = jnp.concatenate(
        [jnp.where(key == c2, 1.0, 0.0) for c2 in range(32)], axis=0
    ).astype(BF16)
    partial[...] = dot(hot, rhs).astype(BF16)
    for copy in fetches(sems, *((partial, copies.at[at]) for at in range(8))):
        copy.wait()


def pair_of(first, second):
    return jnp.where(low_lanes((8, 128)), first, second)


def fine_kernel(
    numbers_h, left, centre, right, ab_ref, x_ref,
    direct, mid_tiles, names_ref,
    table, mixed, w_ref, numbers, sems,
):
    copies = fetches(sems, (numbers_h, numbers))
    build_w(ab_ref, 0, w_ref)
    lanes = lax.broadcasted_iota(jnp.int32, (1, 128), 1)
    low8 = low_lanes((8, 128))
    table[GONE] = jnp.zeros((8, 128), F32)
    table[GONE + 8] = jnp.zeros((8, 128), F32)
    for cell in range(9):
        spread_cell(left, cell, table, cell)
        spread_cell(right, cell, table, 18 + cell)
    for at in range(90):
        table[90 + at] = centre[at]
    names = jnp.full((1, 128), 512, jnp.int32)
    for cell in range(27):
        meta = table[cell * 10 + 9, 0:1, :]
        other = turned(meta)
        name = jnp.where(low8[0:1], meta * 8.0 + other, other * 8.0 + meta).astype(jnp.int32)
        names = jnp.where(lanes == cell, name, names)
    names_ref[...] = names
    for cell in range(28):
        mid_tiles[cell] = table[cell * 10 + 8]

    for copy in copies:
        copy.wait()

    def source(t, ex, e):
        return table[numbers[t, ex * 9 + e]]

    for pair in range(4):
        pieces = []
        for t in (2 * pair, 2 * pair + 1):
            for ep in range(5):
                pieces.append(
                    jnp.concatenate(
                        [
                            pair_of(source(t, ex, 2 * ep), source(t, ex, min(2 * ep + 1, 8)))
                            for ex in range(3)
                        ],
                        axis=0,
                    ).astype(BF16)
                )
        product = dot(x_ref[0], jnp.concatenate(pieces, axis=1))
        for term in range(4):
            row = term * PLANE + pair * 16
            last = None
            for quad in range(QUADS):
                at = (quad * 4 + term) * 8
                tile = jnp.concatenate(
                    [product[at : at + 8, :512], product[at : at + 8, 640:1152]], axis=0
                )
                mixed[row : row + 16, quad * 512 : quad * 512 + 512] = tile.astype(BF16)
                tile = jnp.concatenate(
                    [product[at : at + 8, 512:640], product[at : at + 8, 1152:1280]], axis=0
                )
                if quad % 2 == 0:
                    last = tile
                else:
                    to = 4096 + quad // 2 * 128
                    tile = jnp.where(low_lanes((16, 128)), last, tile)
                    mixed[row : row + 16, to : to + 128] = tile.astype(BF16)
    result = None
    for half in range(2):
        total = None
        own = slice(half * 128, half * 128 + 128)
        for part in range(9):
            some = slice(part * 512, part * 512 + 512)
            term = dot(mixed[own, some], w_ref[some, own])
            total = term if total is None else total + term
        for term in range(2):
            rows = slice(term * PLANE, term * PLANE + PLANE)
            result = total[rows, rows] if result is None else result + total[rows, rows]
    direct[...] = result.reshape(8, 8, PLANE)


def last_kernel(
    numbers_h, names_h, planes, mid_tiles, direct, ab_ref, x_ref, rows_h, filters_h, mids_h,
    fine_out, mid_out,
    coarse, back, rows_p, filters, mids, sems, w_mid, w_coarse, numbers, names,
):
    copies = fetches(
        sems,
        (numbers_h, numbers),
        (names_h, names),
        (rows_h, rows_p),
        (filters_h, filters),
        (mids_h, mids),
    )
    build_w(ab_ref, 1, w_mid)
    build_w(ab_ref, 2, w_coarse)
    low8 = low_lanes((8, 128))

    total = None
    for plane in range(8):
        term = planes[plane].astype(F32)
        total = term if total is None else total + term
    for c2 in range(32):
        tile = total[c2 * 8 : c2 * 8 + 8, :]
        other = turned(tile)
        coarse[2 * c2] = jnp.where(low8, tile, other)
        coarse[2 * c2 + 1] = jnp.where(low8, other, tile)
    coarse[64] = jnp.zeros((8, 128), F32)
    for copy in copies:
        copy.wait()
    octant = numbers[10, 8] & 7

    def coarse_source(ex, e):
        return coarse[numbers[9, ex * 9 + e]]

    sources = jnp.concatenate(
        [
            jnp.concatenate(
                [
                    pair_of(coarse_source(ex, 2 * ep), coarse_source(ex, min(2 * ep + 1, 8)))
                    for ex in range(3)
                ],
                axis=0,
            ).astype(BF16)
            for ep in range(5)
        ],
        axis=1,
    )
    coarse_result = apply_one(sources, x_ref[2], w_coarse)

    uppers, octants, owns = [], [], []
    for ep in range(5):
        for ex in range(3):
            first = numbers[8, ex * 9 + 2 * ep]
            second = numbers[8, ex * 9 + min(2 * ep + 1, 8)]
            name_1, name_2 = names[0, first], names[0, second]
            owns.append(pair_of(mid_tiles[first], mid_tiles[second]))
            both = pair_of(coarse[name_1 >> 3], coarse[name_2 >> 3])
            named = jnp.where(low8, name_1 & 7, name_2 & 7)
            octants.append(named)
            mix_0, mix_1 = two_row_mixes(rows_p, both, 128)
            uppers.append(jnp.where(named >= 4, mix_1, mix_0))
    stacked = jnp.concatenate(uppers, axis=0)
    high = stacked.astype(BF16).astype(F32)
    spread = dot(jnp.concatenate([high, stacked - high], axis=0).astype(BF16), mids[...])
    spread = spread[:120, :512] + spread[120:, :512] + spread[:120, 512:]
    pieces = []
    for ep in range(5):
        tiles = []
        for ex in range(3):
            at = ep * 3 + ex
            which = octants[at] & 3
            chosen = spread[at * 8 : at * 8 + 8, 0:128]
            for jl in range(1, 4):
                chosen = jnp.where(
                    which == jl, spread[at * 8 : at * 8 + 8, jl * 128 : jl * 128 + 128], chosen
                )
            tiles.append(owns[at] - chosen)
        pieces.append(jnp.concatenate(tiles, axis=0).astype(BF16))
    mid_result = apply_one(jnp.concatenate(pieces, axis=1), x_ref[1], w_mid)

    row_at = (octant >> 2) * 8
    upper = row_mix([rows_p[row_at + p, :, :PLANE] for p in range(8)], coarse_result)
    single = filters[pl.ds(pl.multiple_of(256 + (octant & 3) * 64, 64), 64), :]
    middle = mid_result + fine_dot(upper, single)
    for a in range(8):
        mid_out[:, a * PLANE : (a + 1) * PLANE] = middle[a : a + 1, :]
    live = jnp.full((8, PLANE), numbers[10, 9], jnp.int32).astype(F32)
    upper = jnp.concatenate(two_row_mixes(rows_p, middle, PLANE), axis=0)
    prol = jnp.concatenate([filters[64 * k : 64 * k + 64, :] for k in range(4)], axis=1)
    spread = fine_dot(upper, prol)
    for o in range(8):
        i, jl = o // 4, o % 4
        slot = numbers[10, o]
        part = spread[i * 8 : i * 8 + 8, jl * PLANE : (jl + 1) * PLANE]
        back[slot] = live * (direct[slot] + part)
    for a in range(8):
        fine_out[:, a * PLANE : (a + 1) * PLANE] = back[:, a, :]


def call(kernel, kinds, outs, scratch, flops, *args):
    any_space = pl.BlockSpec(memory_space=pl.ANY)
    vmem = pl.BlockSpec(memory_space=pltpu.VMEM)
    specs = dict(s=pl.BlockSpec(memory_space=pltpu.SMEM), v=vmem, w=vmem, h=any_space, a=any_space)
    moved = sum(math.prod(x.shape) * x.dtype.itemsize for x in (*args, *outs))
    spaces = dict(w=pltpu.VMEM, h=pltpu.HBM)
    args = [
        pltpu.with_memory_space_constraint(x, spaces[kind]) if kind in spaces else x
        for kind, x in zip(kinds, args, strict=True)
    ]
    return pl.pallas_call(
        kernel,
        out_shape=outs,
        in_specs=[specs[kind] for kind in kinds],
        out_specs=[any_space if getattr(x, "memory_space", None) == pltpu.HBM else vmem for x in outs],
        scratch_shapes=scratch,
        compiler_params=pltpu.CompilerParams(vmem_limit_bytes=VMEM_LIMIT),
        cost_estimate=pl.CostEstimate(flops=flops, bytes_accessed=moved, transcendentals=0),
        name=kernel.__name__,
    )(*args)


def both_ways(x, axis):
    count = lax.axis_size(axis)
    ends = count - 1
    before = lax.ppermute(x, axis, [(i, i + 1) for i in range(ends)])
    after = lax.ppermute(x, axis, [(i + 1, i) for i in range(ends)])
    return before, after


def shards(
    fine_coef, mid_leaf, mid_child, mid_parent, mid_refined,
    fine_nbr, mid_nbr, coarse_nbr, op_factor, term_weight,
):
    tables = filter_tables()
    select = jnp.asarray(select_tables())
    prol_rows = np.concatenate(np.split(tables["prol"], 4, axis=1), axis=0)
    single_rows = tables["single"].reshape(256, 128)
    first_filters = jnp.asarray(
        np.concatenate([tables["comp"], prol_rows, tables["contrib"].reshape(256, 128)])
    )
    last_filters = jnp.asarray(np.concatenate([prol_rows, single_rows]))
    rows_both = jnp.asarray(np.concatenate([tables["rows_c"], tables["rows_p"]]))
    rows_p = jnp.asarray(tables["rows_p"])
    mids = jnp.asarray(tables["mids"])
    factors = op_factor.transpose(0, 2, 3, 4, 1).reshape(3, 192, TERMS)

    sds = jax.ShapeDtypeStruct
    vmem, smem = pltpu.VMEM, pltpu.SMEM
    i32 = jnp.int32
    halo, payload, numbers = call(
        first_kernel,
        "sshhhhhhhh",
        [sds((48, 128), BF16), pltpu.HBM((64, 8, 128), BF16), sds((16, 128), i32)],
        [
            smem((1, 8), i32),
            vmem((1, 8), i32),
            vmem((8, 27), i32),
            vmem((1, 27), i32),
            vmem((27, 64), i32),
            vmem((8, 512), BF16),
            vmem((1, 512), BF16),
            vmem((768, 128), BF16),
            vmem((32, 8, 128), F32),
            vmem((8, 8, PLANE), F32),
            vmem((8, 8, PLANE), F32),
            pltpu.SemaphoreType.DMA((9,)),
            vmem((64, 8, 128), BF16),
            pltpu.SemaphoreType.DMA,
        ],
        2_000_000,
        mid_parent, mid_refined, mid_child, fine_nbr, mid_nbr, coarse_nbr.T, fine_coef, mid_leaf,
        first_filters, rows_both,
    )
    arrived = lax.all_to_all(payload, ("gy", "gz"), 0, 0, tiled=True)
    before, after = both_ways(halo, "gz")
    line = jnp.concatenate([before, halo, after], axis=0)
    before, after = both_ways(line, "gy")
    sheet = jnp.concatenate([before, line, after], axis=0)
    before, after = both_ways(sheet, "gx")

    (copies,) = call(
        plane_kernel, "v", [pltpu.HBM((8, 256, 128), BF16)],
        [vmem((256, 128), BF16), pltpu.SemaphoreType.DMA((8,))], 33_000_000, arrived
    )
    planes = lax.all_to_all(copies, "gx", 0, 0, tiled=True)

    w_factors, x_tables, centre = call(
        tables_kernel,
        "hhhv",
        [
            pltpu.VMEM((2, 3 * QUADS, 24, 256), F32),
            pltpu.VMEM((3, 256, 24), BF16),
            pltpu.VMEM((90, 8, 128), F32),
        ],
        [
            vmem((3, 192, TERMS), F32),
            vmem((1, TERMS), F32),
            vmem((256, 768), BF16),
            pltpu.SemaphoreType.DMA((3,)),
        ],
        600_000_000,
        factors, term_weight.reshape(1, TERMS), select, sheet,
    )
    direct, mid_tiles, names = call(
        fine_kernel,
        "avvvww",
        [sds((8, 8, PLANE), F32), sds((28, 8, 128), F32), sds((1, 128), i32)],
        [
            vmem((GONE + 9, 8, 128), F32),
            vmem((256, ROWS_W), BF16),
            vmem((ROWS_W, 256), BF16),
            smem((16, 128), i32),
            pltpu.SemaphoreType.DMA((1,)),
        ],
        100_000_000,
        numbers, before, centre, after, w_factors, x_tables,
    )
    fine_out, mid_out = call(
        last_kernel,
        "aavvvwwhhh",
        [sds((8, 512), F32), sds((1, 512), F32)],
        [
            vmem((65, 8, 128), F32),
            vmem((8, 8, PLANE), F32),
            vmem((16, 8, 128), F32),
            vmem((512, 128), BF16),
            vmem((128, 1024), BF16),
            pltpu.SemaphoreType.DMA((5,)),
            vmem((ROWS_W, 256), BF16),
            vmem((ROWS_W, 256), BF16),
            smem((16, 128), i32),
            smem((1, 128), i32),
        ],
        200_000_000,
        numbers, names, planes, mid_tiles, direct, w_factors, x_tables,
        rows_p, last_filters, mids,
    )
    return fine_out, mid_out


def solution(mesh):
    cells = ("gx", "gy", "gz")
    rows = P(cells, None)
    return jax.shard_map(
        shards,
        mesh=mesh,
        in_specs=(rows, rows, rows, P(cells), P(cells), rows, rows, P(), P(), P()),
        out_specs=(rows, rows),
        check_vma=False,
    )
```

```python
import functools
import math

import jax
import jax.numpy as jnp
import ml_dtypes
import numpy as np
from jax import lax
from jax.experimental import pallas as pl
from jax.experimental.pallas import tpu as pltpu
from jax.sharding import PartitionSpec as P

K = 8
PLANE = 64
TERMS = 32
QUADS = 8
ROWS_W = 4608
CELL = 40
GONE = 27 * 10
BF16 = jnp.bfloat16
F32 = jnp.float32
VMEM_LIMIT = 32 * 1024 * 1024


def poly_multiply(left, right):
    result = [0.0] * (len(left) + len(right) - 1)
    for first, left_coef in enumerate(left):
        for second, right_coef in enumerate(right):
            result[first + second] += left_coef * right_coef
    return result


def poly_compose(coeffs, factor, offset):
    result = [0.0]
    power_term = [1.0]
    for coef in coeffs:
        padded = result + [0.0] * (len(power_term) - len(result))
        result = [padded[place] + coef * power_term[place] for place in range(len(power_term))]
        power_term = poly_multiply(power_term, [offset, factor])
    return result


def legendre_table(basis_order):
    polys = [[1.0], [0.0, 1.0]]
    for degree in range(1, basis_order):
        upper = [0.0] + [(2 * degree + 1) * coef for coef in polys[degree]]
        lower = [degree * coef for coef in polys[degree - 1]] + [0.0] * (
            len(upper) - len(polys[degree - 1])
        )
        polys.append([(upper[place] - lower[place]) / (degree + 1) for place in range(len(upper))])
    return [
        [math.sqrt(2 * degree + 1) * coef for coef in poly_compose(polys[degree], 2.0, -1.0)]
        for degree in range(basis_order)
    ]


@functools.cache
def two_scale(basis_order):
    shifted = legendre_table(basis_order)
    filters = np.zeros((2, basis_order, basis_order))
    for which_half in range(2):
        for row_at in range(basis_order):
            halved = poly_compose(shifted[row_at], 0.5, 0.5 * which_half)
            for col_at in range(basis_order):
                product = poly_multiply(halved, shifted[col_at])
                total = sum((coef / (place + 1) for place, coef in enumerate(product)))
                filters[which_half, row_at, col_at] = total / math.sqrt(2.0)
    return filters.astype(np.float32).astype(np.float64)


def two_parts(matrix):
    high = matrix.astype(ml_dtypes.bfloat16)
    low = (matrix - high.astype(np.float64)).astype(ml_dtypes.bfloat16)
    return high, low


@functools.cache
def filter_tables():
    h = two_scale(K)
    pair = np.einsum("jqy,lrz->jlqryz", h, h).reshape(4, PLANE, PLANE)
    to_coarse = pair.transpose(0, 2, 1).reshape(4 * PLANE, PLANE)
    comp = np.concatenate(two_parts(to_coarse), axis=1)
    to_fine = pair.transpose(1, 0, 2).reshape(PLANE, 4 * PLANE)
    prol = np.concatenate(two_parts(to_fine), axis=1)
    contrib = np.stack([np.concatenate(two_parts(pair[k].T), axis=1) for k in range(4)])
    single = np.stack([np.concatenate(two_parts(pair[k]), axis=1) for k in range(4)])
    mid = np.zeros((2, PLANE, 4, 2, PLANE))
    for half in range(2):
        mid[half, :, :, half, :] = pair.transpose(1, 0, 2)
    mids = np.concatenate(two_parts(mid.reshape(128, 512)), axis=1)
    rows_c = np.broadcast_to(h.transpose(0, 2, 1).reshape(16, 8)[:, :, None], (16, 8, 128))
    rows_p = np.broadcast_to(h.reshape(16, 8)[:, :, None], (16, 8, 128))
    return dict(
        comp=comp,
        prol=prol,
        contrib=contrib,
        single=single,
        mids=mids,
        rows_c=np.ascontiguousarray(rows_c).astype(np.float32),
        rows_p=np.ascontiguousarray(rows_p).astype(np.float32),
    )


@functools.cache
def select_tables():
    out = np.arange(256) // TERMS
    term = np.arange(256) % TERMS
    col = np.arange(256)
    group = term[:, None] % 4 == (col // PLANE)[None, :]
    left = group & (out[:, None] == (col // 8 % 8)[None, :])
    right = group & (out[:, None] == (col % 8)[None, :])
    turn = (term[None, :] == (col // 8)[:, None]) & (out[None, :] == (col % 8)[:, None])
    return np.concatenate([left, right, turn], axis=1).astype(ml_dtypes.bfloat16)


def split(value):
    high = value.astype(BF16)
    return high, (value - high.astype(F32)).astype(BF16)


def dot(left, right):
    return jnp.dot(left, right, preferred_element_type=F32)


def fine_dot(value, table):
    rows = value.shape[0]
    width = table.shape[1] // 2
    if rows % 16 == 0:
        result = dot(jnp.concatenate(split(value), axis=0), table)
    else:
        high = value.astype(BF16).astype(F32)
        result = dot(jnp.concatenate([high, value - high], axis=0).astype(BF16), table)
    return result[:rows, :width] + result[rows:, :width] + result[:rows, width:]


def low_lanes(shape):
    return lax.broadcasted_iota(jnp.int32, shape, len(shape) - 1) < PLANE


def turned(value):
    return pltpu.roll(value, PLANE, value.ndim - 1)


def row_mix(tables, tile):
    total = None
    for p in range(8):
        term = tables[p] * tile[p : p + 1, :]
        total = term if total is None else total + term
    return total


def two_row_mixes(rows_ref, tile, width):
    return [
        row_mix([rows_ref[i * 8 + p, :, :width] for p in range(8)], tile) for i in range(2)
    ]


def fetches(sems, *pairs):
    copies = [
        pltpu.make_async_copy(there, here, sems.at[at]) for at, (there, here) in enumerate(pairs)
    ]
    for copy in copies:
        copy.start()
    return copies


def local_cell(device, own):
    step_x = (device >> 6) - (own >> 6) + 1
    step_y = ((device >> 3) & 7) - ((own >> 3) & 7) + 1
    step_z = (device & 7) - (own & 7) + 1
    return step_x * 9 + step_y * 3 + step_z


def tables_kernel(
    factors_h, weights_h, select_h, sheet,
    ab_ref, x_ref, tiles,
    factors, weights, select, sems,
):
    copies = fetches(sems, (factors_h, factors), (weights_h, weights), (select_h, select))
    spread_cells(sheet, tiles, 0)
    for copy in copies:
        copy.wait()
    lane = lax.broadcasted_iota(jnp.int32, (24, 256), 1)
    quad_of = (lane & 31) >> 2
    weight = jnp.concatenate([weights[...]] * 8, axis=1)
    weighted, plain = [], []
    for level in range(3):
        rows = []
        for e in range(3):
            rows.append(
                jnp.concatenate(
                    [factors[level, e * 64 + b * 8 : e * 64 + b * 8 + 8, :] for b in range(8)],
                    axis=1,
                )
            )
        values = jnp.concatenate(rows, axis=0)
        scaled = values * weight
        for quad in range(QUADS):
            weighted.append(jnp.where(quad_of == quad, scaled, 0.0))
            plain.append(jnp.where(quad_of == quad, values, 0.0))
        x_ref[level] = lax.dot_general(
            select[:, 512:768],
            values.astype(BF16),
            (((1,), (1,)), ((), ())),
            preferred_element_type=F32,
        ).astype(BF16)
    for which, parts in enumerate((weighted, plain)):
        both = dot(
            jnp.concatenate(split(jnp.concatenate(parts, axis=0)), axis=0),
            select[:, which * 256 : which * 256 + 256],
        )
        ab_ref[which] = (both[:576] + both[576:]).reshape(24, 24, 256)


def build_w(ab_ref, level, w_ref):
    def one_quad(quad, carry):
        at = level * QUADS + quad
        inner = [ab_ref[1, at, ez * 8 : ez * 8 + 8, :] for ez in range(3)]
        for ey in range(3):
            for pair in range(4):
                row = ey * 8 + 2 * pair
                first = ab_ref[0, at, row : row + 1, :]
                second = ab_ref[0, at, row + 1 : row + 2, :]
                for ez in range(3):
                    tile = jnp.concatenate([first * inner[ez], second * inner[ez]], axis=0)
                    e = ey * 3 + ez
                    to = quad * 512 + e * PLANE if e < 8 else 4096 + quad * PLANE
                    to = pl.multiple_of(to + pair * 16, 16)
                    w_ref[pl.ds(to, 16), :] = tile.astype(BF16)
        return carry

    lax.fori_loop(0, QUADS, one_quad, 0)


def spread_cells(sheet, tiles, at):
    low = low_lanes((8, 128))
    values = sheet[...].astype(F32)
    for cell in range(9):
        to = (at + cell) * 10
        for pair in range(5):
            row = cell * CELL + pair * 8
            tile = values[row : row + 8, :]
            other = turned(tile)
            tiles[to + 2 * pair] = jnp.where(low, tile, other)
            tiles[to + 2 * pair + 1] = tile if pair == 4 else jnp.where(low, other, tile)


def diagonal_sum(result, rows):
    total = None
    for term in range(4):
        piece = result[term * rows : (term + 1) * rows, term * PLANE : (term + 1) * PLANE]
        total = piece if total is None else total + piece
    return total


def apply_one(sources, x_table, w_ref):
    product = dot(x_table, sources)
    low = low_lanes((32, 128))
    groups = [product[quad * 32 : quad * 32 + 32, :] for quad in range(QUADS)]
    pieces = [group[:, :512].astype(BF16) for group in groups]
    for quad in range(0, QUADS, 2):
        both = jnp.where(low, groups[quad][:, 512:], groups[quad + 1][:, 512:])
        pieces.append(both.astype(BF16))
    result = dot(jnp.concatenate(pieces, axis=1), w_ref[...])
    return diagonal_sum(result, 8)


def first_kernel(
    parent, refined, child_h, fine_h, mid_h, coarse_h, coef_h, leaf_h, filters_h, rows_h,
    halo, payload, numbers,
    child, child_v, fine_nbr, mid_nbr, coarse_nbr, coef, leaf, filters, rows,
    source, detail, sems, payload_v, payload_sem,
):
    copies = fetches(
        sems,
        (child_h, child),
        (coef_h, coef),
        (filters_h, filters),
        (rows_h, rows),
        (leaf_h, leaf),
        (child_h, child_v),
        (fine_h, fine_nbr),
        (mid_h, mid_nbr),
        (coarse_h, coarse_nbr),
    )
    for copy in copies[:5]:
        copy.wait()
    comp = filters[0:256, :]
    prol = jnp.concatenate([filters[256 + 64 * k : 320 + 64 * k, :] for k in range(4)], axis=1)
    slot = parent[0] >> 3
    octant = parent[0] & 7

    values = coef[...].astype(F32)
    for a in range(8):
        source[:, a, :] = values[:, a * PLANE : (a + 1) * PLANE]
    tiles = [source[child[0, o]] for o in range(8)]
    lhs = jnp.concatenate(
        [jnp.concatenate(tiles[0:4], axis=1), jnp.concatenate(tiles[4:8], axis=1)], axis=0
    ).astype(BF16)
    both = dot(lhs, comp)
    partial = both[:, :PLANE] + both[:, PLANE:]
    compressed = None
    for k in range(16):
        term = rows[k, :, :PLANE] * partial[k : k + 1, :]
        compressed = term if compressed is None else compressed + term
    leaf_row = leaf[...].astype(F32)
    leaf_tile = jnp.concatenate(
        [leaf_row[:, a * PLANE : (a + 1) * PLANE] for a in range(8)], axis=0
    )
    middle = jnp.where(refined[0] > 0, compressed, leaf_tile).astype(BF16).astype(F32)

    row_at = (octant >> 2) * 8
    inner = row_mix([rows[row_at + x, :, :PLANE] for x in range(8)], middle)
    table = filters[pl.ds(pl.multiple_of(512 + (octant & 3) * 64, 64), 64), :]
    added = fine_dot(inner, table)
    low8 = low_lanes((8, 128))
    tag = jnp.full((8, 128), slot, jnp.int32).astype(F32)
    tile = jnp.where(low8, jnp.concatenate([added, added], axis=1), tag).astype(BF16)
    payload_v[...] = jnp.broadcast_to(tile[None], payload_v.shape)
    send = pltpu.make_async_copy(payload_v, payload, payload_sem)
    send.start()

    live = jnp.full((8, PLANE), refined[0], jnp.int32).astype(F32)
    upper = jnp.concatenate(two_row_mixes(rows.at[16:32], middle, PLANE), axis=0)
    spread = fine_dot(upper, prol)
    for o in range(8):
        i, jl = o // 4, o % 4
        part = spread[i * 8 : i * 8 + 8, jl * PLANE : (jl + 1) * PLANE]
        detail[child[0, o]] = live * (tiles[o] - part)
    lane = lax.broadcasted_iota(jnp.int32, (8, 128), 1)
    name = jnp.where(lane < 96, tag, jnp.full((8, 128), octant, jnp.int32).astype(F32))
    pairs = [jnp.concatenate([detail[2 * k], detail[2 * k + 1]], axis=1) for k in range(4)]
    pairs.append(jnp.where(low8, jnp.concatenate([middle, middle], axis=1), name))
    halo[...] = jnp.concatenate(pairs, axis=0).astype(BF16)

    for copy in copies[5:]:
        copy.wait()
    near = fine_nbr[...]
    own = near[:, 13:14] >> 3
    cell = local_cell(near >> 3, own) * 10 + (near & 7)
    numbers[0:8, 0:27] = jnp.where(near >= 0, cell, GONE)
    near_mid = mid_nbr[...]
    own_mid = near_mid[:, 13:14]
    numbers[8:9, 0:27] = jnp.where(near_mid >= 0, local_cell(near_mid, own_mid), 27)
    numbers[8:9, 27:28] = jnp.full((1, 1), 27, jnp.int32)
    hot = jnp.where(lax.broadcasted_iota(jnp.int32, (8, 64), 1) == slot, 1.0, 0.0).astype(BF16)
    near_coarse = lax.dot_general(
        hot,
        coarse_nbr[...].astype(F32).astype(BF16),
        (((1,), (1,)), ((), ())),
        preferred_element_type=F32,
    )[0:1].astype(jnp.int32)
    numbers[9:10, 0:27] = jnp.where(near_coarse >= 0, near_coarse, 64)
    numbers[9:10, 27:28] = jnp.full((1, 1), 64, jnp.int32)
    numbers[10:11, 0:8] = child_v[...]
    numbers[10:11, 8:9] = jnp.full((1, 1), parent[0], jnp.int32)
    numbers[10:11, 9:10] = jnp.full((1, 1), refined[0], jnp.int32)
    send.wait()


def plane_kernel(arrived, copies, partial, sems):
    rows = arrived[...].astype(F32).reshape(512, 128)
    other = turned(rows)
    low = low_lanes((512, 128))
    value = jnp.where(low, rows, other)
    tag = jnp.where(low, other, rows)
    half = jnp.where(low, 0, 1)
    rhs = jnp.where((tag.astype(jnp.int32) & 1) == half, value, 0.0).astype(BF16)
    pick = jnp.where(lax.broadcasted_iota(jnp.int32, (8, 128), 1) == 0, 1.0, 0.0).astype(BF16)
    along = lax.dot_general(
        pick, tag.astype(BF16), (((1,), (1,)), ((), ())), preferred_element_type=F32
    ).astype(jnp.int32)
    p_of = lax.broadcasted_iota(jnp.int32, (8, 512), 1) & 7
    key = jnp.where(p_of == lax.broadcasted_iota(jnp.int32, (8, 512), 0), along >> 1, -1)
    hot = jnp.concatenate(
        [jnp.where(key == c2, 1.0, 0.0) for c2 in range(32)], axis=0
    ).astype(BF16)
    partial[...] = dot(hot, rhs).astype(BF16)
    for copy in fetches(sems, *((partial, copies.at[at]) for at in range(8))):
        copy.wait()


def pair_of(first, second):
    return jnp.where(low_lanes((8, 128)), first, second)


def fine_kernel(
    numbers_h, left, centre, right, ab_ref, x_ref,
    direct, mid_tiles, names_ref,
    table, mixed, w_ref, numbers, sems,
):
    copies = fetches(sems, (numbers_h, numbers))
    build_w(ab_ref, 0, w_ref)
    lanes = lax.broadcasted_iota(jnp.int32, (1, 128), 1)
    low8 = low_lanes((8, 128))
    table[GONE] = jnp.zeros((8, 128), F32)
    table[GONE + 8] = jnp.zeros((8, 128), F32)
    spread_cells(left, table, 0)
    spread_cells(right, table, 18)
    for at in range(90):
        table[90 + at] = centre[at]
    names = jnp.full((1, 128), 512, jnp.int32)
    for cell in range(27):
        meta = table[cell * 10 + 9, 0:1, :]
        name = meta * 8.0 + pltpu.roll(meta, 96, 1)
        names = jnp.where(lanes == PLANE + cell, name.astype(jnp.int32), names)
    names_ref[...] = names
    for cell in range(28):
        mid_tiles[cell] = table[cell * 10 + 8]

    for copy in copies:
        copy.wait()

    def source(t, ex, e):
        return table[numbers[t, ex * 9 + e]]

    for pair in range(4):
        pieces = []
        for t in (2 * pair, 2 * pair + 1):
            for ep in range(5):
                pieces.append(
                    jnp.concatenate(
                        [
                            pair_of(source(t, ex, 2 * ep), source(t, ex, min(2 * ep + 1, 8)))
                            for ex in range(3)
                        ],
                        axis=0,
                    ).astype(BF16)
                )
        product = dot(x_ref[0], jnp.concatenate(pieces, axis=1))
        for term in range(4):
            row = term * PLANE + pair * 16
            last = None
            for quad in range(QUADS):
                at = (quad * 4 + term) * 8
                tile = jnp.concatenate(
                    [product[at : at + 8, :512], product[at : at + 8, 640:1152]], axis=0
                )
                mixed[row : row + 16, quad * 512 : quad * 512 + 512] = tile.astype(BF16)
                tile = jnp.concatenate(
                    [product[at : at + 8, 512:640], product[at : at + 8, 1152:1280]], axis=0
                )
                if quad % 2 == 0:
                    last = tile
                else:
                    to = 4096 + quad // 2 * 128
                    tile = jnp.where(low_lanes((16, 128)), last, tile)
                    mixed[row : row + 16, to : to + 128] = tile.astype(BF16)
    result = None
    for half in range(2):
        total = None
        own = slice(half * 128, half * 128 + 128)
        for part in range(9):
            some = slice(part * 512, part * 512 + 512)
            term = dot(mixed[own, some], w_ref[some, own])
            total = term if total is None else total + term
        for term in range(2):
            rows = slice(term * PLANE, term * PLANE + PLANE)
            result = total[rows, rows] if result is None else result + total[rows, rows]
    direct[...] = result.reshape(8, 8, PLANE)


def last_kernel(
    numbers_h, names_h, planes, mid_tiles, direct, ab_ref, x_ref, rows_h, filters_h, mids_h,
    fine_out, mid_out,
    coarse, back, rows_p, filters, mids, sems, w_mid, w_coarse, numbers, names,
):
    copies = fetches(
        sems,
        (numbers_h, numbers),
        (names_h, names),
        (rows_h, rows_p),
        (filters_h, filters),
        (mids_h, mids),
    )
    build_w(ab_ref, 1, w_mid)
    build_w(ab_ref, 2, w_coarse)
    low8 = low_lanes((8, 128))

    total = None
    for plane in range(8):
        term = planes[plane].astype(F32)
        total = term if total is None else total + term
    for c2 in range(32):
        tile = total[c2 * 8 : c2 * 8 + 8, :]
        other = turned(tile)
        coarse[2 * c2] = jnp.where(low8, tile, other)
        coarse[2 * c2 + 1] = jnp.where(low8, other, tile)
    coarse[64] = jnp.zeros((8, 128), F32)
    for copy in copies:
        copy.wait()
    octant = numbers[10, 8] & 7

    def coarse_source(ex, e):
        return coarse[numbers[9, ex * 9 + e]]

    sources = jnp.concatenate(
        [
            jnp.concatenate(
                [
                    pair_of(coarse_source(ex, 2 * ep), coarse_source(ex, min(2 * ep + 1, 8)))
                    for ex in range(3)
                ],
                axis=0,
            ).astype(BF16)
            for ep in range(5)
        ],
        axis=1,
    )
    coarse_result = apply_one(sources, x_ref[2], w_coarse)

    uppers, octants, owns = [], [], []
    for ep in range(5):
        for ex in range(3):
            first = numbers[8, ex * 9 + 2 * ep]
            second = numbers[8, ex * 9 + min(2 * ep + 1, 8)]
            name_1, name_2 = names[0, PLANE + first], names[0, PLANE + second]
            owns.append(pair_of(mid_tiles[first], mid_tiles[second]))
            both = pair_of(coarse[name_1 >> 3], coarse[name_2 >> 3])
            named = jnp.where(low8, name_1 & 7, name_2 & 7)
            octants.append(named)
            mix_0, mix_1 = two_row_mixes(rows_p, both, 128)
            uppers.append(jnp.where(named >= 4, mix_1, mix_0))
    stacked = jnp.concatenate(uppers, axis=0)
    high = stacked.astype(BF16).astype(F32)
    spread = dot(jnp.concatenate([high, stacked - high], axis=0).astype(BF16), mids[...])
    spread = spread[:120, :512] + spread[120:, :512] + spread[:120, 512:]
    pieces = []
    for ep in range(5):
        tiles = []
        for ex in range(3):
            at = ep * 3 + ex
            which = octants[at] & 3
            chosen = spread[at * 8 : at * 8 + 8, 0:128]
            for jl in range(1, 4):
                chosen = jnp.where(
                    which == jl, spread[at * 8 : at * 8 + 8, jl * 128 : jl * 128 + 128], chosen
                )
            tiles.append(owns[at] - chosen)
        pieces.append(jnp.concatenate(tiles, axis=0).astype(BF16))
    mid_result = apply_one(jnp.concatenate(pieces, axis=1), x_ref[1], w_mid)

    row_at = (octant >> 2) * 8
    upper = row_mix([rows_p[row_at + p, :, :PLANE] for p in range(8)], coarse_result)
    single = filters[pl.ds(pl.multiple_of(256 + (octant & 3) * 64, 64), 64), :]
    middle = mid_result + fine_dot(upper, single)
    for a in range(8):
        mid_out[:, a * PLANE : (a + 1) * PLANE] = middle[a : a + 1, :]
    live = jnp.full((8, PLANE), numbers[10, 9], jnp.int32).astype(F32)
    upper = jnp.concatenate(two_row_mixes(rows_p, middle, PLANE), axis=0)
    prol = jnp.concatenate([filters[64 * k : 64 * k + 64, :] for k in range(4)], axis=1)
    spread = fine_dot(upper, prol)
    for o in range(8):
        i, jl = o // 4, o % 4
        slot = numbers[10, o]
        part = spread[i * 8 : i * 8 + 8, jl * PLANE : (jl + 1) * PLANE]
        back[slot] = live * (direct[slot] + part)
    for a in range(8):
        fine_out[:, a * PLANE : (a + 1) * PLANE] = back[:, a, :]


def call(kernel, kinds, outs, scratch, flops, *args):
    any_space = pl.BlockSpec(memory_space=pl.ANY)
    vmem = pl.BlockSpec(memory_space=pltpu.VMEM)
    specs = dict(s=pl.BlockSpec(memory_space=pltpu.SMEM), v=vmem, w=vmem, h=any_space, a=any_space)
    moved = sum(math.prod(x.shape) * x.dtype.itemsize for x in (*args, *outs))
    spaces = dict(w=pltpu.VMEM, h=pltpu.HBM)
    args = [
        pltpu.with_memory_space_constraint(x, spaces[kind]) if kind in spaces else x
        for kind, x in zip(kinds, args, strict=True)
    ]
    return pl.pallas_call(
        kernel,
        out_shape=outs,
        in_specs=[specs[kind] for kind in kinds],
        out_specs=[any_space if getattr(x, "memory_space", None) == pltpu.HBM else vmem for x in outs],
        scratch_shapes=scratch,
        compiler_params=pltpu.CompilerParams(vmem_limit_bytes=VMEM_LIMIT),
        cost_estimate=pl.CostEstimate(flops=flops, bytes_accessed=moved, transcendentals=0),
        name=kernel.__name__,
    )(*args)


def both_ways(x, axis):
    count = lax.axis_size(axis)
    ends = count - 1
    before = lax.ppermute(x, axis, [(i, i + 1) for i in range(ends)])
    after = lax.ppermute(x, axis, [(i + 1, i) for i in range(ends)])
    return before, after


def shards(
    fine_coef, mid_leaf, mid_child, mid_parent, mid_refined,
    fine_nbr, mid_nbr, coarse_nbr, op_factor, term_weight,
):
    tables = filter_tables()
    select = jnp.asarray(select_tables())
    prol_rows = np.concatenate(np.split(tables["prol"], 4, axis=1), axis=0)
    single_rows = tables["single"].reshape(256, 128)
    first_filters = jnp.asarray(
        np.concatenate([tables["comp"], prol_rows, tables["contrib"].reshape(256, 128)])
    )
    last_filters = jnp.asarray(np.concatenate([prol_rows, single_rows]))
    rows_both = jnp.asarray(np.concatenate([tables["rows_c"], tables["rows_p"]]))
    rows_p = jnp.asarray(tables["rows_p"])
    mids = jnp.asarray(tables["mids"])
    factors = op_factor.transpose(0, 2, 3, 4, 1).reshape(3, 192, TERMS)

    sds = jax.ShapeDtypeStruct
    vmem, smem = pltpu.VMEM, pltpu.SMEM
    i32 = jnp.int32
    halo, payload, numbers = call(
        first_kernel,
        "sshhhhhhhh",
        [sds((CELL, 128), BF16), pltpu.HBM((64, 8, 128), BF16), sds((16, 128), i32)],
        [
            smem((1, 8), i32),
            vmem((1, 8), i32),
            vmem((8, 27), i32),
            vmem((1, 27), i32),
            vmem((27, 64), i32),
            vmem((8, 512), BF16),
            vmem((1, 512), BF16),
            vmem((768, 128), BF16),
            vmem((32, 8, 128), F32),
            vmem((8, 8, PLANE), F32),
            vmem((8, 8, PLANE), F32),
            pltpu.SemaphoreType.DMA((9,)),
            vmem((64, 8, 128), BF16),
            pltpu.SemaphoreType.DMA,
        ],
        2_000_000,
        mid_parent, mid_refined, mid_child, fine_nbr, mid_nbr, coarse_nbr.T, fine_coef, mid_leaf,
        first_filters, rows_both,
    )
    arrived = lax.all_to_all(payload, ("gy", "gz"), 0, 0, tiled=True)
    before, after = both_ways(halo, "gz")
    line = jnp.concatenate([before, halo, after], axis=0)
    before, after = both_ways(line, "gy")
    sheet = jnp.concatenate([before, line, after], axis=0)
    before, after = both_ways(sheet, "gx")

    (copies,) = call(
        plane_kernel, "v", [pltpu.HBM((8, 256, 128), BF16)],
        [vmem((256, 128), BF16), pltpu.SemaphoreType.DMA((8,))], 33_000_000, arrived
    )
    planes = lax.all_to_all(copies, "gx", 0, 0, tiled=True)

    w_factors, x_tables, centre = call(
        tables_kernel,
        "hhhv",
        [
            pltpu.VMEM((2, 3 * QUADS, 24, 256), F32),
            pltpu.VMEM((3, 256, 24), BF16),
            pltpu.VMEM((90, 8, 128), F32),
        ],
        [
            vmem((3, 192, TERMS), F32),
            vmem((1, TERMS), F32),
            vmem((256, 768), BF16),
            pltpu.SemaphoreType.DMA((3,)),
        ],
        600_000_000,
        factors, term_weight.reshape(1, TERMS), select, sheet,
    )
    direct, mid_tiles, names = call(
        fine_kernel,
        "avvvww",
        [sds((8, 8, PLANE), F32), sds((28, 8, 128), F32), sds((1, 128), i32)],
        [
            vmem((GONE + 9, 8, 128), F32),
            vmem((256, ROWS_W), BF16),
            vmem((ROWS_W, 256), BF16),
            smem((16, 128), i32),
            pltpu.SemaphoreType.DMA((1,)),
        ],
        100_000_000,
        numbers, before, centre, after, w_factors, x_tables,
    )
    fine_out, mid_out = call(
        last_kernel,
        "aavvvwwhhh",
        [sds((8, 512), F32), sds((1, 512), F32)],
        [
            vmem((65, 8, 128), F32),
            vmem((8, 8, PLANE), F32),
            vmem((16, 8, 128), F32),
            vmem((512, 128), BF16),
            vmem((128, 1024), BF16),
            pltpu.SemaphoreType.DMA((5,)),
            vmem((ROWS_W, 256), BF16),
            vmem((ROWS_W, 256), BF16),
            smem((16, 128), i32),
            smem((1, 128), i32),
        ],
        200_000_000,
        numbers, names, planes, mid_tiles, direct, w_factors, x_tables,
        rows_p, last_filters, mids,
    )
    return fine_out, mid_out


def solution(mesh):
    cells = ("gx", "gy", "gz")
    rows = P(cells, None)
    return jax.shard_map(
        shards,
        mesh=mesh,
        in_specs=(rows, rows, rows, P(cells), P(cells), rows, rows, P(), P(), P()),
        out_specs=(rows, rows),
        check_vma=False,
    )
```

```python
import functools
import math

import jax
import jax.numpy as jnp
import ml_dtypes
import numpy as np
from jax import lax
from jax.experimental import pallas as pl
from jax.experimental.pallas import tpu as pltpu
from jax.sharding import PartitionSpec as P

K = 8
PLANE = 64
TERMS = 32
QUADS = 8
ROWS_W = 4608
CELL = 40
GONE = 27 * 10
BF16 = jnp.bfloat16
F32 = jnp.float32
VMEM_LIMIT = 32 * 1024 * 1024


def poly_multiply(left, right):
    result = [0.0] * (len(left) + len(right) - 1)
    for first, left_coef in enumerate(left):
        for second, right_coef in enumerate(right):
            result[first + second] += left_coef * right_coef
    return result


def poly_compose(coeffs, factor, offset):
    result = [0.0]
    power_term = [1.0]
    for coef in coeffs:
        padded = result + [0.0] * (len(power_term) - len(result))
        result = [padded[place] + coef * power_term[place] for place in range(len(power_term))]
        power_term = poly_multiply(power_term, [offset, factor])
    return result


def legendre_table(basis_order):
    polys = [[1.0], [0.0, 1.0]]
    for degree in range(1, basis_order):
        upper = [0.0] + [(2 * degree + 1) * coef for coef in polys[degree]]
        lower = [degree * coef for coef in polys[degree - 1]] + [0.0] * (
            len(upper) - len(polys[degree - 1])
        )
        polys.append([(upper[place] - lower[place]) / (degree + 1) for place in range(len(upper))])
    return [
        [math.sqrt(2 * degree + 1) * coef for coef in poly_compose(polys[degree], 2.0, -1.0)]
        for degree in range(basis_order)
    ]


@functools.cache
def two_scale(basis_order):
    shifted = legendre_table(basis_order)
    filters = np.zeros((2, basis_order, basis_order))
    for which_half in range(2):
        for row_at in range(basis_order):
            halved = poly_compose(shifted[row_at], 0.5, 0.5 * which_half)
            for col_at in range(basis_order):
                product = poly_multiply(halved, shifted[col_at])
                total = sum((coef / (place + 1) for place, coef in enumerate(product)))
                filters[which_half, row_at, col_at] = total / math.sqrt(2.0)
    return filters.astype(np.float32).astype(np.float64)


def two_parts(matrix):
    high = matrix.astype(ml_dtypes.bfloat16)
    low = (matrix - high.astype(np.float64)).astype(ml_dtypes.bfloat16)
    return high, low


@functools.cache
def filter_tables():
    h = two_scale(K)
    pair = np.einsum("jqy,lrz->jlqryz", h, h).reshape(4, PLANE, PLANE)
    to_coarse = pair.transpose(0, 2, 1).reshape(4 * PLANE, PLANE)
    comp = np.concatenate(two_parts(to_coarse), axis=1)
    to_fine = pair.transpose(1, 0, 2).reshape(PLANE, 4 * PLANE)
    prol = np.concatenate(two_parts(to_fine), axis=1)
    contrib = np.stack([np.concatenate(two_parts(pair[k].T), axis=1) for k in range(4)])
    single = np.stack([np.concatenate(two_parts(pair[k]), axis=1) for k in range(4)])
    mid = np.zeros((2, PLANE, 4, 2, PLANE))
    for half in range(2):
        mid[half, :, :, half, :] = pair.transpose(1, 0, 2)
    mids = np.concatenate(two_parts(mid.reshape(128, 512)), axis=1)
    rows_c = np.broadcast_to(h.transpose(0, 2, 1).reshape(16, 8)[:, :, None], (16, 8, 128))
    rows_p = np.broadcast_to(h.reshape(16, 8)[:, :, None], (16, 8, 128))
    return dict(
        comp=comp,
        prol=prol,
        contrib=contrib,
        single=single,
        mids=mids,
        rows_c=np.ascontiguousarray(rows_c).astype(np.float32),
        rows_p=np.ascontiguousarray(rows_p).astype(np.float32),
    )


@functools.cache
def select_tables():
    out = np.arange(256) // TERMS
    term = np.arange(256) % TERMS
    col = np.arange(256)
    group = term[:, None] % 4 == (col // PLANE)[None, :]
    left = group & (out[:, None] == (col // 8 % 8)[None, :])
    right = group & (out[:, None] == (col % 8)[None, :])
    turn = (term[None, :] == (col // 8)[:, None]) & (out[None, :] == (col % 8)[:, None])
    return np.concatenate([left, right, turn], axis=1).astype(ml_dtypes.bfloat16)


def split(value):
    high = value.astype(BF16)
    return high, (value - high.astype(F32)).astype(BF16)


def dot(left, right):
    return jnp.dot(left, right, preferred_element_type=F32)


def fine_dot(value, table):
    rows = value.shape[0]
    width = table.shape[1] // 2
    if rows % 16 == 0:
        result = dot(jnp.concatenate(split(value), axis=0), table)
    else:
        high = value.astype(BF16).astype(F32)
        result = dot(jnp.concatenate([high, value - high], axis=0).astype(BF16), table)
    return result[:rows, :width] + result[rows:, :width] + result[:rows, width:]


def low_lanes(shape):
    return lax.broadcasted_iota(jnp.int32, shape, len(shape) - 1) < PLANE


def turned(value):
    return pltpu.roll(value, PLANE, value.ndim - 1)


def row_mix(tables, tile):
    total = None
    for p in range(8):
        term = tables[p] * tile[p : p + 1, :]
        total = term if total is None else total + term
    return total


def two_row_mixes(rows_ref, tile, width):
    return [
        row_mix([rows_ref[i * 8 + p, :, :width] for p in range(8)], tile) for i in range(2)
    ]


def fetches(sems, *pairs):
    copies = [
        pltpu.make_async_copy(there, here, sems.at[at]) for at, (there, here) in enumerate(pairs)
    ]
    for copy in copies:
        copy.start()
    return copies


def local_cell(device, own):
    step_x = (device >> 6) - (own >> 6) + 1
    step_y = ((device >> 3) & 7) - ((own >> 3) & 7) + 1
    step_z = (device & 7) - (own & 7) + 1
    return step_x * 9 + step_y * 3 + step_z


def tables_kernel(
    factors_h, weights_h, select_h, sheet, rows_h, filters_h, mids_h,
    ab_ref, x_ref, tiles, rows_p, filters, mids,
    factors, weights, select, sems,
):
    copies = fetches(
        sems,
        (factors_h, factors),
        (weights_h, weights),
        (select_h, select),
        (mids_h, mids),
        (filters_h, filters),
        (rows_h, rows_p),
    )
    spread_cells(sheet, tiles, 0)
    for copy in copies[:3]:
        copy.wait()
    lane = lax.broadcasted_iota(jnp.int32, (24, 256), 1)
    quad_of = (lane & 31) >> 2
    weight = jnp.concatenate([weights[...]] * 8, axis=1)
    weighted, plain = [], []
    for level in range(3):
        rows = []
        for e in range(3):
            rows.append(
                jnp.concatenate(
                    [factors[level, e * 64 + b * 8 : e * 64 + b * 8 + 8, :] for b in range(8)],
                    axis=1,
                )
            )
        values = jnp.concatenate(rows, axis=0)
        scaled = values * weight
        for quad in range(QUADS):
            weighted.append(jnp.where(quad_of == quad, scaled, 0.0))
            plain.append(jnp.where(quad_of == quad, values, 0.0))
        x_ref[level] = lax.dot_general(
            select[:, 512:768],
            values.astype(BF16),
            (((1,), (1,)), ((), ())),
            preferred_element_type=F32,
        ).astype(BF16)
    for which, parts in enumerate((weighted, plain)):
        both = dot(
            jnp.concatenate(split(jnp.concatenate(parts, axis=0)), axis=0),
            select[:, which * 256 : which * 256 + 256],
        )
        ab_ref[which] = (both[:576] + both[576:]).reshape(24, 24, 256)
    for copy in copies[3:]:
        copy.wait()


def build_w(ab_ref, level, w_ref):
    def one_quad(quad):
        at = level * QUADS + quad
        inner = [ab_ref[1, at, ez * 8 : ez * 8 + 8, :] for ez in range(3)]
        for ey in range(3):
            for pair in range(4):
                row = ey * 8 + 2 * pair
                first = ab_ref[0, at, row : row + 1, :]
                second = ab_ref[0, at, row + 1 : row + 2, :]
                for ez in range(3):
                    tile = jnp.concatenate([first * inner[ez], second * inner[ez]], axis=0)
                    e = ey * 3 + ez
                    to = quad * 512 + e * PLANE if e < 8 else 4096 + quad * PLANE
                    to += pair * 16
                    w_ref[to : to + 16, :] = tile.astype(BF16)

    for quad in range(QUADS):
        one_quad(quad)


def spread_cells(sheet, tiles, at):
    low = low_lanes((8, 128))
    values = sheet[...].astype(F32)
    for cell in range(9):
        to = (at + cell) * 10
        for pair in range(5):
            row = cell * CELL + pair * 8
            tile = values[row : row + 8, :]
            other = turned(tile)
            tiles[to + 2 * pair] = jnp.where(low, tile, other)
            tiles[to + 2 * pair + 1] = tile if pair == 4 else jnp.where(low, other, tile)


def diagonal_sum(result, rows):
    total = None
    for term in range(4):
        piece = result[term * rows : (term + 1) * rows, term * PLANE : (term + 1) * PLANE]
        total = piece if total is None else total + piece
    return total


def apply_one(sources, x_table, w_ref):
    product = dot(x_table, sources)
    low = low_lanes((32, 128))
    groups = [product[quad * 32 : quad * 32 + 32, :] for quad in range(QUADS)]
    pieces = [group[:, :512].astype(BF16) for group in groups]
    for quad in range(0, QUADS, 2):
        both = jnp.where(low, groups[quad][:, 512:], groups[quad + 1][:, 512:])
        pieces.append(both.astype(BF16))
    result = dot(jnp.concatenate(pieces, axis=1), w_ref[...])
    return diagonal_sum(result, 8)


def first_kernel(
    parent, refined, child_h, fine_h, mid_h, coarse_h, coef_h, leaf_h, filters_h, rows_h,
    halo, payload, numbers,
    child, child_v, fine_nbr, mid_nbr, coarse_nbr, coef, leaf, filters, rows,
    source, detail, sems, payload_v, payload_sem,
):
    copies = fetches(
        sems,
        (child_h, child),
        (coef_h, coef),
        (filters_h, filters),
        (rows_h, rows),
        (leaf_h, leaf),
        (child_h, child_v),
        (fine_h, fine_nbr),
        (mid_h, mid_nbr),
        (coarse_h, coarse_nbr),
    )
    for copy in copies[:5]:
        copy.wait()
    comp = filters[0:256, :]
    prol = jnp.concatenate([filters[256 + 64 * k : 320 + 64 * k, :] for k in range(4)], axis=1)
    slot = parent[0] >> 3
    octant = parent[0] & 7

    values = coef[...].astype(F32)
    for a in range(8):
        source[:, a, :] = values[:, a * PLANE : (a + 1) * PLANE]
    tiles = [source[child[0, o]] for o in range(8)]
    lhs = jnp.concatenate(
        [jnp.concatenate(tiles[0:4], axis=1), jnp.concatenate(tiles[4:8], axis=1)], axis=0
    ).astype(BF16)
    both = dot(lhs, comp)
    partial = both[:, :PLANE] + both[:, PLANE:]
    compressed = None
    for k in range(16):
        term = rows[k, :, :PLANE] * partial[k : k + 1, :]
        compressed = term if compressed is None else compressed + term
    leaf_row = leaf[...].astype(F32)
    leaf_tile = jnp.concatenate(
        [leaf_row[:, a * PLANE : (a + 1) * PLANE] for a in range(8)], axis=0
    )
    middle = jnp.where(refined[0] > 0, compressed, leaf_tile).astype(BF16).astype(F32)

    row_at = (octant >> 2) * 8
    inner = row_mix([rows[row_at + x, :, :PLANE] for x in range(8)], middle)
    table = filters[pl.ds(pl.multiple_of(512 + (octant & 3) * 64, 64), 64), :]
    added = fine_dot(inner, table)
    low8 = low_lanes((8, 128))
    tag = jnp.full((8, 128), slot, jnp.int32).astype(F32)
    tile = jnp.where(low8, jnp.concatenate([added, added], axis=1), tag).astype(BF16)
    payload_v[...] = jnp.broadcast_to(tile[None], payload_v.shape)
    send = pltpu.make_async_copy(payload_v, payload, payload_sem)
    send.start()

    live = jnp.full((8, PLANE), refined[0], jnp.int32).astype(F32)
    upper = jnp.concatenate(two_row_mixes(rows.at[16:32], middle, PLANE), axis=0)
    spread = fine_dot(upper, prol)
    for o in range(8):
        i, jl = o // 4, o % 4
        part = spread[i * 8 : i * 8 + 8, jl * PLANE : (jl + 1) * PLANE]
        detail[child[0, o]] = live * (tiles[o] - part)
    lane = lax.broadcasted_iota(jnp.int32, (8, 128), 1)
    name = jnp.where(lane < 96, tag, jnp.full((8, 128), octant, jnp.int32).astype(F32))
    pairs = [jnp.concatenate([detail[2 * k], detail[2 * k + 1]], axis=1) for k in range(4)]
    pairs.append(jnp.where(low8, jnp.concatenate([middle, middle], axis=1), name))
    halo[...] = jnp.concatenate(pairs, axis=0).astype(BF16)

    for copy in copies[5:]:
        copy.wait()
    near = fine_nbr[...]
    own = near[:, 13:14] >> 3
    cell = local_cell(near >> 3, own) * 10 + (near & 7)
    numbers[0:8, 0:27] = jnp.where(near >= 0, cell, GONE)
    near_mid = mid_nbr[...]
    own_mid = near_mid[:, 13:14]
    numbers[8:9, 0:27] = jnp.where(near_mid >= 0, local_cell(near_mid, own_mid), 27)
    numbers[8:9, 27:28] = jnp.full((1, 1), 27, jnp.int32)
    hot = jnp.where(lax.broadcasted_iota(jnp.int32, (8, 64), 1) == slot, 1.0, 0.0).astype(BF16)
    near_coarse = lax.dot_general(
        hot,
        coarse_nbr[...].astype(F32).astype(BF16),
        (((1,), (1,)), ((), ())),
        preferred_element_type=F32,
    )[0:1].astype(jnp.int32)
    numbers[9:10, 0:27] = jnp.where(near_coarse >= 0, near_coarse, 64)
    numbers[9:10, 27:28] = jnp.full((1, 1), 64, jnp.int32)
    numbers[10:11, 0:8] = child_v[...]
    numbers[10:11, 8:9] = jnp.full((1, 1), parent[0], jnp.int32)
    numbers[10:11, 9:10] = jnp.full((1, 1), refined[0], jnp.int32)
    send.wait()


def plane_kernel(arrived, copies, partial, sems):
    rows = arrived[...].astype(F32).reshape(512, 128)
    other = turned(rows)
    low = low_lanes((512, 128))
    value = jnp.where(low, rows, other)
    tag = jnp.where(low, other, rows)
    half = jnp.where(low, 0, 1)
    rhs = jnp.where((tag.astype(jnp.int32) & 1) == half, value, 0.0).astype(BF16)
    pick = jnp.where(lax.broadcasted_iota(jnp.int32, (8, 128), 1) == 0, 1.0, 0.0).astype(BF16)
    along = lax.dot_general(
        pick, tag.astype(BF16), (((1,), (1,)), ((), ())), preferred_element_type=F32
    ).astype(jnp.int32)
    p_of = lax.broadcasted_iota(jnp.int32, (8, 512), 1) & 7
    key = jnp.where(p_of == lax.broadcasted_iota(jnp.int32, (8, 512), 0), along >> 1, -1)
    hot = jnp.concatenate(
        [jnp.where(key == c2, 1.0, 0.0) for c2 in range(32)], axis=0
    ).astype(BF16)
    partial[...] = dot(hot, rhs).astype(BF16)
    for copy in fetches(sems, *((partial, copies.at[at]) for at in range(8))):
        copy.wait()


def pair_of(first, second):
    return jnp.where(low_lanes((8, 128)), first, second)


def fine_kernel(
    numbers_h, left, centre, right, ab_ref, x_ref,
    direct, mid_tiles, names_ref,
    table, mixed, w_ref, numbers, sems,
):
    copies = fetches(sems, (numbers_h, numbers))
    build_w(ab_ref, 0, w_ref)
    lanes = lax.broadcasted_iota(jnp.int32, (1, 128), 1)
    low8 = low_lanes((8, 128))
    table[GONE] = jnp.zeros((8, 128), F32)
    table[GONE + 8] = jnp.zeros((8, 128), F32)
    spread_cells(left, table, 0)
    spread_cells(right, table, 18)
    for at in range(90):
        table[90 + at] = centre[at]
    names = jnp.full((1, 128), 512, jnp.int32)
    for cell in range(27):
        meta = table[cell * 10 + 9, 0:1, :]
        name = meta * 8.0 + pltpu.roll(meta, 96, 1)
        names = jnp.where(lanes == PLANE + cell, name.astype(jnp.int32), names)
    names_ref[...] = names
    for cell in range(28):
        mid_tiles[cell] = table[cell * 10 + 8]

    for copy in copies:
        copy.wait()

    def source(t, ex, e):
        return table[numbers[t, ex * 9 + e]]

    for pair in range(4):
        pieces = []
        for t in (2 * pair, 2 * pair + 1):
            for ep in range(5):
                pieces.append(
                    jnp.concatenate(
                        [
                            pair_of(source(t, ex, 2 * ep), source(t, ex, min(2 * ep + 1, 8)))
                            for ex in range(3)
                        ],
                        axis=0,
                    ).astype(BF16)
                )
        product = dot(x_ref[0], jnp.concatenate(pieces, axis=1))
        for term in range(4):
            row = term * PLANE + pair * 16
            last = None
            for quad in range(QUADS):
                at = (quad * 4 + term) * 8
                tile = jnp.concatenate(
                    [product[at : at + 8, :512], product[at : at + 8, 640:1152]], axis=0
                )
                mixed[row : row + 16, quad * 512 : quad * 512 + 512] = tile.astype(BF16)
                tile = jnp.concatenate(
                    [product[at : at + 8, 512:640], product[at : at + 8, 1152:1280]], axis=0
                )
                if quad % 2 == 0:
                    last = tile
                else:
                    to = 4096 + quad // 2 * 128
                    tile = jnp.where(low_lanes((16, 128)), last, tile)
                    mixed[row : row + 16, to : to + 128] = tile.astype(BF16)
    result = None
    for half in range(2):
        total = None
        own = slice(half * 128, half * 128 + 128)
        for part in range(9):
            some = slice(part * 512, part * 512 + 512)
            term = dot(mixed[own, some], w_ref[some, own])
            total = term if total is None else total + term
        for term in range(2):
            rows = slice(term * PLANE, term * PLANE + PLANE)
            result = total[rows, rows] if result is None else result + total[rows, rows]
    direct[...] = result.reshape(8, 8, PLANE)


def last_kernel(
    numbers_h, names_h, planes, mid_tiles, direct, ab_ref, x_ref, rows_p, filters, mids,
    fine_out, mid_out,
    coarse, back, sems, w_mid, w_coarse, numbers, names,
):
    copies = fetches(sems, (numbers_h, numbers), (names_h, names))
    build_w(ab_ref, 1, w_mid)
    build_w(ab_ref, 2, w_coarse)
    low8 = low_lanes((8, 128))

    total = None
    for plane in range(8):
        term = planes[plane].astype(F32)
        total = term if total is None else total + term
    for c2 in range(32):
        tile = total[c2 * 8 : c2 * 8 + 8, :]
        other = turned(tile)
        coarse[2 * c2] = jnp.where(low8, tile, other)
        coarse[2 * c2 + 1] = jnp.where(low8, other, tile)
    coarse[64] = jnp.zeros((8, 128), F32)
    for copy in copies:
        copy.wait()
    octant = numbers[10, 8] & 7

    def coarse_source(ex, e):
        return coarse[numbers[9, ex * 9 + e]]

    sources = jnp.concatenate(
        [
            jnp.concatenate(
                [
                    pair_of(coarse_source(ex, 2 * ep), coarse_source(ex, min(2 * ep + 1, 8)))
                    for ex in range(3)
                ],
                axis=0,
            ).astype(BF16)
            for ep in range(5)
        ],
        axis=1,
    )
    coarse_result = apply_one(sources, x_ref[2], w_coarse)

    uppers, octants, owns = [], [], []
    for ep in range(5):
        for ex in range(3):
            first = numbers[8, ex * 9 + 2 * ep]
            second = numbers[8, ex * 9 + min(2 * ep + 1, 8)]
            name_1, name_2 = names[0, PLANE + first], names[0, PLANE + second]
            owns.append(pair_of(mid_tiles[first], mid_tiles[second]))
            both = pair_of(coarse[name_1 >> 3], coarse[name_2 >> 3])
            named = jnp.where(low8, name_1 & 7, name_2 & 7)
            octants.append(named)
            mix_0, mix_1 = two_row_mixes(rows_p, both, 128)
            uppers.append(jnp.where(named >= 4, mix_1, mix_0))
    stacked = jnp.concatenate(uppers, axis=0)
    high = stacked.astype(BF16).astype(F32)
    spread = dot(jnp.concatenate([high, stacked - high], axis=0).astype(BF16), mids[...])
    spread = spread[:120, :512] + spread[120:, :512] + spread[:120, 512:]
    pieces = []
    for ep in range(5):
        tiles = []
        for ex in range(3):
            at = ep * 3 + ex
            which = octants[at] & 3
            chosen = spread[at * 8 : at * 8 + 8, 0:128]
            for jl in range(1, 4):
                chosen = jnp.where(
                    which == jl, spread[at * 8 : at * 8 + 8, jl * 128 : jl * 128 + 128], chosen
                )
            tiles.append(owns[at] - chosen)
        pieces.append(jnp.concatenate(tiles, axis=0).astype(BF16))
    mid_result = apply_one(jnp.concatenate(pieces, axis=1), x_ref[1], w_mid)

    row_at = (octant >> 2) * 8
    upper = row_mix([rows_p[row_at + p, :, :PLANE] for p in range(8)], coarse_result)
    single = filters[pl.ds(pl.multiple_of(256 + (octant & 3) * 64, 64), 64), :]
    middle = mid_result + fine_dot(upper, single)
    for a in range(8):
        mid_out[:, a * PLANE : (a + 1) * PLANE] = middle[a : a + 1, :]
    live = jnp.full((8, PLANE), numbers[10, 9], jnp.int32).astype(F32)
    upper = jnp.concatenate(two_row_mixes(rows_p, middle, PLANE), axis=0)
    prol = jnp.concatenate([filters[64 * k : 64 * k + 64, :] for k in range(4)], axis=1)
    spread = fine_dot(upper, prol)
    for o in range(8):
        i, jl = o // 4, o % 4
        slot = numbers[10, o]
        part = spread[i * 8 : i * 8 + 8, jl * PLANE : (jl + 1) * PLANE]
        back[slot] = live * (direct[slot] + part)
    for a in range(8):
        fine_out[:, a * PLANE : (a + 1) * PLANE] = back[:, a, :]


def call(kernel, kinds, outs, scratch, flops, *args):
    any_space = pl.BlockSpec(memory_space=pl.ANY)
    vmem = pl.BlockSpec(memory_space=pltpu.VMEM)
    specs = dict(s=pl.BlockSpec(memory_space=pltpu.SMEM), v=vmem, w=vmem, h=any_space, a=any_space)
    moved = sum(math.prod(x.shape) * x.dtype.itemsize for x in (*args, *outs))
    spaces = dict(w=pltpu.VMEM, h=pltpu.HBM)
    args = [
        pltpu.with_memory_space_constraint(x, spaces[kind]) if kind in spaces else x
        for kind, x in zip(kinds, args, strict=True)
    ]
    return pl.pallas_call(
        kernel,
        out_shape=outs,
        in_specs=[specs[kind] for kind in kinds],
        out_specs=[any_space if getattr(x, "memory_space", None) == pltpu.HBM else vmem for x in outs],
        scratch_shapes=scratch,
        compiler_params=pltpu.CompilerParams(vmem_limit_bytes=VMEM_LIMIT),
        cost_estimate=pl.CostEstimate(flops=flops, bytes_accessed=moved, transcendentals=0),
        name=kernel.__name__,
    )(*args)


def both_ways(x, axis):
    count = lax.axis_size(axis)
    ends = count - 1
    before = lax.ppermute(x, axis, [(i, i + 1) for i in range(ends)])
    after = lax.ppermute(x, axis, [(i + 1, i) for i in range(ends)])
    return before, after


def shards(
    fine_coef, mid_leaf, mid_child, mid_parent, mid_refined,
    fine_nbr, mid_nbr, coarse_nbr, op_factor, term_weight,
):
    tables = filter_tables()
    select = jnp.asarray(select_tables())
    prol_rows = np.concatenate(np.split(tables["prol"], 4, axis=1), axis=0)
    single_rows = tables["single"].reshape(256, 128)
    first_filters = jnp.asarray(
        np.concatenate([tables["comp"], prol_rows, tables["contrib"].reshape(256, 128)])
    )
    last_filters = jnp.asarray(np.concatenate([prol_rows, single_rows]))
    rows_both = jnp.asarray(np.concatenate([tables["rows_c"], tables["rows_p"]]))
    rows_p = jnp.asarray(tables["rows_p"])
    mids = jnp.asarray(tables["mids"])
    factors = op_factor.transpose(0, 2, 3, 4, 1).reshape(3, 192, TERMS)

    sds = jax.ShapeDtypeStruct
    vmem, smem = pltpu.VMEM, pltpu.SMEM
    i32 = jnp.int32
    halo, payload, numbers = call(
        first_kernel,
        "sshhhhhhhh",
        [sds((CELL, 128), BF16), pltpu.HBM((64, 8, 128), BF16), sds((16, 128), i32)],
        [
            smem((1, 8), i32),
            vmem((1, 8), i32),
            vmem((8, 27), i32),
            vmem((1, 27), i32),
            vmem((27, 64), i32),
            vmem((8, 512), BF16),
            vmem((1, 512), BF16),
            vmem((768, 128), BF16),
            vmem((32, 8, 128), F32),
            vmem((8, 8, PLANE), F32),
            vmem((8, 8, PLANE), F32),
            pltpu.SemaphoreType.DMA((9,)),
            vmem((64, 8, 128), BF16),
            pltpu.SemaphoreType.DMA,
        ],
        2_000_000,
        mid_parent, mid_refined, mid_child, fine_nbr, mid_nbr, coarse_nbr.T, fine_coef, mid_leaf,
        first_filters, rows_both,
    )
    arrived = lax.all_to_all(payload, ("gy", "gz"), 0, 0, tiled=True)
    before, after = both_ways(halo, "gz")
    line = jnp.concatenate([before, halo, after], axis=0)
    before, after = both_ways(line, "gy")
    sheet = jnp.concatenate([before, line, after], axis=0)
    before, after = both_ways(sheet, "gx")

    (copies,) = call(
        plane_kernel, "v", [pltpu.HBM((8, 256, 128), BF16)],
        [vmem((256, 128), BF16), pltpu.SemaphoreType.DMA((8,))], 33_000_000, arrived
    )
    planes = lax.all_to_all(copies, "gx", 0, 0, tiled=True)

    w_factors, x_tables, centre, rows_p, last_filters, mids = call(
        tables_kernel,
        "hhhvhhh",
        [
            pltpu.VMEM((2, 3 * QUADS, 24, 256), F32),
            pltpu.VMEM((3, 256, 24), BF16),
            pltpu.VMEM((90, 8, 128), F32),
            pltpu.VMEM((16, 8, 128), F32),
            pltpu.VMEM((512, 128), BF16),
            pltpu.VMEM((128, 1024), BF16),
        ],
        [
            vmem((3, 192, TERMS), F32),
            vmem((1, TERMS), F32),
            vmem((256, 768), BF16),
            pltpu.SemaphoreType.DMA((6,)),
        ],
        600_000_000,
        factors, term_weight.reshape(1, TERMS), select, sheet, rows_p, last_filters, mids,
    )
    direct, mid_tiles, names = call(
        fine_kernel,
        "avvvww",
        [sds((8, 8, PLANE), F32), sds((28, 8, 128), F32), sds((1, 128), i32)],
        [
            vmem((GONE + 9, 8, 128), F32),
            vmem((256, ROWS_W), BF16),
            vmem((ROWS_W, 256), BF16),
            smem((16, 128), i32),
            pltpu.SemaphoreType.DMA((1,)),
        ],
        100_000_000,
        numbers, before, centre, after, w_factors, x_tables,
    )
    fine_out, mid_out = call(
        last_kernel,
        "aavvvwwwww",
        [sds((8, 512), F32), sds((1, 512), F32)],
        [
            vmem((65, 8, 128), F32),
            vmem((8, 8, PLANE), F32),
            pltpu.SemaphoreType.DMA((2,)),
            vmem((ROWS_W, 256), BF16),
            vmem((ROWS_W, 256), BF16),
            smem((16, 128), i32),
            smem((1, 128), i32),
        ],
        200_000_000,
        numbers, names, planes, mid_tiles, direct, w_factors, x_tables,
        rows_p, last_filters, mids,
    )
    return fine_out, mid_out


def solution(mesh):
    cells = ("gx", "gy", "gz")
    rows = P(cells, None)
    return jax.shard_map(
        shards,
        mesh=mesh,
        in_specs=(rows, rows, rows, P(cells), P(cells), rows, rows, P(), P(), P()),
        out_specs=(rows, rows),
        check_vma=False,
    )
```

```python
import functools
import math

import jax
import jax.numpy as jnp
import ml_dtypes
import numpy as np
from jax import lax
from jax.experimental import pallas as pl
from jax.experimental.pallas import tpu as pltpu
from jax.sharding import PartitionSpec as P

K = 8
PLANE = 64
TERMS = 32
QUADS = 8
ROWS_W = 4608
CELL = 40
GONE = 27 * 10
BF16 = jnp.bfloat16
F32 = jnp.float32
VMEM_LIMIT = 32 * 1024 * 1024


def poly_multiply(left, right):
    result = [0.0] * (len(left) + len(right) - 1)
    for first, left_coef in enumerate(left):
        for second, right_coef in enumerate(right):
            result[first + second] += left_coef * right_coef
    return result


def poly_compose(coeffs, factor, offset):
    result = [0.0]
    power_term = [1.0]
    for coef in coeffs:
        padded = result + [0.0] * (len(power_term) - len(result))
        result = [padded[place] + coef * power_term[place] for place in range(len(power_term))]
        power_term = poly_multiply(power_term, [offset, factor])
    return result


def legendre_table(basis_order):
    polys = [[1.0], [0.0, 1.0]]
    for degree in range(1, basis_order):
        upper = [0.0] + [(2 * degree + 1) * coef for coef in polys[degree]]
        lower = [degree * coef for coef in polys[degree - 1]] + [0.0] * (
            len(upper) - len(polys[degree - 1])
        )
        polys.append([(upper[place] - lower[place]) / (degree + 1) for place in range(len(upper))])
    return [
        [math.sqrt(2 * degree + 1) * coef for coef in poly_compose(polys[degree], 2.0, -1.0)]
        for degree in range(basis_order)
    ]


@functools.cache
def two_scale(basis_order):
    shifted = legendre_table(basis_order)
    filters = np.zeros((2, basis_order, basis_order))
    for which_half in range(2):
        for row_at in range(basis_order):
            halved = poly_compose(shifted[row_at], 0.5, 0.5 * which_half)
            for col_at in range(basis_order):
                product = poly_multiply(halved, shifted[col_at])
                total = sum((coef / (place + 1) for place, coef in enumerate(product)))
                filters[which_half, row_at, col_at] = total / math.sqrt(2.0)
    return filters.astype(np.float32).astype(np.float64)


def two_parts(matrix):
    high = matrix.astype(ml_dtypes.bfloat16)
    low = (matrix - high.astype(np.float64)).astype(ml_dtypes.bfloat16)
    return high, low


@functools.cache
def filter_tables():
    h = two_scale(K)
    pair = np.einsum("jqy,lrz->jlqryz", h, h).reshape(4, PLANE, PLANE)
    to_coarse = pair.transpose(0, 2, 1).reshape(4 * PLANE, PLANE)
    comp = np.concatenate(two_parts(to_coarse), axis=1)
    to_fine = pair.transpose(1, 0, 2).reshape(PLANE, 4 * PLANE)
    prol = np.concatenate(two_parts(to_fine), axis=1)
    contrib = np.stack([np.concatenate(two_parts(pair[k].T), axis=1) for k in range(4)])
    single = np.stack([np.concatenate(two_parts(pair[k]), axis=1) for k in range(4)])
    mid = np.zeros((2, PLANE, 4, 2, PLANE))
    for half in range(2):
        mid[half, :, :, half, :] = pair.transpose(1, 0, 2)
    mids = np.concatenate(two_parts(mid.reshape(128, 512)), axis=1)
    rows_c = np.broadcast_to(h.transpose(0, 2, 1).reshape(16, 8)[:, :, None], (16, 8, 128))
    rows_p = np.broadcast_to(h.reshape(16, 8)[:, :, None], (16, 8, 128))
    return dict(
        comp=comp,
        prol=prol,
        contrib=contrib,
        single=single,
        mids=mids,
        rows_c=np.ascontiguousarray(rows_c).astype(np.float32),
        rows_p=np.ascontiguousarray(rows_p).astype(np.float32),
    )


@functools.cache
def select_tables():
    out = np.arange(256) // TERMS
    term = np.arange(256) % TERMS
    col = np.arange(256)
    group = term[:, None] % 4 == (col // PLANE)[None, :]
    left = group & (out[:, None] == (col // 8 % 8)[None, :])
    right = group & (out[:, None] == (col % 8)[None, :])
    turn = (term[None, :] == (col // 8)[:, None]) & (out[None, :] == (col % 8)[:, None])
    return np.concatenate([left, right, turn], axis=1).astype(ml_dtypes.bfloat16)


def split(value):
    high = value.astype(BF16)
    return high, (value - high.astype(F32)).astype(BF16)


def dot(left, right):
    return jnp.dot(left, right, preferred_element_type=F32)


def fine_dot(value, table):
    rows = value.shape[0]
    width = table.shape[1] // 2
    if rows % 16 == 0:
        result = dot(jnp.concatenate(split(value), axis=0), table)
    else:
        high = value.astype(BF16).astype(F32)
        result = dot(jnp.concatenate([high, value - high], axis=0).astype(BF16), table)
    return result[:rows, :width] + result[rows:, :width] + result[:rows, width:]


def low_lanes(shape):
    return lax.broadcasted_iota(jnp.int32, shape, len(shape) - 1) < PLANE


def turned(value):
    return pltpu.roll(value, PLANE, value.ndim - 1)


def row_mix(tables, tile):
    total = None
    for p in range(8):
        term = tables[p] * tile[p : p + 1, :]
        total = term if total is None else total + term
    return total


def two_row_mixes(rows_ref, tile, width):
    return [
        row_mix([rows_ref[i * 8 + p, :, :width] for p in range(8)], tile) for i in range(2)
    ]


def fetches(sems, *pairs):
    copies = [
        pltpu.make_async_copy(there, here, sems.at[at]) for at, (there, here) in enumerate(pairs)
    ]
    for copy in copies:
        copy.start()
    return copies


def local_cell(device, own):
    step_x = (device >> 6) - (own >> 6) + 1
    step_y = ((device >> 3) & 7) - ((own >> 3) & 7) + 1
    step_z = (device & 7) - (own & 7) + 1
    return step_x * 9 + step_y * 3 + step_z


def tables_kernel(
    factors_h, weights_h, select_h, sheet, rows_h, filters_h, mids_h,
    ab_ref, x_ref, tiles, rows_p, filters, mids,
    factors, weights, select, sems,
):
    copies = fetches(
        sems,
        (factors_h, factors),
        (weights_h, weights),
        (select_h, select),
        (mids_h, mids),
        (filters_h, filters),
        (rows_h, rows_p),
    )
    spread_cells(sheet, tiles, 0)
    for copy in copies[:3]:
        copy.wait()
    lane = lax.broadcasted_iota(jnp.int32, (24, 256), 1)
    quad_of = (lane & 31) >> 2
    weight = jnp.concatenate([weights[...]] * 8, axis=1)
    weighted, plain = [], []
    for level in range(3):
        rows = []
        for e in range(3):
            rows.append(
                jnp.concatenate(
                    [factors[level, e * 64 + b * 8 : e * 64 + b * 8 + 8, :] for b in range(8)],
                    axis=1,
                )
            )
        values = jnp.concatenate(rows, axis=0)
        scaled = values * weight
        for quad in range(QUADS):
            weighted.append(jnp.where(quad_of == quad, scaled, 0.0))
            plain.append(jnp.where(quad_of == quad, values, 0.0))
        x_ref[level] = lax.dot_general(
            select[:, 512:768],
            values.astype(BF16),
            (((1,), (1,)), ((), ())),
            preferred_element_type=F32,
        ).astype(BF16)
    for which, parts in enumerate((weighted, plain)):
        both = dot(
            jnp.concatenate(split(jnp.concatenate(parts, axis=0)), axis=0),
            select[:, which * 256 : which * 256 + 256],
        )
        ab_ref[which] = (both[:576] + both[576:]).reshape(24, 24, 256)
    for copy in copies[3:]:
        copy.wait()


def build_w(ab_ref, level, w_ref):
    def one_quad(quad):
        at = level * QUADS + quad
        inner = [ab_ref[1, at, ez * 8 : ez * 8 + 8, :] for ez in range(3)]
        for ey in range(3):
            for pair in range(4):
                row = ey * 8 + 2 * pair
                first = ab_ref[0, at, row : row + 1, :]
                second = ab_ref[0, at, row + 1 : row + 2, :]
                for ez in range(3):
                    tile = jnp.concatenate([first * inner[ez], second * inner[ez]], axis=0)
                    e = ey * 3 + ez
                    to = quad * 512 + e * PLANE if e < 8 else 4096 + quad * PLANE
                    to += pair * 16
                    w_ref[to : to + 16, :] = tile.astype(BF16)

    for quad in range(QUADS):
        one_quad(quad)


def spread_cells(sheet, tiles, at):
    low = low_lanes((8, 128))
    values = sheet[...].astype(F32)
    for cell in range(9):
        to = (at + cell) * 10
        for pair in range(5):
            row = cell * CELL + pair * 8
            tile = values[row : row + 8, :]
            other = turned(tile)
            tiles[to + 2 * pair] = jnp.where(low, tile, other)
            tiles[to + 2 * pair + 1] = tile if pair == 4 else jnp.where(low, other, tile)


def diagonal_sum(result, rows):
    total = None
    for term in range(4):
        piece = result[term * rows : (term + 1) * rows, term * PLANE : (term + 1) * PLANE]
        total = piece if total is None else total + piece
    return total


def apply_one(sources, x_table, w_ref):
    product = dot(x_table, sources)
    low = low_lanes((32, 128))
    groups = [product[quad * 32 : quad * 32 + 32, :] for quad in range(QUADS)]
    pieces = [group[:, :512].astype(BF16) for group in groups]
    for quad in range(0, QUADS, 2):
        both = jnp.where(low, groups[quad][:, 512:], groups[quad + 1][:, 512:])
        pieces.append(both.astype(BF16))
    result = None
    for quad in range(QUADS):
        part = dot(pieces[quad], w_ref[quad * 512 : quad * 512 + 512, :])
        result = part if result is None else result + part
    for pair in range(4):
        at = 4096 + pair * 128
        result += dot(pieces[QUADS + pair], w_ref[at : at + 128, :])
    return diagonal_sum(result, 8)


def first_kernel(
    parent, refined, child_h, fine_h, mid_h, coarse_h, coef_h, leaf_h, filters_h, rows_h,
    halo, payload, numbers,
    child, child_v, fine_nbr, mid_nbr, coarse_nbr, coef, leaf, filters, rows,
    source, detail, sems, payload_v, payload_sem, contrib,
):
    slot = parent[0] >> 3
    octant = parent[0] & 7
    contrib_at = pl.multiple_of(512 + (octant & 3) * 64, 64)
    copies = fetches(
        sems,
        (child_h, child),
        (coef_h, coef),
        (filters_h.at[pl.ds(0, 256)], filters.at[pl.ds(0, 256)]),
        (rows_h.at[pl.ds(0, 16)], rows.at[pl.ds(0, 16)]),
        (leaf_h, leaf),
        (filters_h.at[pl.ds(contrib_at, 64)], contrib),
        (filters_h.at[pl.ds(256, 256)], filters.at[pl.ds(256, 256)]),
        (rows_h.at[pl.ds(16, 16)], rows.at[pl.ds(16, 16)]),
        (child_h, child_v),
        (fine_h, fine_nbr),
        (mid_h, mid_nbr),
        (coarse_h, coarse_nbr),
    )
    for copy in copies[:5]:
        copy.wait()
    comp = filters[0:256, :]

    values = coef[...].astype(F32)
    for a in range(8):
        source[:, a, :] = values[:, a * PLANE : (a + 1) * PLANE]
    tiles = [source[child[0, o]] for o in range(8)]
    lhs = jnp.concatenate(
        [jnp.concatenate(tiles[0:4], axis=1), jnp.concatenate(tiles[4:8], axis=1)], axis=0
    ).astype(BF16)
    both = dot(lhs, comp)
    partial = both[:, :PLANE] + both[:, PLANE:]
    compressed = None
    for k in range(16):
        term = rows[k, :, :PLANE] * partial[k : k + 1, :]
        compressed = term if compressed is None else compressed + term
    leaf_row = leaf[...].astype(F32)
    leaf_tile = jnp.concatenate(
        [leaf_row[:, a * PLANE : (a + 1) * PLANE] for a in range(8)], axis=0
    )
    middle = jnp.where(refined[0] > 0, compressed, leaf_tile).astype(BF16).astype(F32)

    row_at = (octant >> 2) * 8
    inner = row_mix([rows[row_at + x, :, :PLANE] for x in range(8)], middle)
    copies[5].wait()
    added = fine_dot(inner, contrib[...])
    low8 = low_lanes((8, 128))
    tag = jnp.full((8, 128), slot, jnp.int32).astype(F32)
    tile = jnp.where(low8, jnp.concatenate([added, added], axis=1), tag).astype(BF16)
    payload_v[...] = jnp.broadcast_to(tile[None], payload_v.shape)
    send = pltpu.make_async_copy(payload_v, payload, payload_sem)
    send.start()

    for copy in copies[6:8]:
        copy.wait()
    prol = jnp.concatenate([filters[256 + 64 * k : 320 + 64 * k, :] for k in range(4)], axis=1)
    live = jnp.full((8, PLANE), refined[0], jnp.int32).astype(F32)
    upper = jnp.concatenate(two_row_mixes(rows.at[16:32], middle, PLANE), axis=0)
    spread = fine_dot(upper, prol)
    for o in range(8):
        i, jl = o // 4, o % 4
        part = spread[i * 8 : i * 8 + 8, jl * PLANE : (jl + 1) * PLANE]
        detail[child[0, o]] = live * (tiles[o] - part)
    lane = lax.broadcasted_iota(jnp.int32, (8, 128), 1)
    name = jnp.where(lane < 96, tag, jnp.full((8, 128), octant, jnp.int32).astype(F32))
    pairs = [jnp.concatenate([detail[2 * k], detail[2 * k + 1]], axis=1) for k in range(4)]
    pairs.append(jnp.where(low8, jnp.concatenate([middle, middle], axis=1), name))
    halo[...] = jnp.concatenate(pairs, axis=0).astype(BF16)

    for copy in copies[8:]:
        copy.wait()
    near = fine_nbr[...]
    own = near[:, 13:14] >> 3
    cell = local_cell(near >> 3, own) * 10 + (near & 7)
    numbers[0:8, 0:27] = jnp.where(near >= 0, cell, GONE)
    near_mid = mid_nbr[...]
    own_mid = near_mid[:, 13:14]
    numbers[8:9, 0:27] = jnp.where(near_mid >= 0, local_cell(near_mid, own_mid), 27)
    numbers[8:9, 27:28] = jnp.full((1, 1), 27, jnp.int32)
    hot = jnp.where(lax.broadcasted_iota(jnp.int32, (8, 64), 1) == slot, 1.0, 0.0).astype(BF16)
    near_coarse = lax.dot_general(
        hot,
        coarse_nbr[...].astype(F32).astype(BF16),
        (((1,), (1,)), ((), ())),
        preferred_element_type=F32,
    )[0:1].astype(jnp.int32)
    numbers[9:10, 0:27] = jnp.where(near_coarse >= 0, near_coarse, 64)
    numbers[9:10, 27:28] = jnp.full((1, 1), 64, jnp.int32)
    numbers[10:11, 0:8] = child_v[...]
    numbers[10:11, 8:9] = jnp.full((1, 1), parent[0], jnp.int32)
    numbers[10:11, 9:10] = jnp.full((1, 1), refined[0], jnp.int32)
    send.wait()


def plane_kernel(arrived, copies, partial, sems):
    rows = arrived[...].astype(F32).reshape(512, 128)
    other = turned(rows)
    low = low_lanes((512, 128))
    value = jnp.where(low, rows, other)
    tag = jnp.where(low, other, rows)
    half = jnp.where(low, 0, 1)
    rhs = jnp.where((tag.astype(jnp.int32) & 1) == half, value, 0.0).astype(BF16)
    pick = jnp.where(lax.broadcasted_iota(jnp.int32, (8, 128), 1) == 0, 1.0, 0.0).astype(BF16)
    along = lax.dot_general(
        pick, tag.astype(BF16), (((1,), (1,)), ((), ())), preferred_element_type=F32
    ).astype(jnp.int32)
    p_of = lax.broadcasted_iota(jnp.int32, (8, 512), 1) & 7
    key = jnp.where(p_of == lax.broadcasted_iota(jnp.int32, (8, 512), 0), along >> 1, -1)
    hot = jnp.concatenate(
        [jnp.where(key == c2, 1.0, 0.0) for c2 in range(32)], axis=0
    ).astype(BF16)
    partial[...] = dot(hot, rhs).astype(BF16)
    for copy in fetches(sems, *((partial, copies.at[at]) for at in range(8))):
        copy.wait()


def pair_of(first, second):
    return jnp.where(low_lanes((8, 128)), first, second)


def fine_kernel(
    numbers_h, left, centre, right, ab_ref, x_ref,
    direct, mid_tiles, names_ref,
    table, mixed, w_ref, numbers, sems,
):
    copies = fetches(sems, (numbers_h, numbers))
    build_w(ab_ref, 0, w_ref)
    lanes = lax.broadcasted_iota(jnp.int32, (1, 128), 1)
    low8 = low_lanes((8, 128))
    table[GONE] = jnp.zeros((8, 128), F32)
    table[GONE + 8] = jnp.zeros((8, 128), F32)
    spread_cells(left, table, 0)
    spread_cells(right, table, 18)
    for at in range(90):
        table[90 + at] = centre[at]
    names = jnp.full((1, 128), 512, jnp.int32)
    for cell in range(27):
        meta = table[cell * 10 + 9, 0:1, :]
        name = meta * 8.0 + pltpu.roll(meta, 96, 1)
        names = jnp.where(lanes == PLANE + cell, name.astype(jnp.int32), names)
    names_ref[...] = names
    for cell in range(28):
        mid_tiles[cell] = table[cell * 10 + 8]

    for copy in copies:
        copy.wait()

    def source(t, ex, e):
        return table[numbers[t, ex * 9 + e]]

    for pair in range(4):
        pieces = []
        for t in (2 * pair, 2 * pair + 1):
            for ep in range(5):
                pieces.append(
                    jnp.concatenate(
                        [
                            pair_of(source(t, ex, 2 * ep), source(t, ex, min(2 * ep + 1, 8)))
                            for ex in range(3)
                        ],
                        axis=0,
                    ).astype(BF16)
                )
        product = dot(x_ref[0], jnp.concatenate(pieces, axis=1))
        for term in range(4):
            row = term * PLANE + pair * 16
            last = None
            for quad in range(QUADS):
                at = (quad * 4 + term) * 8
                tile = jnp.concatenate(
                    [product[at : at + 8, :512], product[at : at + 8, 640:1152]], axis=0
                )
                mixed[row : row + 16, quad * 512 : quad * 512 + 512] = tile.astype(BF16)
                tile = jnp.concatenate(
                    [product[at : at + 8, 512:640], product[at : at + 8, 1152:1280]], axis=0
                )
                if quad % 2 == 0:
                    last = tile
                else:
                    to = 4096 + quad // 2 * 128
                    tile = jnp.where(low_lanes((16, 128)), last, tile)
                    mixed[row : row + 16, to : to + 128] = tile.astype(BF16)
    result = None
    for half in range(2):
        total = None
        own = slice(half * 128, half * 128 + 128)
        for part in range(9):
            some = slice(part * 512, part * 512 + 512)
            term = dot(mixed[own, some], w_ref[some, own])
            total = term if total is None else total + term
        for term in range(2):
            rows = slice(term * PLANE, term * PLANE + PLANE)
            result = total[rows, rows] if result is None else result + total[rows, rows]
    direct[...] = result.reshape(8, 8, PLANE)


def last_kernel(
    numbers_h, names_h, planes, mid_tiles, direct, ab_ref, x_ref, rows_p, filters, mids,
    fine_out, mid_out,
    coarse, back, sems, w_mid, w_coarse, numbers, names,
):
    copies = fetches(sems, (numbers_h, numbers), (names_h, names))
    build_w(ab_ref, 1, w_mid)
    build_w(ab_ref, 2, w_coarse)
    low8 = low_lanes((8, 128))

    total = None
    for plane in range(8):
        term = planes[plane].astype(F32)
        total = term if total is None else total + term
    for c2 in range(32):
        tile = total[c2 * 8 : c2 * 8 + 8, :]
        other = turned(tile)
        coarse[2 * c2] = jnp.where(low8, tile, other)
        coarse[2 * c2 + 1] = jnp.where(low8, other, tile)
    coarse[64] = jnp.zeros((8, 128), F32)
    for copy in copies:
        copy.wait()
    octant = numbers[10, 8] & 7

    uppers, octants, owns = [], [], []
    for ep in range(5):
        for ex in range(3):
            first = numbers[8, ex * 9 + 2 * ep]
            second = numbers[8, ex * 9 + min(2 * ep + 1, 8)]
            name_1, name_2 = names[0, PLANE + first], names[0, PLANE + second]
            owns.append(pair_of(mid_tiles[first], mid_tiles[second]))
            both = pair_of(coarse[name_1 >> 3], coarse[name_2 >> 3])
            named = jnp.where(low8, name_1 & 7, name_2 & 7)
            octants.append(named)
            mix_0, mix_1 = two_row_mixes(rows_p, both, 128)
            uppers.append(jnp.where(named >= 4, mix_1, mix_0))
    stacked = jnp.concatenate(uppers, axis=0)
    high = stacked.astype(BF16).astype(F32)
    spread = dot(jnp.concatenate([high, stacked - high], axis=0).astype(BF16), mids[...])
    spread = spread[:120, :512] + spread[120:, :512] + spread[:120, 512:]
    pieces = []
    for ep in range(5):
        tiles = []
        for ex in range(3):
            at = ep * 3 + ex
            which = octants[at] & 3
            chosen = spread[at * 8 : at * 8 + 8, 0:128]
            for jl in range(1, 4):
                chosen = jnp.where(
                    which == jl, spread[at * 8 : at * 8 + 8, jl * 128 : jl * 128 + 128], chosen
                )
            tiles.append(owns[at] - chosen)
        pieces.append(jnp.concatenate(tiles, axis=0).astype(BF16))
    mid_result = apply_one(jnp.concatenate(pieces, axis=1), x_ref[1], w_mid)

    def coarse_source(ex, e):
        return coarse[numbers[9, ex * 9 + e]]

    sources = jnp.concatenate(
        [
            jnp.concatenate(
                [
                    pair_of(coarse_source(ex, 2 * ep), coarse_source(ex, min(2 * ep + 1, 8)))
                    for ex in range(3)
                ],
                axis=0,
            ).astype(BF16)
            for ep in range(5)
        ],
        axis=1,
    )
    coarse_result = apply_one(sources, x_ref[2], w_coarse)

    row_at = (octant >> 2) * 8
    upper = row_mix([rows_p[row_at + p, :, :PLANE] for p in range(8)], coarse_result)
    single = filters[pl.ds(pl.multiple_of(256 + (octant & 3) * 64, 64), 64), :]
    middle = mid_result + fine_dot(upper, single)
    for a in range(8):
        mid_out[:, a * PLANE : (a + 1) * PLANE] = middle[a : a + 1, :]
    live = jnp.full((8, PLANE), numbers[10, 9], jnp.int32).astype(F32)
    upper = jnp.concatenate(two_row_mixes(rows_p, middle, PLANE), axis=0)
    prol = jnp.concatenate([filters[64 * k : 64 * k + 64, :] for k in range(4)], axis=1)
    spread = fine_dot(upper, prol)
    for o in range(8):
        i, jl = o // 4, o % 4
        slot = numbers[10, o]
        part = spread[i * 8 : i * 8 + 8, jl * PLANE : (jl + 1) * PLANE]
        back[slot] = live * (direct[slot] + part)
    for a in range(8):
        fine_out[:, a * PLANE : (a + 1) * PLANE] = back[:, a, :]


def call(kernel, kinds, outs, scratch, flops, *args):
    any_space = pl.BlockSpec(memory_space=pl.ANY)
    vmem = pl.BlockSpec(memory_space=pltpu.VMEM)
    specs = dict(s=pl.BlockSpec(memory_space=pltpu.SMEM), v=vmem, w=vmem, h=any_space, a=any_space)
    moved = sum(math.prod(x.shape) * x.dtype.itemsize for x in (*args, *outs))
    spaces = dict(w=pltpu.VMEM, h=pltpu.HBM)
    args = [
        pltpu.with_memory_space_constraint(x, spaces[kind]) if kind in spaces else x
        for kind, x in zip(kinds, args, strict=True)
    ]
    return pl.pallas_call(
        kernel,
        out_shape=outs,
        in_specs=[specs[kind] for kind in kinds],
        out_specs=[any_space if getattr(x, "memory_space", None) == pltpu.HBM else vmem for x in outs],
        scratch_shapes=scratch,
        compiler_params=pltpu.CompilerParams(vmem_limit_bytes=VMEM_LIMIT),
        cost_estimate=pl.CostEstimate(flops=flops, bytes_accessed=moved, transcendentals=0),
        name=kernel.__name__,
    )(*args)


def both_ways(x, axis):
    count = lax.axis_size(axis)
    ends = count - 1
    before = lax.ppermute(x, axis, [(i, i + 1) for i in range(ends)])
    after = lax.ppermute(x, axis, [(i + 1, i) for i in range(ends)])
    return before, after


def shards(
    fine_coef, mid_leaf, mid_child, mid_parent, mid_refined,
    fine_nbr, mid_nbr, coarse_nbr, op_factor, term_weight,
):
    tables = filter_tables()
    select = jnp.asarray(select_tables())
    prol_rows = np.concatenate(np.split(tables["prol"], 4, axis=1), axis=0)
    single_rows = tables["single"].reshape(256, 128)
    first_filters = jnp.asarray(
        np.concatenate([tables["comp"], prol_rows, tables["contrib"].reshape(256, 128)])
    )
    last_filters = jnp.asarray(np.concatenate([prol_rows, single_rows]))
    rows_both = jnp.asarray(np.concatenate([tables["rows_c"], tables["rows_p"]]))
    rows_p = jnp.asarray(tables["rows_p"])
    mids = jnp.asarray(tables["mids"])
    factors = op_factor.transpose(0, 2, 3, 4, 1).reshape(3, 192, TERMS)

    sds = jax.ShapeDtypeStruct
    vmem, smem = pltpu.VMEM, pltpu.SMEM
    i32 = jnp.int32
    halo, payload, numbers = call(
        first_kernel,
        "sshhhhhhhh",
        [sds((CELL, 128), BF16), pltpu.HBM((64, 8, 128), BF16), sds((16, 128), i32)],
        [
            smem((1, 8), i32),
            vmem((1, 8), i32),
            vmem((8, 27), i32),
            vmem((1, 27), i32),
            vmem((27, 64), i32),
            vmem((8, 512), BF16),
            vmem((1, 512), BF16),
            vmem((512, 128), BF16),
            vmem((32, 8, 128), F32),
            vmem((8, 8, PLANE), F32),
            vmem((8, 8, PLANE), F32),
            pltpu.SemaphoreType.DMA((12,)),
            vmem((64, 8, 128), BF16),
            pltpu.SemaphoreType.DMA,
            vmem((64, 128), BF16),
        ],
        2_000_000,
        mid_parent, mid_refined, mid_child, fine_nbr, mid_nbr, coarse_nbr.T, fine_coef, mid_leaf,
        first_filters, rows_both,
    )
    arrived = lax.all_to_all(payload, ("gy", "gz"), 0, 0, tiled=True)
    before, after = both_ways(halo, "gz")
    line = jnp.concatenate([before, halo, after], axis=0)
    before, after = both_ways(line, "gy")
    sheet = jnp.concatenate([before, line, after], axis=0)
    before, after = both_ways(sheet, "gx")

    (copies,) = call(
        plane_kernel, "v", [pltpu.HBM((8, 256, 128), BF16)],
        [vmem((256, 128), BF16), pltpu.SemaphoreType.DMA((8,))], 33_000_000, arrived
    )
    planes = lax.all_to_all(copies, "gx", 0, 0, tiled=True)

    w_factors, x_tables, centre, rows_p, last_filters, mids = call(
        tables_kernel,
        "hhhvhhh",
        [
            pltpu.VMEM((2, 3 * QUADS, 24, 256), F32),
            pltpu.VMEM((3, 256, 24), BF16),
            pltpu.VMEM((90, 8, 128), F32),
            pltpu.VMEM((16, 8, 128), F32),
            pltpu.VMEM((512, 128), BF16),
            pltpu.VMEM((128, 1024), BF16),
        ],
        [
            vmem((3, 192, TERMS), F32),
            vmem((1, TERMS), F32),
            vmem((256, 768), BF16),
            pltpu.SemaphoreType.DMA((6,)),
        ],
        600_000_000,
        factors, term_weight.reshape(1, TERMS), select, sheet, rows_p, last_filters, mids,
    )
    direct, mid_tiles, names = call(
        fine_kernel,
        "avvvww",
        [sds((8, 8, PLANE), F32), sds((28, 8, 128), F32), sds((1, 128), i32)],
        [
            vmem((GONE + 9, 8, 128), F32),
            vmem((256, ROWS_W), BF16),
            vmem((ROWS_W, 256), BF16),
            smem((16, 128), i32),
            pltpu.SemaphoreType.DMA((1,)),
        ],
        100_000_000,
        numbers, before, centre, after, w_factors, x_tables,
    )
    fine_out, mid_out = call(
        last_kernel,
        "aavvvwwwww",
        [sds((8, 512), F32), sds((1, 512), F32)],
        [
            vmem((65, 8, 128), F32),
            vmem((8, 8, PLANE), F32),
            pltpu.SemaphoreType.DMA((2,)),
            vmem((ROWS_W, 256), BF16),
            vmem((ROWS_W, 256), BF16),
            smem((16, 128), i32),
            smem((1, 128), i32),
        ],
        200_000_000,
        numbers, names, planes, mid_tiles, direct, w_factors, x_tables,
        rows_p, last_filters, mids,
    )
    return fine_out, mid_out


def solution(mesh):
    cells = ("gx", "gy", "gz")
    rows = P(cells, None)
    return jax.shard_map(
        shards,
        mesh=mesh,
        in_specs=(rows, rows, rows, P(cells), P(cells), rows, rows, P(), P(), P()),
        out_specs=(rows, rows),
        check_vma=False,
    )
```

```python
import functools
import math

import jax
import jax.numpy as jnp
import ml_dtypes
import numpy as np
from jax import lax
from jax.experimental import pallas as pl
from jax.experimental.pallas import tpu as pltpu
from jax.sharding import PartitionSpec as P

K = 8
PLANE = 64
TERMS = 32
QUADS = 8
ROWS_W = 4608
CELL = 40
GONE = 27 * 10
BF16 = jnp.bfloat16
F32 = jnp.float32
VMEM_LIMIT = 32 * 1024 * 1024


def poly_multiply(left, right):
    result = [0.0] * (len(left) + len(right) - 1)
    for first, left_coef in enumerate(left):
        for second, right_coef in enumerate(right):
            result[first + second] += left_coef * right_coef
    return result


def poly_compose(coeffs, factor, offset):
    result = [0.0]
    power_term = [1.0]
    for coef in coeffs:
        padded = result + [0.0] * (len(power_term) - len(result))
        result = [padded[place] + coef * power_term[place] for place in range(len(power_term))]
        power_term = poly_multiply(power_term, [offset, factor])
    return result


def legendre_table(basis_order):
    polys = [[1.0], [0.0, 1.0]]
    for degree in range(1, basis_order):
        upper = [0.0] + [(2 * degree + 1) * coef for coef in polys[degree]]
        lower = [degree * coef for coef in polys[degree - 1]] + [0.0] * (
            len(upper) - len(polys[degree - 1])
        )
        polys.append([(upper[place] - lower[place]) / (degree + 1) for place in range(len(upper))])
    return [
        [math.sqrt(2 * degree + 1) * coef for coef in poly_compose(polys[degree], 2.0, -1.0)]
        for degree in range(basis_order)
    ]


@functools.cache
def two_scale(basis_order):
    shifted = legendre_table(basis_order)
    filters = np.zeros((2, basis_order, basis_order))
    for which_half in range(2):
        for row_at in range(basis_order):
            halved = poly_compose(shifted[row_at], 0.5, 0.5 * which_half)
            for col_at in range(basis_order):
                product = poly_multiply(halved, shifted[col_at])
                total = sum((coef / (place + 1) for place, coef in enumerate(product)))
                filters[which_half, row_at, col_at] = total / math.sqrt(2.0)
    return filters.astype(np.float32).astype(np.float64)


def two_parts(matrix):
    high = matrix.astype(ml_dtypes.bfloat16)
    low = (matrix - high.astype(np.float64)).astype(ml_dtypes.bfloat16)
    return high, low


@functools.cache
def filter_tables():
    h = two_scale(K)
    pair = np.einsum("jqy,lrz->jlqryz", h, h).reshape(4, PLANE, PLANE)
    to_coarse = pair.transpose(0, 2, 1).reshape(4 * PLANE, PLANE)
    comp = np.concatenate(two_parts(to_coarse), axis=1)
    to_fine = pair.transpose(1, 0, 2).reshape(PLANE, 4 * PLANE)
    prol = np.concatenate(two_parts(to_fine), axis=1)
    contrib = np.stack([np.concatenate(two_parts(pair[k].T), axis=1) for k in range(4)])
    single = np.stack([np.concatenate(two_parts(pair[k]), axis=1) for k in range(4)])
    mid = np.zeros((2, PLANE, 4, 2, PLANE))
    for half in range(2):
        mid[half, :, :, half, :] = pair.transpose(1, 0, 2)
    mids = np.concatenate(two_parts(mid.reshape(128, 512)), axis=1)
    rows_c = np.broadcast_to(h.transpose(0, 2, 1).reshape(16, 8)[:, :, None], (16, 8, 128))
    rows_p = np.broadcast_to(h.reshape(16, 8)[:, :, None], (16, 8, 128))
    return dict(
        comp=comp,
        prol=prol,
        contrib=contrib,
        single=single,
        mids=mids,
        rows_c=np.ascontiguousarray(rows_c).astype(np.float32),
        rows_p=np.ascontiguousarray(rows_p).astype(np.float32),
    )


@functools.cache
def select_tables():
    out = np.arange(256) // TERMS
    term = np.arange(256) % TERMS
    col = np.arange(256)
    group = term[:, None] % 4 == (col // PLANE)[None, :]
    left = group & (out[:, None] == (col // 8 % 8)[None, :])
    right = group & (out[:, None] == (col % 8)[None, :])
    turn = (term[None, :] == (col // 8)[:, None]) & (out[None, :] == (col % 8)[:, None])
    return np.concatenate([left, right, turn], axis=1).astype(ml_dtypes.bfloat16)


def split(value):
    high = value.astype(BF16)
    return high, (value - high.astype(F32)).astype(BF16)


def dot(left, right):
    return jnp.dot(left, right, preferred_element_type=F32)


def fine_dot(value, table):
    rows = value.shape[0]
    width = table.shape[1] // 2
    if rows % 16 == 0:
        result = dot(jnp.concatenate(split(value), axis=0), table)
    else:
        high = value.astype(BF16).astype(F32)
        result = dot(jnp.concatenate([high, value - high], axis=0).astype(BF16), table)
    return result[:rows, :width] + result[rows:, :width] + result[:rows, width:]


def low_lanes(shape):
    return lax.broadcasted_iota(jnp.int32, shape, len(shape) - 1) < PLANE


def turned(value):
    return pltpu.roll(value, PLANE, value.ndim - 1)


def row_mix(tables, tile):
    total = None
    for p in range(8):
        term = tables[p] * tile[p : p + 1, :]
        total = term if total is None else total + term
    return total


def two_row_mixes(rows_ref, tile, width):
    return [
        row_mix([rows_ref[i * 8 + p, :, :width] for p in range(8)], tile) for i in range(2)
    ]


def fetches(sems, *pairs):
    copies = [
        pltpu.make_async_copy(there, here, sems.at[at]) for at, (there, here) in enumerate(pairs)
    ]
    for copy in copies:
        copy.start()
    return copies


def local_cell(device, own):
    step_x = (device >> 6) - (own >> 6) + 1
    step_y = ((device >> 3) & 7) - ((own >> 3) & 7) + 1
    step_z = (device & 7) - (own & 7) + 1
    return step_y * 9 + step_z * 3 + step_x


def tables_kernel(
    factors_h, weights_h, select_h, sheet, rows_h, filters_h, mids_h,
    ab_ref, x_ref, tiles, rows_p, filters, mids,
    factors, weights, select, sems,
):
    copies = fetches(
        sems,
        (factors_h, factors),
        (weights_h, weights),
        (select_h, select),
        (mids_h, mids),
        (filters_h, filters),
        (rows_h, rows_p),
    )
    spread_cells(sheet, tiles, 0)
    for copy in copies[:3]:
        copy.wait()
    lane = lax.broadcasted_iota(jnp.int32, (24, 256), 1)
    quad_of = (lane & 31) >> 2
    weight = jnp.concatenate([weights[...]] * 8, axis=1)
    weighted, plain = [], []
    for level in range(3):
        rows = []
        for e in range(3):
            rows.append(
                jnp.concatenate(
                    [factors[level, e * 64 + b * 8 : e * 64 + b * 8 + 8, :] for b in range(8)],
                    axis=1,
                )
            )
        values = jnp.concatenate(rows, axis=0)
        scaled = values * weight
        for quad in range(QUADS):
            weighted.append(jnp.where(quad_of == quad, scaled, 0.0))
            plain.append(jnp.where(quad_of == quad, values, 0.0))
        x_ref[level] = lax.dot_general(
            select[:, 512:768],
            values.astype(BF16),
            (((1,), (1,)), ((), ())),
            preferred_element_type=F32,
        ).astype(BF16)
    for which, parts in enumerate((weighted, plain)):
        both = dot(
            jnp.concatenate(split(jnp.concatenate(parts, axis=0)), axis=0),
            select[:, which * 256 : which * 256 + 256],
        )
        ab_ref[which] = (both[:576] + both[576:]).reshape(24, 24, 256)
    for copy in copies[3:]:
        copy.wait()


def build_w(ab_ref, level, w_ref):
    def one_quad(quad):
        at = level * QUADS + quad
        inner = [ab_ref[1, at, ez * 8 : ez * 8 + 8, :] for ez in range(3)]
        for ey in range(3):
            for pair in range(4):
                row = ey * 8 + 2 * pair
                first = ab_ref[0, at, row : row + 1, :]
                second = ab_ref[0, at, row + 1 : row + 2, :]
                for ez in range(3):
                    tile = jnp.concatenate([first * inner[ez], second * inner[ez]], axis=0)
                    e = ey * 3 + ez
                    to = quad * 512 + e * PLANE if e < 8 else 4096 + quad * PLANE
                    to += pair * 16
                    w_ref[to : to + 16, :] = tile.astype(BF16)

    for quad in range(QUADS):
        one_quad(quad)


def spread_cells(sheet, tiles, at):
    low = low_lanes((8, 128))
    values = sheet[...].astype(F32)
    for cell in range(9):
        to = (at + cell) * 10
        for pair in range(5):
            row = cell * CELL + pair * 8
            tile = values[row : row + 8, :]
            other = turned(tile)
            tiles[to + 2 * pair] = jnp.where(low, tile, other)
            tiles[to + 2 * pair + 1] = tile if pair == 4 else jnp.where(low, other, tile)


def diagonal_sum(result, rows):
    total = None
    for term in range(4):
        piece = result[term * rows : (term + 1) * rows, term * PLANE : (term + 1) * PLANE]
        total = piece if total is None else total + piece
    return total


def apply_one(sources, x_table, w_ref):
    product = dot(x_table, sources)
    low = low_lanes((32, 128))
    groups = [product[quad * 32 : quad * 32 + 32, :] for quad in range(QUADS)]
    pieces = [group[:, :512].astype(BF16) for group in groups]
    for quad in range(0, QUADS, 2):
        both = jnp.where(low, groups[quad][:, 512:], groups[quad + 1][:, 512:])
        pieces.append(both.astype(BF16))
    result = None
    for quad in range(QUADS):
        part = dot(pieces[quad], w_ref[quad * 512 : quad * 512 + 512, :])
        result = part if result is None else result + part
    for pair in range(4):
        at = 4096 + pair * 128
        result += dot(pieces[QUADS + pair], w_ref[at : at + 128, :])
    return diagonal_sum(result, 8)


def first_kernel(
    parent, refined, child_h, fine_h, mid_h, coarse_h, coef_h, leaf_h, filters_h, rows_h,
    halo, payload, numbers,
    child, child_v, fine_nbr, mid_nbr, coarse_nbr, coef, leaf, filters, rows,
    source, detail, sems, payload_v, payload_sem, contrib,
):
    slot = parent[0] >> 3
    octant = parent[0] & 7
    contrib_at = pl.multiple_of(512 + (octant & 3) * 64, 64)
    copies = fetches(
        sems,
        (child_h, child),
        (coef_h, coef),
        (filters_h.at[pl.ds(0, 256)], filters.at[pl.ds(0, 256)]),
        (rows_h.at[pl.ds(0, 16)], rows.at[pl.ds(0, 16)]),
        (leaf_h, leaf),
        (filters_h.at[pl.ds(contrib_at, 64)], contrib),
        (filters_h.at[pl.ds(256, 256)], filters.at[pl.ds(256, 256)]),
        (rows_h.at[pl.ds(16, 16)], rows.at[pl.ds(16, 16)]),
        (child_h, child_v),
        (fine_h, fine_nbr),
        (mid_h, mid_nbr),
        (coarse_h, coarse_nbr),
    )
    for copy in copies[:5]:
        copy.wait()
    comp = filters[0:256, :]

    values = coef[...].astype(F32)
    for a in range(8):
        source[:, a, :] = values[:, a * PLANE : (a + 1) * PLANE]
    tiles = [source[child[0, o]] for o in range(8)]
    lhs = jnp.concatenate(
        [jnp.concatenate(tiles[0:4], axis=1), jnp.concatenate(tiles[4:8], axis=1)], axis=0
    ).astype(BF16)
    both = dot(lhs, comp)
    partial = both[:, :PLANE] + both[:, PLANE:]
    compressed = None
    for k in range(16):
        term = rows[k, :, :PLANE] * partial[k : k + 1, :]
        compressed = term if compressed is None else compressed + term
    leaf_row = leaf[...].astype(F32)
    leaf_tile = jnp.concatenate(
        [leaf_row[:, a * PLANE : (a + 1) * PLANE] for a in range(8)], axis=0
    )
    middle = jnp.where(refined[0] > 0, compressed, leaf_tile).astype(BF16).astype(F32)

    row_at = (octant >> 2) * 8
    inner = row_mix([rows[row_at + x, :, :PLANE] for x in range(8)], middle)
    copies[5].wait()
    added = fine_dot(inner, contrib[...])
    low8 = low_lanes((8, 128))
    tag = jnp.full((8, 128), slot, jnp.int32).astype(F32)
    tile = jnp.where(low8, jnp.concatenate([added, added], axis=1), tag).astype(BF16)
    payload_v[...] = jnp.broadcast_to(tile[None], payload_v.shape)
    send = pltpu.make_async_copy(payload_v, payload, payload_sem)
    send.start()

    for copy in copies[6:8]:
        copy.wait()
    prol = jnp.concatenate([filters[256 + 64 * k : 320 + 64 * k, :] for k in range(4)], axis=1)
    live = jnp.full((8, PLANE), refined[0], jnp.int32).astype(F32)
    upper = jnp.concatenate(two_row_mixes(rows.at[16:32], middle, PLANE), axis=0)
    spread = fine_dot(upper, prol)
    for o in range(8):
        i, jl = o // 4, o % 4
        part = spread[i * 8 : i * 8 + 8, jl * PLANE : (jl + 1) * PLANE]
        detail[child[0, o]] = live * (tiles[o] - part)
    lane = lax.broadcasted_iota(jnp.int32, (8, 128), 1)
    name = jnp.where(lane < 96, tag, jnp.full((8, 128), octant, jnp.int32).astype(F32))
    pairs = [jnp.concatenate([detail[2 * k], detail[2 * k + 1]], axis=1) for k in range(4)]
    pairs.append(jnp.where(low8, jnp.concatenate([middle, middle], axis=1), name))
    halo[...] = jnp.concatenate(pairs, axis=0).astype(BF16)

    for copy in copies[8:]:
        copy.wait()
    near = fine_nbr[...]
    own = near[:, 13:14] >> 3
    cell = local_cell(near >> 3, own) * 10 + (near & 7)
    numbers[0:8, 0:27] = jnp.where(near >= 0, cell, GONE)
    near_mid = mid_nbr[...]
    own_mid = near_mid[:, 13:14]
    numbers[8:9, 0:27] = jnp.where(near_mid >= 0, local_cell(near_mid, own_mid), 27)
    numbers[8:9, 27:28] = jnp.full((1, 1), 27, jnp.int32)
    hot = jnp.where(lax.broadcasted_iota(jnp.int32, (8, 64), 1) == slot, 1.0, 0.0).astype(BF16)
    near_coarse = lax.dot_general(
        hot,
        coarse_nbr[...].astype(F32).astype(BF16),
        (((1,), (1,)), ((), ())),
        preferred_element_type=F32,
    )[0:1].astype(jnp.int32)
    numbers[9:10, 0:27] = jnp.where(near_coarse >= 0, near_coarse, 64)
    numbers[9:10, 27:28] = jnp.full((1, 1), 64, jnp.int32)
    numbers[10:11, 0:8] = child_v[...]
    numbers[10:11, 8:9] = jnp.full((1, 1), parent[0], jnp.int32)
    numbers[10:11, 9:10] = jnp.full((1, 1), refined[0], jnp.int32)
    send.wait()


def plane_kernel(arrived, copies, partial, sems):
    rows = arrived[...].astype(F32).reshape(512, 128)
    other = turned(rows)
    low = low_lanes((512, 128))
    value = jnp.where(low, rows, other)
    tag = jnp.where(low, other, rows)
    half = jnp.where(low, 0, 1)
    rhs = jnp.where((tag.astype(jnp.int32) & 1) == half, value, 0.0).astype(BF16)
    pick = jnp.where(lax.broadcasted_iota(jnp.int32, (8, 128), 1) == 0, 1.0, 0.0).astype(BF16)
    along = lax.dot_general(
        pick, tag.astype(BF16), (((1,), (1,)), ((), ())), preferred_element_type=F32
    ).astype(jnp.int32)
    p_of = lax.broadcasted_iota(jnp.int32, (8, 512), 1) & 7
    key = jnp.where(p_of == lax.broadcasted_iota(jnp.int32, (8, 512), 0), along >> 1, -1)
    hot = jnp.concatenate(
        [jnp.where(key == c2, 1.0, 0.0) for c2 in range(32)], axis=0
    ).astype(BF16)
    partial[...] = dot(hot, rhs).astype(BF16)
    for copy in fetches(sems, *((partial, copies.at[at]) for at in range(8))):
        copy.wait()


def pair_of(first, second):
    return jnp.where(low_lanes((8, 128)), first, second)


def fine_kernel(
    numbers_h, left, centre, right, ab_ref, x_ref,
    direct, mid_tiles, names_ref,
    table, mixed, w_ref, numbers, sems,
):
    copies = fetches(sems, (numbers_h, numbers))
    build_w(ab_ref, 0, w_ref)
    lanes = lax.broadcasted_iota(jnp.int32, (1, 128), 1)
    low8 = low_lanes((8, 128))
    table[GONE] = jnp.zeros((8, 128), F32)
    table[GONE + 8] = jnp.zeros((8, 128), F32)
    spread_cells(left, table, 0)
    spread_cells(right, table, 18)
    for at in range(90):
        table[90 + at] = centre[at]
    names = jnp.full((1, 128), 512, jnp.int32)
    for cell in range(27):
        meta = table[cell * 10 + 9, 0:1, :]
        name = meta * 8.0 + pltpu.roll(meta, 96, 1)
        names = jnp.where(lanes == PLANE + cell, name.astype(jnp.int32), names)
    names_ref[...] = names
    for cell in range(28):
        mid_tiles[cell] = table[cell * 10 + 8]

    for copy in copies:
        copy.wait()

    def source(t, ex, e):
        return table[numbers[t, ex * 9 + e]]

    for pair in range(4):
        pieces = []
        for t in (2 * pair, 2 * pair + 1):
            for ep in range(5):
                pieces.append(
                    jnp.concatenate(
                        [
                            pair_of(source(t, ex, 2 * ep), source(t, ex, min(2 * ep + 1, 8)))
                            for ex in range(3)
                        ],
                        axis=0,
                    ).astype(BF16)
                )
        product = dot(x_ref[0], jnp.concatenate(pieces, axis=1))
        for term in range(4):
            row = term * PLANE + pair * 16
            last = None
            for quad in range(QUADS):
                at = (quad * 4 + term) * 8
                tile = jnp.concatenate(
                    [product[at : at + 8, :512], product[at : at + 8, 640:1152]], axis=0
                )
                mixed[row : row + 16, quad * 512 : quad * 512 + 512] = tile.astype(BF16)
                tile = jnp.concatenate(
                    [product[at : at + 8, 512:640], product[at : at + 8, 1152:1280]], axis=0
                )
                if quad % 2 == 0:
                    last = tile
                else:
                    to = 4096 + quad // 2 * 128
                    tile = jnp.where(low_lanes((16, 128)), last, tile)
                    mixed[row : row + 16, to : to + 128] = tile.astype(BF16)
    result = None
    for half in range(2):
        total = None
        own = slice(half * 128, half * 128 + 128)
        for part in range(9):
            some = slice(part * 512, part * 512 + 512)
            term = dot(mixed[own, some], w_ref[some, own])
            total = term if total is None else total + term
        for term in range(2):
            rows = slice(term * PLANE, term * PLANE + PLANE)
            result = total[rows, rows] if result is None else result + total[rows, rows]
    direct[...] = result.reshape(8, 8, PLANE)


def last_kernel(
    numbers_h, names_h, planes, mid_tiles, direct, ab_ref, x_ref, rows_p, filters, mids,
    fine_out, mid_out,
    coarse, back, sems, w_mid, w_coarse, numbers, names,
):
    copies = fetches(sems, (numbers_h, numbers), (names_h, names))
    build_w(ab_ref, 1, w_mid)
    build_w(ab_ref, 2, w_coarse)
    low8 = low_lanes((8, 128))

    total = None
    for plane in range(8):
        term = planes[plane].astype(F32)
        total = term if total is None else total + term
    for c2 in range(32):
        tile = total[c2 * 8 : c2 * 8 + 8, :]
        other = turned(tile)
        coarse[2 * c2] = jnp.where(low8, tile, other)
        coarse[2 * c2 + 1] = jnp.where(low8, other, tile)
    coarse[64] = jnp.zeros((8, 128), F32)
    for copy in copies:
        copy.wait()
    octant = numbers[10, 8] & 7

    uppers, octants, owns = [], [], []
    for ep in range(5):
        for ex in range(3):
            first = numbers[8, ex * 9 + 2 * ep]
            second = numbers[8, ex * 9 + min(2 * ep + 1, 8)]
            name_1, name_2 = names[0, PLANE + first], names[0, PLANE + second]
            owns.append(pair_of(mid_tiles[first], mid_tiles[second]))
            both = pair_of(coarse[name_1 >> 3], coarse[name_2 >> 3])
            named = jnp.where(low8, name_1 & 7, name_2 & 7)
            octants.append(named)
            mix_0, mix_1 = two_row_mixes(rows_p, both, 128)
            uppers.append(jnp.where(named >= 4, mix_1, mix_0))
    stacked = jnp.concatenate(uppers, axis=0)
    high = stacked.astype(BF16).astype(F32)
    spread = dot(jnp.concatenate([high, stacked - high], axis=0).astype(BF16), mids[...])
    spread = spread[:120, :512] + spread[120:, :512] + spread[:120, 512:]
    pieces = []
    for ep in range(5):
        tiles = []
        for ex in range(3):
            at = ep * 3 + ex
            which = octants[at] & 3
            chosen = spread[at * 8 : at * 8 + 8, 0:128]
            for jl in range(1, 4):
                chosen = jnp.where(
                    which == jl, spread[at * 8 : at * 8 + 8, jl * 128 : jl * 128 + 128], chosen
                )
            tiles.append(owns[at] - chosen)
        pieces.append(jnp.concatenate(tiles, axis=0).astype(BF16))
    mid_result = apply_one(jnp.concatenate(pieces, axis=1), x_ref[1], w_mid)

    def coarse_source(ex, e):
        return coarse[numbers[9, ex * 9 + e]]

    sources = jnp.concatenate(
        [
            jnp.concatenate(
                [
                    pair_of(coarse_source(ex, 2 * ep), coarse_source(ex, min(2 * ep + 1, 8)))
                    for ex in range(3)
                ],
                axis=0,
            ).astype(BF16)
            for ep in range(5)
        ],
        axis=1,
    )
    coarse_result = apply_one(sources, x_ref[2], w_coarse)

    row_at = (octant >> 2) * 8
    upper = row_mix([rows_p[row_at + p, :, :PLANE] for p in range(8)], coarse_result)
    single = filters[pl.ds(pl.multiple_of(256 + (octant & 3) * 64, 64), 64), :]
    middle = mid_result + fine_dot(upper, single)
    for a in range(8):
        mid_out[:, a * PLANE : (a + 1) * PLANE] = middle[a : a + 1, :]
    live = jnp.full((8, PLANE), numbers[10, 9], jnp.int32).astype(F32)
    upper = jnp.concatenate(two_row_mixes(rows_p, middle, PLANE), axis=0)
    prol = jnp.concatenate([filters[64 * k : 64 * k + 64, :] for k in range(4)], axis=1)
    spread = fine_dot(upper, prol)
    for o in range(8):
        i, jl = o // 4, o % 4
        slot = numbers[10, o]
        part = spread[i * 8 : i * 8 + 8, jl * PLANE : (jl + 1) * PLANE]
        back[slot] = live * (direct[slot] + part)
    for a in range(8):
        fine_out[:, a * PLANE : (a + 1) * PLANE] = back[:, a, :]


def call(kernel, kinds, outs, scratch, flops, *args):
    any_space = pl.BlockSpec(memory_space=pl.ANY)
    vmem = pl.BlockSpec(memory_space=pltpu.VMEM)
    specs = dict(s=pl.BlockSpec(memory_space=pltpu.SMEM), v=vmem, w=vmem, h=any_space, a=any_space)
    moved = sum(math.prod(x.shape) * x.dtype.itemsize for x in (*args, *outs))
    spaces = dict(w=pltpu.VMEM, h=pltpu.HBM)
    args = [
        pltpu.with_memory_space_constraint(x, spaces[kind]) if kind in spaces else x
        for kind, x in zip(kinds, args, strict=True)
    ]
    return pl.pallas_call(
        kernel,
        out_shape=outs,
        in_specs=[specs[kind] for kind in kinds],
        out_specs=[any_space if getattr(x, "memory_space", None) == pltpu.HBM else vmem for x in outs],
        scratch_shapes=scratch,
        compiler_params=pltpu.CompilerParams(vmem_limit_bytes=VMEM_LIMIT),
        cost_estimate=pl.CostEstimate(flops=flops, bytes_accessed=moved, transcendentals=0),
        name=kernel.__name__,
    )(*args)


def both_ways(x, axis):
    count = lax.axis_size(axis)
    ends = count - 1
    before = lax.ppermute(x, axis, [(i, i + 1) for i in range(ends)])
    after = lax.ppermute(x, axis, [(i + 1, i) for i in range(ends)])
    return before, after


def shards(
    fine_coef, mid_leaf, mid_child, mid_parent, mid_refined,
    fine_nbr, mid_nbr, coarse_nbr, op_factor, term_weight,
):
    tables = filter_tables()
    select = jnp.asarray(select_tables())
    prol_rows = np.concatenate(np.split(tables["prol"], 4, axis=1), axis=0)
    single_rows = tables["single"].reshape(256, 128)
    first_filters = jnp.asarray(
        np.concatenate([tables["comp"], prol_rows, tables["contrib"].reshape(256, 128)])
    )
    last_filters = jnp.asarray(np.concatenate([prol_rows, single_rows]))
    rows_both = jnp.asarray(np.concatenate([tables["rows_c"], tables["rows_p"]]))
    rows_p = jnp.asarray(tables["rows_p"])
    mids = jnp.asarray(tables["mids"])
    factors = op_factor.transpose(0, 2, 3, 4, 1).reshape(3, 192, TERMS)

    sds = jax.ShapeDtypeStruct
    vmem, smem = pltpu.VMEM, pltpu.SMEM
    i32 = jnp.int32
    halo, payload, numbers = call(
        first_kernel,
        "sshhhhhhhh",
        [sds((CELL, 128), BF16), pltpu.HBM((64, 8, 128), BF16), sds((16, 128), i32)],
        [
            smem((1, 8), i32),
            vmem((1, 8), i32),
            vmem((8, 27), i32),
            vmem((1, 27), i32),
            vmem((27, 64), i32),
            vmem((8, 512), BF16),
            vmem((1, 512), BF16),
            vmem((512, 128), BF16),
            vmem((32, 8, 128), F32),
            vmem((8, 8, PLANE), F32),
            vmem((8, 8, PLANE), F32),
            pltpu.SemaphoreType.DMA((12,)),
            vmem((64, 8, 128), BF16),
            pltpu.SemaphoreType.DMA,
            vmem((64, 128), BF16),
        ],
        2_000_000,
        mid_parent, mid_refined, mid_child, fine_nbr, mid_nbr, coarse_nbr.T, fine_coef, mid_leaf,
        first_filters, rows_both,
    )
    arrived = lax.all_to_all(payload, ("gy", "gz"), 0, 0, tiled=True)
    before, after = both_ways(halo, "gx")
    line = jnp.concatenate([before, halo, after], axis=0)
    before, after = both_ways(line, "gz")
    sheet = jnp.concatenate([before, line, after], axis=0)
    before, after = both_ways(sheet, "gy")

    (copies,) = call(
        plane_kernel, "v", [pltpu.HBM((8, 256, 128), BF16)],
        [vmem((256, 128), BF16), pltpu.SemaphoreType.DMA((8,))], 33_000_000, arrived
    )
    planes = lax.all_to_all(copies, "gx", 0, 0, tiled=True)

    w_factors, x_tables, centre, rows_p, last_filters, mids = call(
        tables_kernel,
        "hhhvhhh",
        [
            pltpu.VMEM((2, 3 * QUADS, 24, 256), F32),
            pltpu.VMEM((3, 256, 24), BF16),
            pltpu.VMEM((90, 8, 128), F32),
            pltpu.VMEM((16, 8, 128), F32),
            pltpu.VMEM((512, 128), BF16),
            pltpu.VMEM((128, 1024), BF16),
        ],
        [
            vmem((3, 192, TERMS), F32),
            vmem((1, TERMS), F32),
            vmem((256, 768), BF16),
            pltpu.SemaphoreType.DMA((6,)),
        ],
        600_000_000,
        factors, term_weight.reshape(1, TERMS), select, sheet, rows_p, last_filters, mids,
    )
    direct, mid_tiles, names = call(
        fine_kernel,
        "avvvww",
        [sds((8, 8, PLANE), F32), sds((28, 8, 128), F32), sds((1, 128), i32)],
        [
            vmem((GONE + 9, 8, 128), F32),
            vmem((256, ROWS_W), BF16),
            vmem((ROWS_W, 256), BF16),
            smem((16, 128), i32),
            pltpu.SemaphoreType.DMA((1,)),
        ],
        100_000_000,
        numbers, before, centre, after, w_factors, x_tables,
    )
    fine_out, mid_out = call(
        last_kernel,
        "aavvvwwwww",
        [sds((8, 512), F32), sds((1, 512), F32)],
        [
            vmem((65, 8, 128), F32),
            vmem((8, 8, PLANE), F32),
            pltpu.SemaphoreType.DMA((2,)),
            vmem((ROWS_W, 256), BF16),
            vmem((ROWS_W, 256), BF16),
            smem((16, 128), i32),
            smem((1, 128), i32),
        ],
        200_000_000,
        numbers, names, planes, mid_tiles, direct, w_factors, x_tables,
        rows_p, last_filters, mids,
    )
    return fine_out, mid_out


def solution(mesh):
    cells = ("gx", "gy", "gz")
    rows = P(cells, None)
    return jax.shard_map(
        shards,
        mesh=mesh,
        in_specs=(rows, rows, rows, P(cells), P(cells), rows, rows, P(), P(), P()),
        out_specs=(rows, rows),
        check_vma=False,
    )
```

```python
import functools
import math

import jax
import jax.numpy as jnp
import ml_dtypes
import numpy as np
from jax import lax
from jax.experimental import pallas as pl
from jax.experimental.pallas import tpu as pltpu
from jax.sharding import PartitionSpec as P

K = 8
PLANE = 64
TERMS = 32
QUADS = 8
ROWS_W = 4608
CELL = 40
GONE = 27 * 10
BF16 = jnp.bfloat16
F32 = jnp.float32
VMEM_LIMIT = 32 * 1024 * 1024


def poly_multiply(left, right):
    result = [0.0] * (len(left) + len(right) - 1)
    for first, left_coef in enumerate(left):
        for second, right_coef in enumerate(right):
            result[first + second] += left_coef * right_coef
    return result


def poly_compose(coeffs, factor, offset):
    result = [0.0]
    power_term = [1.0]
    for coef in coeffs:
        padded = result + [0.0] * (len(power_term) - len(result))
        result = [padded[place] + coef * power_term[place] for place in range(len(power_term))]
        power_term = poly_multiply(power_term, [offset, factor])
    return result


def legendre_table(basis_order):
    polys = [[1.0], [0.0, 1.0]]
    for degree in range(1, basis_order):
        upper = [0.0] + [(2 * degree + 1) * coef for coef in polys[degree]]
        lower = [degree * coef for coef in polys[degree - 1]] + [0.0] * (
            len(upper) - len(polys[degree - 1])
        )
        polys.append([(upper[place] - lower[place]) / (degree + 1) for place in range(len(upper))])
    return [
        [math.sqrt(2 * degree + 1) * coef for coef in poly_compose(polys[degree], 2.0, -1.0)]
        for degree in range(basis_order)
    ]


@functools.cache
def two_scale(basis_order):
    shifted = legendre_table(basis_order)
    filters = np.zeros((2, basis_order, basis_order))
    for which_half in range(2):
        for row_at in range(basis_order):
            halved = poly_compose(shifted[row_at], 0.5, 0.5 * which_half)
            for col_at in range(basis_order):
                product = poly_multiply(halved, shifted[col_at])
                total = sum((coef / (place + 1) for place, coef in enumerate(product)))
                filters[which_half, row_at, col_at] = total / math.sqrt(2.0)
    return filters.astype(np.float32).astype(np.float64)


def two_parts(matrix):
    high = matrix.astype(ml_dtypes.bfloat16)
    low = (matrix - high.astype(np.float64)).astype(ml_dtypes.bfloat16)
    return high, low


@functools.cache
def filter_tables():
    h = two_scale(K)
    pair = np.einsum("jqy,lrz->jlqryz", h, h).reshape(4, PLANE, PLANE)
    to_coarse = pair.transpose(0, 2, 1).reshape(4 * PLANE, PLANE)
    comp = np.concatenate(two_parts(to_coarse), axis=1)
    to_fine = pair.transpose(1, 0, 2).reshape(PLANE, 4 * PLANE)
    prol = np.concatenate(two_parts(to_fine), axis=1)
    contrib = np.stack([np.concatenate(two_parts(pair[k].T), axis=1) for k in range(4)])
    single = np.stack([np.concatenate(two_parts(pair[k]), axis=1) for k in range(4)])
    mid = np.zeros((2, PLANE, 4, 2, PLANE))
    for half in range(2):
        mid[half, :, :, half, :] = pair.transpose(1, 0, 2)
    mids = np.concatenate(two_parts(mid.reshape(128, 512)), axis=1)
    rows_c = np.broadcast_to(h.transpose(0, 2, 1).reshape(16, 8)[:, :, None], (16, 8, 128))
    rows_p = np.broadcast_to(h.reshape(16, 8)[:, :, None], (16, 8, 128))
    return dict(
        comp=comp,
        prol=prol,
        contrib=contrib,
        single=single,
        mids=mids,
        rows_c=np.ascontiguousarray(rows_c).astype(np.float32),
        rows_p=np.ascontiguousarray(rows_p).astype(np.float32),
    )


@functools.cache
def select_tables():
    out = np.arange(256) // TERMS
    term = np.arange(256) % TERMS
    col = np.arange(256)
    group = term[:, None] % 4 == (col // PLANE)[None, :]
    left = group & (out[:, None] == (col // 8 % 8)[None, :])
    right = group & (out[:, None] == (col % 8)[None, :])
    turn = (term[None, :] == (col // 8)[:, None]) & (out[None, :] == (col % 8)[:, None])
    return np.concatenate([left, right, turn], axis=1).astype(ml_dtypes.bfloat16)


def split(value):
    high = value.astype(BF16)
    return high, (value - high.astype(F32)).astype(BF16)


def dot(left, right):
    return jnp.dot(left, right, preferred_element_type=F32)


def fine_dot(value, table):
    rows = value.shape[0]
    width = table.shape[1] // 2
    if rows % 16 == 0:
        result = dot(jnp.concatenate(split(value), axis=0), table)
    else:
        high = value.astype(BF16).astype(F32)
        result = dot(jnp.concatenate([high, value - high], axis=0).astype(BF16), table)
    return result[:rows, :width] + result[rows:, :width] + result[:rows, width:]


def low_lanes(shape):
    return lax.broadcasted_iota(jnp.int32, shape, len(shape) - 1) < PLANE


def turned(value):
    return pltpu.roll(value, PLANE, value.ndim - 1)


def row_mix(tables, tile):
    total = None
    for p in range(8):
        term = tables[p] * tile[p : p + 1, :]
        total = term if total is None else total + term
    return total


def two_row_mixes(rows_ref, tile, width):
    return [
        row_mix([rows_ref[i * 8 + p, :, :width] for p in range(8)], tile) for i in range(2)
    ]


def fetches(sems, *pairs):
    copies = [
        pltpu.make_async_copy(there, here, sems.at[at]) for at, (there, here) in enumerate(pairs)
    ]
    for copy in copies:
        copy.start()
    return copies


def local_cell(device, own):
    step_x = (device >> 6) - (own >> 6) + 1
    step_y = ((device >> 3) & 7) - ((own >> 3) & 7) + 1
    step_z = (device & 7) - (own & 7) + 1
    return step_z * 9 + step_y * 3 + step_x


def tables_kernel(
    factors_h, weights_h, select_h, sheet, rows_h, filters_h, mids_h,
    ab_ref, x_ref, tiles, rows_p, filters, mids,
    factors, weights, select, sems,
):
    copies = fetches(
        sems,
        (factors_h, factors),
        (weights_h, weights),
        (select_h, select),
        (mids_h, mids),
        (filters_h, filters),
        (rows_h, rows_p),
    )
    spread_cells(sheet, tiles, 0)
    for copy in copies[:3]:
        copy.wait()
    lane = lax.broadcasted_iota(jnp.int32, (24, 256), 1)
    quad_of = (lane & 31) >> 2
    weight = jnp.concatenate([weights[...]] * 8, axis=1)
    weighted, plain = [], []
    for level in range(3):
        rows = []
        for e in range(3):
            rows.append(
                jnp.concatenate(
                    [factors[level, e * 64 + b * 8 : e * 64 + b * 8 + 8, :] for b in range(8)],
                    axis=1,
                )
            )
        values = jnp.concatenate(rows, axis=0)
        scaled = values * weight
        for quad in range(QUADS):
            weighted.append(jnp.where(quad_of == quad, scaled, 0.0))
            plain.append(jnp.where(quad_of == quad, values, 0.0))
        x_ref[level] = lax.dot_general(
            select[:, 512:768],
            values.astype(BF16),
            (((1,), (1,)), ((), ())),
            preferred_element_type=F32,
        ).astype(BF16)
    for which, parts in enumerate((weighted, plain)):
        both = dot(
            jnp.concatenate(split(jnp.concatenate(parts, axis=0)), axis=0),
            select[:, which * 256 : which * 256 + 256],
        )
        ab_ref[which] = (both[:576] + both[576:]).reshape(24, 24, 256)
    for copy in copies[3:]:
        copy.wait()


def build_w(ab_ref, level, w_ref):
    def one_quad(quad):
        at = level * QUADS + quad
        inner = [ab_ref[1, at, ez * 8 : ez * 8 + 8, :] for ez in range(3)]
        for ey in range(3):
            for pair in range(4):
                row = ey * 8 + 2 * pair
                first = ab_ref[0, at, row : row + 1, :]
                second = ab_ref[0, at, row + 1 : row + 2, :]
                for ez in range(3):
                    tile = jnp.concatenate([first * inner[ez], second * inner[ez]], axis=0)
                    e = ey * 3 + ez
                    to = quad * 512 + e * PLANE if e < 8 else 4096 + quad * PLANE
                    to += pair * 16
                    w_ref[to : to + 16, :] = tile.astype(BF16)

    for quad in range(QUADS):
        one_quad(quad)


def spread_cells(sheet, tiles, at):
    low = low_lanes((8, 128))
    values = sheet[...].astype(F32)
    for cell in range(9):
        to = (at + cell) * 10
        for pair in range(5):
            row = cell * CELL + pair * 8
            tile = values[row : row + 8, :]
            other = turned(tile)
            tiles[to + 2 * pair] = jnp.where(low, tile, other)
            tiles[to + 2 * pair + 1] = tile if pair == 4 else jnp.where(low, other, tile)


def diagonal_sum(result, rows):
    total = None
    for term in range(4):
        piece = result[term * rows : (term + 1) * rows, term * PLANE : (term + 1) * PLANE]
        total = piece if total is None else total + piece
    return total


def apply_one(sources, x_table, w_ref):
    product = dot(x_table, sources)
    low = low_lanes((32, 128))
    groups = [product[quad * 32 : quad * 32 + 32, :] for quad in range(QUADS)]
    pieces = [group[:, :512].astype(BF16) for group in groups]
    for quad in range(0, QUADS, 2):
        both = jnp.where(low, groups[quad][:, 512:], groups[quad + 1][:, 512:])
        pieces.append(both.astype(BF16))
    result = None
    for quad in range(QUADS):
        part = dot(pieces[quad], w_ref[quad * 512 : quad * 512 + 512, :])
        result = part if result is None else result + part
    for pair in range(4):
        at = 4096 + pair * 128
        result += dot(pieces[QUADS + pair], w_ref[at : at + 128, :])
    return diagonal_sum(result, 8)


def first_kernel(
    parent, refined, child_h, fine_h, mid_h, coarse_h, coef_h, leaf_h, filters_h, rows_h,
    halo, payload, numbers,
    child, child_v, fine_nbr, mid_nbr, coarse_nbr, coef, leaf, filters, rows,
    source, detail, sems, payload_v, payload_sem, contrib,
):
    slot = parent[0] >> 3
    octant = parent[0] & 7
    contrib_at = pl.multiple_of(512 + (octant & 3) * 64, 64)
    copies = fetches(
        sems,
        (child_h, child),
        (coef_h, coef),
        (filters_h.at[pl.ds(0, 256)], filters.at[pl.ds(0, 256)]),
        (rows_h.at[pl.ds(0, 16)], rows.at[pl.ds(0, 16)]),
        (leaf_h, leaf),
        (filters_h.at[pl.ds(contrib_at, 64)], contrib),
        (filters_h.at[pl.ds(256, 256)], filters.at[pl.ds(256, 256)]),
        (rows_h.at[pl.ds(16, 16)], rows.at[pl.ds(16, 16)]),
        (child_h, child_v),
        (fine_h, fine_nbr),
        (mid_h, mid_nbr),
        (coarse_h, coarse_nbr),
    )
    for copy in copies[:5]:
        copy.wait()
    comp = filters[0:256, :]

    values = coef[...].astype(F32)
    for a in range(8):
        source[:, a, :] = values[:, a * PLANE : (a + 1) * PLANE]
    tiles = [source[child[0, o]] for o in range(8)]
    lhs = jnp.concatenate(
        [jnp.concatenate(tiles[0:4], axis=1), jnp.concatenate(tiles[4:8], axis=1)], axis=0
    ).astype(BF16)
    both = dot(lhs, comp)
    partial = both[:, :PLANE] + both[:, PLANE:]
    compressed = None
    for k in range(16):
        term = rows[k, :, :PLANE] * partial[k : k + 1, :]
        compressed = term if compressed is None else compressed + term
    leaf_row = leaf[...].astype(F32)
    leaf_tile = jnp.concatenate(
        [leaf_row[:, a * PLANE : (a + 1) * PLANE] for a in range(8)], axis=0
    )
    middle = jnp.where(refined[0] > 0, compressed, leaf_tile).astype(BF16).astype(F32)

    row_at = (octant >> 2) * 8
    inner = row_mix([rows[row_at + x, :, :PLANE] for x in range(8)], middle)
    copies[5].wait()
    added = fine_dot(inner, contrib[...])
    low8 = low_lanes((8, 128))
    tag = jnp.full((8, 128), slot, jnp.int32).astype(F32)
    tile = jnp.where(low8, jnp.concatenate([added, added], axis=1), tag).astype(BF16)
    payload_v[...] = jnp.broadcast_to(tile[None], payload_v.shape)
    send = pltpu.make_async_copy(payload_v, payload, payload_sem)
    send.start()

    for copy in copies[6:8]:
        copy.wait()
    prol = jnp.concatenate([filters[256 + 64 * k : 320 + 64 * k, :] for k in range(4)], axis=1)
    live = jnp.full((8, PLANE), refined[0], jnp.int32).astype(F32)
    upper = jnp.concatenate(two_row_mixes(rows.at[16:32], middle, PLANE), axis=0)
    spread = fine_dot(upper, prol)
    for o in range(8):
        i, jl = o // 4, o % 4
        part = spread[i * 8 : i * 8 + 8, jl * PLANE : (jl + 1) * PLANE]
        detail[child[0, o]] = live * (tiles[o] - part)
    lane = lax.broadcasted_iota(jnp.int32, (8, 128), 1)
    name = jnp.where(lane < 96, tag, jnp.full((8, 128), octant, jnp.int32).astype(F32))
    pairs = [jnp.concatenate([detail[2 * k], detail[2 * k + 1]], axis=1) for k in range(4)]
    pairs.append(jnp.where(low8, jnp.concatenate([middle, middle], axis=1), name))
    halo[...] = jnp.concatenate(pairs, axis=0).astype(BF16)

    for copy in copies[8:]:
        copy.wait()
    near = fine_nbr[...]
    own = near[:, 13:14] >> 3
    cell = local_cell(near >> 3, own) * 10 + (near & 7)
    numbers[0:8, 0:27] = jnp.where(near >= 0, cell, GONE)
    near_mid = mid_nbr[...]
    own_mid = near_mid[:, 13:14]
    numbers[8:9, 0:27] = jnp.where(near_mid >= 0, local_cell(near_mid, own_mid), 27)
    numbers[8:9, 27:28] = jnp.full((1, 1), 27, jnp.int32)
    hot = jnp.where(lax.broadcasted_iota(jnp.int32, (8, 64), 1) == slot, 1.0, 0.0).astype(BF16)
    near_coarse = lax.dot_general(
        hot,
        coarse_nbr[...].astype(F32).astype(BF16),
        (((1,), (1,)), ((), ())),
        preferred_element_type=F32,
    )[0:1].astype(jnp.int32)
    numbers[9:10, 0:27] = jnp.where(near_coarse >= 0, near_coarse, 64)
    numbers[9:10, 27:28] = jnp.full((1, 1), 64, jnp.int32)
    numbers[10:11, 0:8] = child_v[...]
    numbers[10:11, 8:9] = jnp.full((1, 1), parent[0], jnp.int32)
    numbers[10:11, 9:10] = jnp.full((1, 1), refined[0], jnp.int32)
    send.wait()


def plane_kernel(arrived, copies, partial, sems):
    rows = arrived[...].astype(F32).reshape(512, 128)
    other = turned(rows)
    low = low_lanes((512, 128))
    value = jnp.where(low, rows, other)
    tag = jnp.where(low, other, rows)
    half = jnp.where(low, 0, 1)
    rhs = jnp.where((tag.astype(jnp.int32) & 1) == half, value, 0.0).astype(BF16)
    pick = jnp.where(lax.broadcasted_iota(jnp.int32, (8, 128), 1) == 0, 1.0, 0.0).astype(BF16)
    along = lax.dot_general(
        pick, tag.astype(BF16), (((1,), (1,)), ((), ())), preferred_element_type=F32
    ).astype(jnp.int32)
    p_of = lax.broadcasted_iota(jnp.int32, (8, 512), 1) & 7
    key = jnp.where(p_of == lax.broadcasted_iota(jnp.int32, (8, 512), 0), along >> 1, -1)
    hot = jnp.concatenate(
        [jnp.where(key == c2, 1.0, 0.0) for c2 in range(32)], axis=0
    ).astype(BF16)
    partial[...] = dot(hot, rhs).astype(BF16)
    for copy in fetches(sems, *((partial, copies.at[at]) for at in range(8))):
        copy.wait()


def pair_of(first, second):
    return jnp.where(low_lanes((8, 128)), first, second)


def fine_kernel(
    numbers_h, left, centre, right, ab_ref, x_ref,
    direct, mid_tiles, names_ref,
    table, mixed, w_ref, numbers, sems,
):
    copies = fetches(sems, (numbers_h, numbers))
    build_w(ab_ref, 0, w_ref)
    lanes = lax.broadcasted_iota(jnp.int32, (1, 128), 1)
    low8 = low_lanes((8, 128))
    table[GONE] = jnp.zeros((8, 128), F32)
    table[GONE + 8] = jnp.zeros((8, 128), F32)
    spread_cells(left, table, 0)
    spread_cells(right, table, 18)
    for at in range(90):
        table[90 + at] = centre[at]
    names = jnp.full((1, 128), 512, jnp.int32)
    for cell in range(27):
        meta = table[cell * 10 + 9, 0:1, :]
        name = meta * 8.0 + pltpu.roll(meta, 96, 1)
        names = jnp.where(lanes == PLANE + cell, name.astype(jnp.int32), names)
    names_ref[...] = names
    for cell in range(28):
        mid_tiles[cell] = table[cell * 10 + 8]

    for copy in copies:
        copy.wait()

    def source(t, ex, e):
        return table[numbers[t, ex * 9 + e]]

    for pair in range(4):
        pieces = []
        for t in (2 * pair, 2 * pair + 1):
            for ep in range(5):
                pieces.append(
                    jnp.concatenate(
                        [
                            pair_of(source(t, ex, 2 * ep), source(t, ex, min(2 * ep + 1, 8)))
                            for ex in range(3)
                        ],
                        axis=0,
                    ).astype(BF16)
                )
        product = dot(x_ref[0], jnp.concatenate(pieces, axis=1))
        for term in range(4):
            row = term * PLANE + pair * 16
            last = None
            for quad in range(QUADS):
                at = (quad * 4 + term) * 8
                tile = jnp.concatenate(
                    [product[at : at + 8, :512], product[at : at + 8, 640:1152]], axis=0
                )
                mixed[row : row + 16, quad * 512 : quad * 512 + 512] = tile.astype(BF16)
                tile = jnp.concatenate(
                    [product[at : at + 8, 512:640], product[at : at + 8, 1152:1280]], axis=0
                )
                if quad % 2 == 0:
                    last = tile
                else:
                    to = 4096 + quad // 2 * 128
                    tile = jnp.where(low_lanes((16, 128)), last, tile)
                    mixed[row : row + 16, to : to + 128] = tile.astype(BF16)
    result = None
    for half in range(2):
        total = None
        own = slice(half * 128, half * 128 + 128)
        for part in range(9):
            some = slice(part * 512, part * 512 + 512)
            term = dot(mixed[own, some], w_ref[some, own])
            total = term if total is None else total + term
        for term in range(2):
            rows = slice(term * PLANE, term * PLANE + PLANE)
            result = total[rows, rows] if result is None else result + total[rows, rows]
    direct[...] = result.reshape(8, 8, PLANE)


def last_kernel(
    numbers_h, names_h, planes, mid_tiles, direct, ab_ref, x_ref, rows_p, filters, mids,
    fine_out, mid_out,
    coarse, back, sems, w_mid, w_coarse, numbers, names,
):
    copies = fetches(sems, (numbers_h, numbers), (names_h, names))
    build_w(ab_ref, 1, w_mid)
    build_w(ab_ref, 2, w_coarse)
    low8 = low_lanes((8, 128))

    total = None
    for plane in range(8):
        term = planes[plane].astype(F32)
        total = term if total is None else total + term
    for c2 in range(32):
        tile = total[c2 * 8 : c2 * 8 + 8, :]
        other = turned(tile)
        coarse[2 * c2] = jnp.where(low8, tile, other)
        coarse[2 * c2 + 1] = jnp.where(low8, other, tile)
    coarse[64] = jnp.zeros((8, 128), F32)
    for copy in copies:
        copy.wait()
    octant = numbers[10, 8] & 7

    uppers, octants, owns = [], [], []
    for ep in range(5):
        for ex in range(3):
            first = numbers[8, ex * 9 + 2 * ep]
            second = numbers[8, ex * 9 + min(2 * ep + 1, 8)]
            name_1, name_2 = names[0, PLANE + first], names[0, PLANE + second]
            owns.append(pair_of(mid_tiles[first], mid_tiles[second]))
            both = pair_of(coarse[name_1 >> 3], coarse[name_2 >> 3])
            named = jnp.where(low8, name_1 & 7, name_2 & 7)
            octants.append(named)
            mix_0, mix_1 = two_row_mixes(rows_p, both, 128)
            uppers.append(jnp.where(named >= 4, mix_1, mix_0))
    stacked = jnp.concatenate(uppers, axis=0)
    high = stacked.astype(BF16).astype(F32)
    spread = dot(jnp.concatenate([high, stacked - high], axis=0).astype(BF16), mids[...])
    spread = spread[:120, :512] + spread[120:, :512] + spread[:120, 512:]
    pieces = []
    for ep in range(5):
        tiles = []
        for ex in range(3):
            at = ep * 3 + ex
            which = octants[at] & 3
            chosen = spread[at * 8 : at * 8 + 8, 0:128]
            for jl in range(1, 4):
                chosen = jnp.where(
                    which == jl, spread[at * 8 : at * 8 + 8, jl * 128 : jl * 128 + 128], chosen
                )
            tiles.append(owns[at] - chosen)
        pieces.append(jnp.concatenate(tiles, axis=0).astype(BF16))
    mid_result = apply_one(jnp.concatenate(pieces, axis=1), x_ref[1], w_mid)

    def coarse_source(ex, e):
        return coarse[numbers[9, ex * 9 + e]]

    sources = jnp.concatenate(
        [
            jnp.concatenate(
                [
                    pair_of(coarse_source(ex, 2 * ep), coarse_source(ex, min(2 * ep + 1, 8)))
                    for ex in range(3)
                ],
                axis=0,
            ).astype(BF16)
            for ep in range(5)
        ],
        axis=1,
    )
    coarse_result = apply_one(sources, x_ref[2], w_coarse)

    row_at = (octant >> 2) * 8
    upper = row_mix([rows_p[row_at + p, :, :PLANE] for p in range(8)], coarse_result)
    single = filters[pl.ds(pl.multiple_of(256 + (octant & 3) * 64, 64), 64), :]
    middle = mid_result + fine_dot(upper, single)
    for a in range(8):
        mid_out[:, a * PLANE : (a + 1) * PLANE] = middle[a : a + 1, :]
    live = jnp.full((8, PLANE), numbers[10, 9], jnp.int32).astype(F32)
    upper = jnp.concatenate(two_row_mixes(rows_p, middle, PLANE), axis=0)
    prol = jnp.concatenate([filters[64 * k : 64 * k + 64, :] for k in range(4)], axis=1)
    spread = fine_dot(upper, prol)
    for o in range(8):
        i, jl = o // 4, o % 4
        slot = numbers[10, o]
        part = spread[i * 8 : i * 8 + 8, jl * PLANE : (jl + 1) * PLANE]
        back[slot] = live * (direct[slot] + part)
    for a in range(8):
        fine_out[:, a * PLANE : (a + 1) * PLANE] = back[:, a, :]


def call(kernel, kinds, outs, scratch, flops, *args):
    any_space = pl.BlockSpec(memory_space=pl.ANY)
    vmem = pl.BlockSpec(memory_space=pltpu.VMEM)
    specs = dict(s=pl.BlockSpec(memory_space=pltpu.SMEM), v=vmem, w=vmem, h=any_space, a=any_space)
    moved = sum(math.prod(x.shape) * x.dtype.itemsize for x in (*args, *outs))
    spaces = dict(w=pltpu.VMEM, h=pltpu.HBM)
    args = [
        pltpu.with_memory_space_constraint(x, spaces[kind]) if kind in spaces else x
        for kind, x in zip(kinds, args, strict=True)
    ]
    return pl.pallas_call(
        kernel,
        out_shape=outs,
        in_specs=[specs[kind] for kind in kinds],
        out_specs=[any_space if getattr(x, "memory_space", None) == pltpu.HBM else vmem for x in outs],
        scratch_shapes=scratch,
        compiler_params=pltpu.CompilerParams(vmem_limit_bytes=VMEM_LIMIT),
        cost_estimate=pl.CostEstimate(flops=flops, bytes_accessed=moved, transcendentals=0),
        name=kernel.__name__,
    )(*args)


def both_ways(x, axis):
    count = lax.axis_size(axis)
    ends = count - 1
    before = lax.ppermute(x, axis, [(i, i + 1) for i in range(ends)])
    after = lax.ppermute(x, axis, [(i + 1, i) for i in range(ends)])
    return before, after


def shards(
    fine_coef, mid_leaf, mid_child, mid_parent, mid_refined,
    fine_nbr, mid_nbr, coarse_nbr, op_factor, term_weight,
):
    tables = filter_tables()
    select = jnp.asarray(select_tables())
    prol_rows = np.concatenate(np.split(tables["prol"], 4, axis=1), axis=0)
    single_rows = tables["single"].reshape(256, 128)
    first_filters = jnp.asarray(
        np.concatenate([tables["comp"], prol_rows, tables["contrib"].reshape(256, 128)])
    )
    last_filters = jnp.asarray(np.concatenate([prol_rows, single_rows]))
    rows_both = jnp.asarray(np.concatenate([tables["rows_c"], tables["rows_p"]]))
    rows_p = jnp.asarray(tables["rows_p"])
    mids = jnp.asarray(tables["mids"])
    factors = op_factor.transpose(0, 2, 3, 4, 1).reshape(3, 192, TERMS)

    sds = jax.ShapeDtypeStruct
    vmem, smem = pltpu.VMEM, pltpu.SMEM
    i32 = jnp.int32
    halo, payload, numbers = call(
        first_kernel,
        "sshhhhhhhh",
        [sds((CELL, 128), BF16), pltpu.HBM((64, 8, 128), BF16), sds((16, 128), i32)],
        [
            smem((1, 8), i32),
            vmem((1, 8), i32),
            vmem((8, 27), i32),
            vmem((1, 27), i32),
            vmem((27, 64), i32),
            vmem((8, 512), BF16),
            vmem((1, 512), BF16),
            vmem((512, 128), BF16),
            vmem((32, 8, 128), F32),
            vmem((8, 8, PLANE), F32),
            vmem((8, 8, PLANE), F32),
            pltpu.SemaphoreType.DMA((12,)),
            vmem((64, 8, 128), BF16),
            pltpu.SemaphoreType.DMA,
            vmem((64, 128), BF16),
        ],
        2_000_000,
        mid_parent, mid_refined, mid_child, fine_nbr, mid_nbr, coarse_nbr.T, fine_coef, mid_leaf,
        first_filters, rows_both,
    )
    arrived = lax.all_to_all(payload, ("gy", "gz"), 0, 0, tiled=True)
    before, after = both_ways(halo, "gx")
    line = jnp.concatenate([before, halo, after], axis=0)
    before, after = both_ways(line, "gy")
    sheet = jnp.concatenate([before, line, after], axis=0)
    before, after = both_ways(sheet, "gz")

    (copies,) = call(
        plane_kernel, "v", [pltpu.HBM((8, 256, 128), BF16)],
        [vmem((256, 128), BF16), pltpu.SemaphoreType.DMA((8,))], 33_000_000, arrived
    )
    planes = lax.all_to_all(copies, "gx", 0, 0, tiled=True)

    w_factors, x_tables, centre, rows_p, last_filters, mids = call(
        tables_kernel,
        "hhhvhhh",
        [
            pltpu.VMEM((2, 3 * QUADS, 24, 256), F32),
            pltpu.VMEM((3, 256, 24), BF16),
            pltpu.VMEM((90, 8, 128), F32),
            pltpu.VMEM((16, 8, 128), F32),
            pltpu.VMEM((512, 128), BF16),
            pltpu.VMEM((128, 1024), BF16),
        ],
        [
            vmem((3, 192, TERMS), F32),
            vmem((1, TERMS), F32),
            vmem((256, 768), BF16),
            pltpu.SemaphoreType.DMA((6,)),
        ],
        600_000_000,
        factors, term_weight.reshape(1, TERMS), select, sheet, rows_p, last_filters, mids,
    )
    direct, mid_tiles, names = call(
        fine_kernel,
        "avvvww",
        [sds((8, 8, PLANE), F32), sds((28, 8, 128), F32), sds((1, 128), i32)],
        [
            vmem((GONE + 9, 8, 128), F32),
            vmem((256, ROWS_W), BF16),
            vmem((ROWS_W, 256), BF16),
            smem((16, 128), i32),
            pltpu.SemaphoreType.DMA((1,)),
        ],
        100_000_000,
        numbers, before, centre, after, w_factors, x_tables,
    )
    fine_out, mid_out = call(
        last_kernel,
        "aavvvwwwww",
        [sds((8, 512), F32), sds((1, 512), F32)],
        [
            vmem((65, 8, 128), F32),
            vmem((8, 8, PLANE), F32),
            pltpu.SemaphoreType.DMA((2,)),
            vmem((ROWS_W, 256), BF16),
            vmem((ROWS_W, 256), BF16),
            smem((16, 128), i32),
            smem((1, 128), i32),
        ],
        200_000_000,
        numbers, names, planes, mid_tiles, direct, w_factors, x_tables,
        rows_p, last_filters, mids,
    )
    return fine_out, mid_out


def solution(mesh):
    cells = ("gx", "gy", "gz")
    rows = P(cells, None)
    return jax.shard_map(
        shards,
        mesh=mesh,
        in_specs=(rows, rows, rows, P(cells), P(cells), rows, rows, P(), P(), P()),
        out_specs=(rows, rows),
        check_vma=False,
    )
```

```python
import functools
import math

import jax
import jax.numpy as jnp
import ml_dtypes
import numpy as np
from jax import lax
from jax.experimental import pallas as pl
from jax.experimental.pallas import tpu as pltpu
from jax.sharding import PartitionSpec as P

K = 8
PLANE = 64
TERMS = 32
QUADS = 8
ROWS_W = 4608
CELL = 40
GONE = 27 * 10
BF16 = jnp.bfloat16
F32 = jnp.float32
VMEM_LIMIT = 32 * 1024 * 1024


def poly_multiply(left, right):
    result = [0.0] * (len(left) + len(right) - 1)
    for first, left_coef in enumerate(left):
        for second, right_coef in enumerate(right):
            result[first + second] += left_coef * right_coef
    return result


def poly_compose(coeffs, factor, offset):
    result = [0.0]
    power_term = [1.0]
    for coef in coeffs:
        padded = result + [0.0] * (len(power_term) - len(result))
        result = [padded[place] + coef * power_term[place] for place in range(len(power_term))]
        power_term = poly_multiply(power_term, [offset, factor])
    return result


def legendre_table(basis_order):
    polys = [[1.0], [0.0, 1.0]]
    for degree in range(1, basis_order):
        upper = [0.0] + [(2 * degree + 1) * coef for coef in polys[degree]]
        lower = [degree * coef for coef in polys[degree - 1]] + [0.0] * (
            len(upper) - len(polys[degree - 1])
        )
        polys.append([(upper[place] - lower[place]) / (degree + 1) for place in range(len(upper))])
    return [
        [math.sqrt(2 * degree + 1) * coef for coef in poly_compose(polys[degree], 2.0, -1.0)]
        for degree in range(basis_order)
    ]


@functools.cache
def two_scale(basis_order):
    shifted = legendre_table(basis_order)
    filters = np.zeros((2, basis_order, basis_order))
    for which_half in range(2):
        for row_at in range(basis_order):
            halved = poly_compose(shifted[row_at], 0.5, 0.5 * which_half)
            for col_at in range(basis_order):
                product = poly_multiply(halved, shifted[col_at])
                total = sum((coef / (place + 1) for place, coef in enumerate(product)))
                filters[which_half, row_at, col_at] = total / math.sqrt(2.0)
    return filters.astype(np.float32).astype(np.float64)


def two_parts(matrix):
    high = matrix.astype(ml_dtypes.bfloat16)
    low = (matrix - high.astype(np.float64)).astype(ml_dtypes.bfloat16)
    return high, low


@functools.cache
def filter_tables():
    h = two_scale(K)
    pair = np.einsum("jqy,lrz->jlqryz", h, h).reshape(4, PLANE, PLANE)
    to_coarse = pair.transpose(0, 2, 1).reshape(4 * PLANE, PLANE)
    comp = np.concatenate(two_parts(to_coarse), axis=1)
    to_fine = pair.transpose(1, 0, 2).reshape(PLANE, 4 * PLANE)
    prol = np.concatenate(two_parts(to_fine), axis=1)
    contrib = np.stack([np.concatenate(two_parts(pair[k].T), axis=1) for k in range(4)])
    single = np.stack([np.concatenate(two_parts(pair[k]), axis=1) for k in range(4)])
    mid = np.zeros((2, PLANE, 4, 2, PLANE))
    for half in range(2):
        mid[half, :, :, half, :] = pair.transpose(1, 0, 2)
    mids = np.concatenate(two_parts(mid.reshape(128, 512)), axis=1)
    rows_c = np.broadcast_to(h.transpose(0, 2, 1).reshape(16, 8)[:, :, None], (16, 8, 128))
    rows_p = np.broadcast_to(h.reshape(16, 8)[:, :, None], (16, 8, 128))
    return dict(
        comp=comp,
        prol=prol,
        contrib=contrib,
        single=single,
        mids=mids,
        rows_c=np.ascontiguousarray(rows_c).astype(np.float32),
        rows_p=np.ascontiguousarray(rows_p).astype(np.float32),
    )


@functools.cache
def select_tables():
    out = np.arange(256) // TERMS
    term = np.arange(256) % TERMS
    col = np.arange(256)
    group = term[:, None] % 4 == (col // PLANE)[None, :]
    left = group & (out[:, None] == (col // 8 % 8)[None, :])
    right = group & (out[:, None] == (col % 8)[None, :])
    turn = (term[None, :] == (col // 8)[:, None]) & (out[None, :] == (col % 8)[:, None])
    return np.concatenate([left, right, turn], axis=1).astype(ml_dtypes.bfloat16)


def split(value):
    high = value.astype(BF16)
    return high, (value - high.astype(F32)).astype(BF16)


def dot(left, right):
    return jnp.dot(left, right, preferred_element_type=F32)


def fine_dot(value, table):
    rows = value.shape[0]
    width = table.shape[1] // 2
    if rows % 16 == 0:
        result = dot(jnp.concatenate(split(value), axis=0), table)
    else:
        high = value.astype(BF16).astype(F32)
        result = dot(jnp.concatenate([high, value - high], axis=0).astype(BF16), table)
    return result[:rows, :width] + result[rows:, :width] + result[:rows, width:]


def low_lanes(shape):
    return lax.broadcasted_iota(jnp.int32, shape, len(shape) - 1) < PLANE


def turned(value):
    return pltpu.roll(value, PLANE, value.ndim - 1)


def row_mix(tables, tile):
    total = None
    for p in range(8):
        term = tables[p] * tile[p : p + 1, :]
        total = term if total is None else total + term
    return total


def two_row_mixes(rows_ref, tile, width):
    return [
        row_mix([rows_ref[i * 8 + p, :, :width] for p in range(8)], tile) for i in range(2)
    ]


def fetches(sems, *pairs):
    copies = [
        pltpu.make_async_copy(there, here, sems.at[at]) for at, (there, here) in enumerate(pairs)
    ]
    for copy in copies:
        copy.start()
    return copies


def local_cell(device, own):
    step_x = (device >> 6) - (own >> 6) + 1
    step_y = ((device >> 3) & 7) - ((own >> 3) & 7) + 1
    step_z = (device & 7) - (own & 7) + 1
    return step_z * 9 + step_y * 3 + step_x


def tables_kernel(
    factors_h, weights_h, select_h, sheet, rows_h, filters_h, mids_h,
    ab_ref, x_ref, tiles, rows_p, filters, mids,
    factors, weights, select, sems,
):
    copies = fetches(
        sems,
        (factors_h, factors),
        (weights_h, weights),
        (select_h, select),
        (mids_h, mids),
        (filters_h, filters),
        (rows_h, rows_p),
    )
    spread_cells(sheet, tiles, 0)
    for copy in copies[:3]:
        copy.wait()
    lane = lax.broadcasted_iota(jnp.int32, (24, 256), 1)
    quad_of = (lane & 31) >> 2
    weight = jnp.concatenate([weights[...]] * 8, axis=1)
    weighted, plain = [], []
    for level in range(3):
        rows = []
        for e in range(3):
            rows.append(
                jnp.concatenate(
                    [factors[level, e * 64 + b * 8 : e * 64 + b * 8 + 8, :] for b in range(8)],
                    axis=1,
                )
            )
        values = jnp.concatenate(rows, axis=0)
        scaled = values * weight
        for quad in range(QUADS):
            weighted.append(jnp.where(quad_of == quad, scaled, 0.0))
            plain.append(jnp.where(quad_of == quad, values, 0.0))
        x_ref[level] = lax.dot_general(
            select[:, 512:768],
            values.astype(BF16),
            (((1,), (1,)), ((), ())),
            preferred_element_type=F32,
        ).astype(BF16)
    for which, parts in enumerate((weighted, plain)):
        both = dot(
            jnp.concatenate(split(jnp.concatenate(parts, axis=0)), axis=0),
            select[:, which * 256 : which * 256 + 256],
        )
        ab_ref[which] = (both[:576] + both[576:]).reshape(24, 24, 256)
    for copy in copies[3:]:
        copy.wait()


def build_w(ab_ref, level, w_ref):
    def one_quad(quad):
        at = level * QUADS + quad
        inner = [ab_ref[1, at, ez * 8 : ez * 8 + 8, :] for ez in range(3)]
        for ey in range(3):
            for pair in range(4):
                row = ey * 8 + 2 * pair
                first = ab_ref[0, at, row : row + 1, :]
                second = ab_ref[0, at, row + 1 : row + 2, :]
                for ez in range(3):
                    tile = jnp.concatenate([first * inner[ez], second * inner[ez]], axis=0)
                    e = ey * 3 + ez
                    to = quad * 512 + e * PLANE if e < 8 else 4096 + quad * PLANE
                    to += pair * 16
                    w_ref[to : to + 16, :] = tile.astype(BF16)

    for quad in range(QUADS):
        one_quad(quad)


def spread_cells(sheet, tiles, at):
    low = low_lanes((8, 128))
    values = sheet[...].astype(F32)
    for cell in range(9):
        to = (at + cell) * 10
        for pair in range(5):
            row = cell * CELL + pair * 8
            tile = values[row : row + 8, :]
            other = turned(tile)
            tiles[to + 2 * pair] = jnp.where(low, tile, other)
            tiles[to + 2 * pair + 1] = tile if pair == 4 else jnp.where(low, other, tile)


def diagonal_sum(result, rows):
    total = None
    for term in range(4):
        piece = result[term * rows : (term + 1) * rows, term * PLANE : (term + 1) * PLANE]
        total = piece if total is None else total + piece
    return total


def apply_one(sources, x_table, w_ref):
    product = dot(x_table, sources)
    low = low_lanes((32, 128))
    groups = [product[quad * 32 : quad * 32 + 32, :] for quad in range(QUADS)]
    pieces = [group[:, :512].astype(BF16) for group in groups]
    for quad in range(0, QUADS, 2):
        both = jnp.where(low, groups[quad][:, 512:], groups[quad + 1][:, 512:])
        pieces.append(both.astype(BF16))
    result = None
    for quad in range(QUADS):
        part = dot(pieces[quad], w_ref[quad * 512 : quad * 512 + 512, :])
        result = part if result is None else result + part
    for pair in range(4):
        at = 4096 + pair * 128
        result += dot(pieces[QUADS + pair], w_ref[at : at + 128, :])
    return diagonal_sum(result, 8)


def first_kernel(
    parent, refined, child_h, fine_h, mid_h, coarse_h, coef_h, leaf_h, filters_h, rows_h,
    halo, payload, numbers,
    child, child_v, fine_nbr, mid_nbr, coarse_nbr, coef, leaf, filters, rows,
    source, detail, sems, payload_v, payload_sem, contrib,
):
    slot = parent[0] >> 3
    octant = parent[0] & 7
    contrib_at = pl.multiple_of(512 + (octant & 3) * 64, 64)
    copies = fetches(
        sems,
        (child_h, child),
        (coef_h, coef),
        (filters_h.at[pl.ds(0, 256)], filters.at[pl.ds(0, 256)]),
        (rows_h.at[pl.ds(0, 16)], rows.at[pl.ds(0, 16)]),
        (leaf_h, leaf),
        (filters_h.at[pl.ds(contrib_at, 64)], contrib),
        (filters_h.at[pl.ds(256, 256)], filters.at[pl.ds(256, 256)]),
        (rows_h.at[pl.ds(16, 16)], rows.at[pl.ds(16, 16)]),
        (child_h, child_v),
        (fine_h, fine_nbr),
        (mid_h, mid_nbr),
        (coarse_h, coarse_nbr),
    )
    for copy in copies[:5]:
        copy.wait()
    comp = filters[0:256, :]

    values = coef[...].astype(F32)
    for a in range(8):
        source[:, a, :] = values[:, a * PLANE : (a + 1) * PLANE]
    tiles = [source[child[0, o]] for o in range(8)]
    lhs = jnp.concatenate(
        [jnp.concatenate(tiles[0:4], axis=1), jnp.concatenate(tiles[4:8], axis=1)], axis=0
    ).astype(BF16)
    both = dot(lhs, comp)
    partial = both[:, :PLANE] + both[:, PLANE:]
    compressed = None
    for k in range(16):
        term = rows[k, :, :PLANE] * partial[k : k + 1, :]
        compressed = term if compressed is None else compressed + term
    leaf_row = leaf[...].astype(F32)
    leaf_tile = jnp.concatenate(
        [leaf_row[:, a * PLANE : (a + 1) * PLANE] for a in range(8)], axis=0
    )
    middle = jnp.where(refined[0] > 0, compressed, leaf_tile).astype(BF16).astype(F32)

    row_at = (octant >> 2) * 8
    inner = row_mix([rows[row_at + x, :, :PLANE] for x in range(8)], middle)
    copies[5].wait()
    added = fine_dot(inner, contrib[...])
    low8 = low_lanes((8, 128))
    tag = jnp.full((8, 128), slot, jnp.int32).astype(F32)
    tile = jnp.where(low8, jnp.concatenate([added, added], axis=1), tag).astype(BF16)
    payload_v[...] = jnp.broadcast_to(tile[None], payload_v.shape)
    send = pltpu.make_async_copy(payload_v, payload, payload_sem)
    send.start()

    for copy in copies[6:8]:
        copy.wait()
    prol = jnp.concatenate([filters[256 + 64 * k : 320 + 64 * k, :] for k in range(4)], axis=1)
    live = jnp.full((8, PLANE), refined[0], jnp.int32).astype(F32)
    upper = jnp.concatenate(two_row_mixes(rows.at[16:32], middle, PLANE), axis=0)
    spread = fine_dot(upper, prol)
    for o in range(8):
        i, jl = o // 4, o % 4
        part = spread[i * 8 : i * 8 + 8, jl * PLANE : (jl + 1) * PLANE]
        detail[child[0, o]] = live * (tiles[o] - part)
    lane = lax.broadcasted_iota(jnp.int32, (8, 128), 1)
    name = jnp.where(lane < 96, tag, jnp.full((8, 128), octant, jnp.int32).astype(F32))
    pairs = [jnp.concatenate([detail[2 * k], detail[2 * k + 1]], axis=1) for k in range(4)]
    pairs.append(jnp.where(low8, jnp.concatenate([middle, middle], axis=1), name))
    halo[...] = jnp.concatenate(pairs, axis=0).astype(BF16)

    for copy in copies[8:]:
        copy.wait()
    near = fine_nbr[...]
    own = near[:, 13:14] >> 3
    cell = local_cell(near >> 3, own) * 10 + (near & 7)
    numbers[0:8, 0:27] = jnp.where(near >= 0, cell, GONE)
    near_mid = mid_nbr[...]
    own_mid = near_mid[:, 13:14]
    numbers[8:9, 0:27] = jnp.where(near_mid >= 0, local_cell(near_mid, own_mid), 27)
    numbers[8:9, 27:28] = jnp.full((1, 1), 27, jnp.int32)
    hot = jnp.where(lax.broadcasted_iota(jnp.int32, (8, 64), 1) == slot, 1.0, 0.0).astype(BF16)
    near_coarse = lax.dot_general(
        hot,
        coarse_nbr[...].astype(F32).astype(BF16),
        (((1,), (1,)), ((), ())),
        preferred_element_type=F32,
    )[0:1].astype(jnp.int32)
    numbers[9:10, 0:27] = jnp.where(near_coarse >= 0, near_coarse, 64)
    numbers[9:10, 27:28] = jnp.full((1, 1), 64, jnp.int32)
    numbers[10:11, 0:8] = child_v[...]
    numbers[10:11, 8:9] = jnp.full((1, 1), parent[0], jnp.int32)
    numbers[10:11, 9:10] = jnp.full((1, 1), refined[0], jnp.int32)
    send.wait()


def plane_kernel(arrived, copies, partial, sems):
    rows = arrived[...].astype(F32).reshape(512, 128)
    other = turned(rows)
    low = low_lanes((512, 128))
    value = jnp.where(low, rows, other)
    tag = jnp.where(low, other, rows)
    half = jnp.where(low, 0, 1)
    rhs = jnp.where((tag.astype(jnp.int32) & 1) == half, value, 0.0).astype(BF16)
    pick = jnp.where(lax.broadcasted_iota(jnp.int32, (8, 128), 1) == 0, 1.0, 0.0).astype(BF16)
    along = lax.dot_general(
        pick, tag.astype(BF16), (((1,), (1,)), ((), ())), preferred_element_type=F32
    ).astype(jnp.int32)
    p_of = lax.broadcasted_iota(jnp.int32, (8, 512), 1) & 7
    key = jnp.where(p_of == lax.broadcasted_iota(jnp.int32, (8, 512), 0), along >> 1, -1)
    hot = jnp.concatenate(
        [jnp.where(key == c2, 1.0, 0.0) for c2 in range(32)], axis=0
    ).astype(BF16)
    partial[...] = dot(hot, rhs).astype(BF16)
    for copy in fetches(sems, *((partial, copies.at[at]) for at in range(8))):
        copy.wait()


def pair_of(first, second):
    return jnp.where(low_lanes((8, 128)), first, second)


def fine_kernel(
    numbers_h, left, centre, right, ab_ref, x_ref,
    direct, mid_tiles, names_ref,
    table, mixed, w_ref, numbers, sems,
):
    copies = fetches(sems, (numbers_h, numbers))
    build_w(ab_ref, 0, w_ref)
    lanes = lax.broadcasted_iota(jnp.int32, (1, 128), 1)
    low8 = low_lanes((8, 128))
    table[GONE] = jnp.zeros((8, 128), F32)
    table[GONE + 8] = jnp.zeros((8, 128), F32)
    spread_cells(left, table, 0)
    spread_cells(right, table, 18)
    for at in range(90):
        table[90 + at] = centre[at]
    names = jnp.full((1, 128), 512, jnp.int32)
    for cell in range(27):
        meta = table[cell * 10 + 9, 0:1, :]
        name = meta * 8.0 + pltpu.roll(meta, 96, 1)
        names = jnp.where(lanes == PLANE + cell, name.astype(jnp.int32), names)
    names_ref[...] = names
    for cell in range(28):
        mid_tiles[cell] = table[cell * 10 + 8]

    for copy in copies:
        copy.wait()

    def source(t, ex, e):
        return table[numbers[t, ex * 9 + e]]

    for pair in range(4):
        pieces = []
        for t in (2 * pair, 2 * pair + 1):
            for ep in range(5):
                pieces.append(
                    jnp.concatenate(
                        [
                            pair_of(source(t, ex, 2 * ep), source(t, ex, min(2 * ep + 1, 8)))
                            for ex in range(3)
                        ],
                        axis=0,
                    ).astype(BF16)
                )
        product = dot(x_ref[0], jnp.concatenate(pieces, axis=1))
        for term in range(4):
            row = term * PLANE + pair * 16
            last = None
            for quad in range(QUADS):
                at = (quad * 4 + term) * 8
                tile = jnp.concatenate(
                    [product[at : at + 8, :512], product[at : at + 8, 640:1152]], axis=0
                )
                mixed[row : row + 16, quad * 512 : quad * 512 + 512] = tile.astype(BF16)
                tile = jnp.concatenate(
                    [product[at : at + 8, 512:640], product[at : at + 8, 1152:1280]], axis=0
                )
                if quad % 2 == 0:
                    last = tile
                else:
                    to = 4096 + quad // 2 * 128
                    tile = jnp.where(low_lanes((16, 128)), last, tile)
                    mixed[row : row + 16, to : to + 128] = tile.astype(BF16)
    result = None
    for half in range(2):
        total = None
        own = slice(half * 128, half * 128 + 128)
        for part in range(9):
            some = slice(part * 512, part * 512 + 512)
            term = dot(mixed[own, some], w_ref[some, own])
            total = term if total is None else total + term
        for term in range(2):
            rows = slice(term * PLANE, term * PLANE + PLANE)
            result = total[rows, rows] if result is None else result + total[rows, rows]
    direct[...] = result.reshape(8, 8, PLANE)


def coarse_kernel(numbers_h, planes, ab_ref, x_ref, coarse, result, w_coarse, numbers, sems):
    copies = fetches(sems, (numbers_h, numbers))
    build_w(ab_ref, 2, w_coarse)
    low8 = low_lanes((8, 128))

    total = None
    for plane in range(8):
        term = planes[plane].astype(F32)
        total = term if total is None else total + term
    for c2 in range(32):
        tile = total[c2 * 8 : c2 * 8 + 8, :]
        other = turned(tile)
        coarse[2 * c2] = jnp.where(low8, tile, other)
        coarse[2 * c2 + 1] = jnp.where(low8, other, tile)
    coarse[64] = jnp.zeros((8, 128), F32)
    for copy in copies:
        copy.wait()

    def coarse_source(ex, e):
        return coarse[numbers[9, ex * 9 + e]]

    sources = jnp.concatenate(
        [
            jnp.concatenate(
                [
                    pair_of(coarse_source(ex, 2 * ep), coarse_source(ex, min(2 * ep + 1, 8)))
                    for ex in range(3)
                ],
                axis=0,
            ).astype(BF16)
            for ep in range(5)
        ],
        axis=1,
    )
    result[...] = apply_one(sources, x_ref[2], w_coarse)


def last_kernel(
    numbers_h, names_h, coarse, coarse_ref, mid_tiles, direct, ab_ref, x_ref, rows_p, filters, mids,
    fine_out, mid_out,
    back, sems, w_mid, numbers, names,
):
    copies = fetches(sems, (numbers_h, numbers), (names_h, names))
    build_w(ab_ref, 1, w_mid)
    low8 = low_lanes((8, 128))

    for copy in copies:
        copy.wait()
    octant = numbers[10, 8] & 7
    coarse_result = coarse_ref[...]

    uppers, octants, owns = [], [], []
    for ep in range(5):
        for ex in range(3):
            first = numbers[8, ex * 9 + 2 * ep]
            second = numbers[8, ex * 9 + min(2 * ep + 1, 8)]
            name_1, name_2 = names[0, PLANE + first], names[0, PLANE + second]
            owns.append(pair_of(mid_tiles[first], mid_tiles[second]))
            both = pair_of(coarse[name_1 >> 3], coarse[name_2 >> 3])
            named = jnp.where(low8, name_1 & 7, name_2 & 7)
            octants.append(named)
            mix_0, mix_1 = two_row_mixes(rows_p, both, 128)
            uppers.append(jnp.where(named >= 4, mix_1, mix_0))
    stacked = jnp.concatenate(uppers, axis=0)
    high = stacked.astype(BF16).astype(F32)
    spread = dot(jnp.concatenate([high, stacked - high], axis=0).astype(BF16), mids[...])
    spread = spread[:120, :512] + spread[120:, :512] + spread[:120, 512:]
    pieces = []
    for ep in range(5):
        tiles = []
        for ex in range(3):
            at = ep * 3 + ex
            which = octants[at] & 3
            chosen = spread[at * 8 : at * 8 + 8, 0:128]
            for jl in range(1, 4):
                chosen = jnp.where(
                    which == jl, spread[at * 8 : at * 8 + 8, jl * 128 : jl * 128 + 128], chosen
                )
            tiles.append(owns[at] - chosen)
        pieces.append(jnp.concatenate(tiles, axis=0).astype(BF16))
    mid_result = apply_one(jnp.concatenate(pieces, axis=1), x_ref[1], w_mid)

    row_at = (octant >> 2) * 8
    upper = row_mix([rows_p[row_at + p, :, :PLANE] for p in range(8)], coarse_result)
    single = filters[pl.ds(pl.multiple_of(256 + (octant & 3) * 64, 64), 64), :]
    middle = mid_result + fine_dot(upper, single)
    for a in range(8):
        mid_out[:, a * PLANE : (a + 1) * PLANE] = middle[a : a + 1, :]
    live = jnp.full((8, PLANE), numbers[10, 9], jnp.int32).astype(F32)
    upper = jnp.concatenate(two_row_mixes(rows_p, middle, PLANE), axis=0)
    prol = jnp.concatenate([filters[64 * k : 64 * k + 64, :] for k in range(4)], axis=1)
    spread = fine_dot(upper, prol)
    for o in range(8):
        i, jl = o // 4, o % 4
        slot = numbers[10, o]
        part = spread[i * 8 : i * 8 + 8, jl * PLANE : (jl + 1) * PLANE]
        back[slot] = live * (direct[slot] + part)
    for a in range(8):
        fine_out[:, a * PLANE : (a + 1) * PLANE] = back[:, a, :]


def call(kernel, kinds, outs, scratch, flops, *args):
    any_space = pl.BlockSpec(memory_space=pl.ANY)
    vmem = pl.BlockSpec(memory_space=pltpu.VMEM)
    specs = dict(s=pl.BlockSpec(memory_space=pltpu.SMEM), v=vmem, w=vmem, h=any_space, a=any_space)
    moved = sum(math.prod(x.shape) * x.dtype.itemsize for x in (*args, *outs))
    spaces = dict(w=pltpu.VMEM, h=pltpu.HBM)
    args = [
        pltpu.with_memory_space_constraint(x, spaces[kind]) if kind in spaces else x
        for kind, x in zip(kinds, args, strict=True)
    ]
    return pl.pallas_call(
        kernel,
        out_shape=outs,
        in_specs=[specs[kind] for kind in kinds],
        out_specs=[any_space if getattr(x, "memory_space", None) == pltpu.HBM else vmem for x in outs],
        scratch_shapes=scratch,
        compiler_params=pltpu.CompilerParams(vmem_limit_bytes=VMEM_LIMIT),
        cost_estimate=pl.CostEstimate(flops=flops, bytes_accessed=moved, transcendentals=0),
        name=kernel.__name__,
    )(*args)


def both_ways(x, axis):
    count = lax.axis_size(axis)
    ends = count - 1
    before = lax.ppermute(x, axis, [(i, i + 1) for i in range(ends)])
    after = lax.ppermute(x, axis, [(i + 1, i) for i in range(ends)])
    return before, after


def shards(
    fine_coef, mid_leaf, mid_child, mid_parent, mid_refined,
    fine_nbr, mid_nbr, coarse_nbr, op_factor, term_weight,
):
    tables = filter_tables()
    select = jnp.asarray(select_tables())
    prol_rows = np.concatenate(np.split(tables["prol"], 4, axis=1), axis=0)
    single_rows = tables["single"].reshape(256, 128)
    first_filters = jnp.asarray(
        np.concatenate([tables["comp"], prol_rows, tables["contrib"].reshape(256, 128)])
    )
    last_filters = jnp.asarray(np.concatenate([prol_rows, single_rows]))
    rows_both = jnp.asarray(np.concatenate([tables["rows_c"], tables["rows_p"]]))
    rows_p = jnp.asarray(tables["rows_p"])
    mids = jnp.asarray(tables["mids"])
    factors = op_factor.transpose(0, 2, 3, 4, 1).reshape(3, 192, TERMS)

    sds = jax.ShapeDtypeStruct
    vmem, smem = pltpu.VMEM, pltpu.SMEM
    i32 = jnp.int32
    halo, payload, numbers = call(
        first_kernel,
        "sshhhhhhhh",
        [sds((CELL, 128), BF16), pltpu.HBM((64, 8, 128), BF16), sds((16, 128), i32)],
        [
            smem((1, 8), i32),
            vmem((1, 8), i32),
            vmem((8, 27), i32),
            vmem((1, 27), i32),
            vmem((27, 64), i32),
            vmem((8, 512), BF16),
            vmem((1, 512), BF16),
            vmem((512, 128), BF16),
            vmem((32, 8, 128), F32),
            vmem((8, 8, PLANE), F32),
            vmem((8, 8, PLANE), F32),
            pltpu.SemaphoreType.DMA((12,)),
            vmem((64, 8, 128), BF16),
            pltpu.SemaphoreType.DMA,
            vmem((64, 128), BF16),
        ],
        2_000_000,
        mid_parent, mid_refined, mid_child, fine_nbr, mid_nbr, coarse_nbr.T, fine_coef, mid_leaf,
        first_filters, rows_both,
    )
    arrived = lax.all_to_all(payload, ("gy", "gz"), 0, 0, tiled=True)
    before, after = both_ways(halo, "gx")
    line = jnp.concatenate([before, halo, after], axis=0)
    before, after = both_ways(line, "gy")
    sheet = jnp.concatenate([before, line, after], axis=0)
    before, after = both_ways(sheet, "gz")

    (copies,) = call(
        plane_kernel, "v", [pltpu.HBM((8, 256, 128), BF16)],
        [vmem((256, 128), BF16), pltpu.SemaphoreType.DMA((8,))], 33_000_000, arrived
    )
    planes = lax.all_to_all(copies, "gx", 0, 0, tiled=True)

    w_factors, x_tables, centre, rows_p, last_filters, mids = call(
        tables_kernel,
        "hhhvhhh",
        [
            pltpu.VMEM((2, 3 * QUADS, 24, 256), F32),
            pltpu.VMEM((3, 256, 24), BF16),
            pltpu.VMEM((90, 8, 128), F32),
            pltpu.VMEM((16, 8, 128), F32),
            pltpu.VMEM((512, 128), BF16),
            pltpu.VMEM((128, 1024), BF16),
        ],
        [
            vmem((3, 192, TERMS), F32),
            vmem((1, TERMS), F32),
            vmem((256, 768), BF16),
            pltpu.SemaphoreType.DMA((6,)),
        ],
        600_000_000,
        factors, term_weight.reshape(1, TERMS), select, sheet, rows_p, last_filters, mids,
    )
    coarse, coarse_result = call(
        coarse_kernel,
        "avww",
        [sds((65, 8, 128), F32), sds((8, PLANE), F32)],
        [vmem((ROWS_W, 256), BF16), smem((16, 128), i32), pltpu.SemaphoreType.DMA((1,))],
        20_000_000,
        numbers, planes, w_factors, x_tables,
    )
    centre, coarse_result = lax.optimization_barrier((centre, coarse_result))
    direct, mid_tiles, names = call(
        fine_kernel,
        "avvvww",
        [sds((8, 8, PLANE), F32), sds((28, 8, 128), F32), sds((1, 128), i32)],
        [
            vmem((GONE + 9, 8, 128), F32),
            vmem((256, ROWS_W), BF16),
            vmem((ROWS_W, 256), BF16),
            smem((16, 128), i32),
            pltpu.SemaphoreType.DMA((1,)),
        ],
        100_000_000,
        numbers, before, centre, after, w_factors, x_tables,
    )
    fine_out, mid_out = call(
        last_kernel,
        "aavvvvwwwww",
        [sds((8, 512), F32), sds((1, 512), F32)],
        [
            vmem((8, 8, PLANE), F32),
            pltpu.SemaphoreType.DMA((2,)),
            vmem((ROWS_W, 256), BF16),
            smem((16, 128), i32),
            smem((1, 128), i32),
        ],
        200_000_000,
        numbers, names, coarse, coarse_result, mid_tiles, direct, w_factors, x_tables,
        rows_p, last_filters, mids,
    )
    return fine_out, mid_out


def solution(mesh):
    cells = ("gx", "gy", "gz")
    rows = P(cells, None)
    return jax.shard_map(
        shards,
        mesh=mesh,
        in_specs=(rows, rows, rows, P(cells), P(cells), rows, rows, P(), P(), P()),
        out_specs=(rows, rows),
        check_vma=False,
    )
```
